32 devices in a mesh: dp: 2 (over y), ctx: 4 (over x, core), mp: 4 (over z).
Axes of the slice: x: 2, y: 2, z: 4, core: 2. Of those that a mesh axis runs over, the one named last changes fastest.
Arguments:
- tokens: bfloat16 [4, 512, 2048], P('dp', 'ctx'), may hold values from -6 to 6
- segments: int32 [4, 512], P('dp', 'ctx'), may hold values from 0 to 5, never falling along the last dimension, each value on 1 to 256 neighbouring positions
- cotangent: bfloat16 [4, 512, 2048], P('dp', 'ctx'), may hold values from -6 to 6
- first_gain: float32 [2, 2048], replicated, may hold values from 0.1 to 1.9
- first_bias: float32 [2, 2048], replicated, may hold values from -1.5 to 1.5
- qkv_weight: bfloat16 [2, 2048, 3, 2048], P(None, ('dp', 'ctx'), None, 'mp'), may hold values from -0.125 to 0.125
- qkv_bias: float32 [2, 3, 2048], P(None, None, 'mp'), may hold values from -2.5 to 2.5
- out_weight: bfloat16 [2, 2048, 2048], P(None, ('dp', 'ctx'), 'mp'), may hold values from -1 to 1
- second_gain: float32 [2, 2048], replicated, may hold values from 0.1 to 1.9
- second_bias: float32 [2, 2048], replicated, may hold values from -1.5 to 1.5
- gate_up_weight: bfloat16 [2, 2048, 2, 5632], P(None, ('dp', 'ctx'), None, 'mp'), may hold values from -0.125 to 0.125
- down_weight: bfloat16 [2, 2048, 5632], P(None, ('dp', 'ctx'), 'mp'), may hold values from -0.078125 to 0.078125
Outputs:
- activations: bfloat16 [4, 512, 2048], P('dp', 'ctx')
- tokens_grad: float32 [4, 512, 2048], P('dp', 'ctx')
- first_gain_grad: float32 [2, 2048], replicated
- first_bias_grad: float32 [2, 2048], replicated
- qkv_weight_grad: float32 [2, 2048, 3, 2048], P(None, ('dp', 'ctx'), None, 'mp')
- qkv_bias_grad: float32 [2, 3, 2048], P(None, None, 'mp')
- out_weight_grad: float32 [2, 2048, 2048], P(None, ('dp', 'ctx'), 'mp')
- second_gain_grad: float32 [2, 2048], replicated
- second_bias_grad: float32 [2, 2048], replicated
- gate_up_grad: float32 [2, 2048, 2, 5632], P(None, ('dp', 'ctx'), None, 'mp')
- down_grad: float32 [2, 2048, 5632], P(None, ('dp', 'ctx'), 'mp')
The draws below stay inside these ranges and needn't reach their ends.
Inputs may be any that keep to these rules, and one draw needn't show every extreme that they name: `segments`: in each sequence the document numbers never fall, and each document has 1 to 256 tokens.
All inputs are finite; a program needn't handle non-finite values.
Results may differ from the reference program's by a relative error of at most 0.03.
Values may be sent and summed in bfloat16 or wider, within the bound.
No kernel may reach another device: no remote copies, remote signals or barrier semaphores. Data moves between devices by JAX's collectives and lax.ppermute only.
A program may use at most 256 MiB of HBM per device.

```python
import math
import jax
import jax.numpy as jnp
import numpy as np
from jax import lax

D = 2048
HEADS = 32
HEAD = 64
FF = 5632
ROT = 16
LAYERS = 2
SEQ_LEN = 512
DOCS = 6
SEQS = 4


def block_scale(rng, dims, cuts, low, high):
    def one(axis_at, shards_of):
        steps = jax.random.uniform(jax.random.fold_in(jax.random.fold_in(rng, 6), axis_at), (shards_of,), jnp.float32, low / len(cuts), high / len(cuts))
        return jnp.repeat(jnp.exp(steps), dims[axis_at] // shards_of).reshape((-1,) + (1,) * (len(dims) - axis_at - 1))

    gain = one(*cuts[0])
    for cut in cuts[1:]:
        gain = gain * one(*cut)
    return gain


def profile(amount, total, bound, skew):
    portions = [(1 << 20) // math.isqrt(grade ** skew) + 1 for grade in range(2, amount + 1)]
    spare, holding = total - bound - (amount - 1), [1] * (amount - 1)
    while spare > 0:
        movable = [i for i in range(amount - 1) if holding[i] < bound]
        pool, left = sum([portions[i] for i in movable]), spare
        for i in movable:
            extra = min(bound - holding[i], max(1, left * portions[i] // pool), spare)
            holding[i] = holding[i] + extra
            spare = spare - extra
    return np.array([bound] + holding)


def ragged(rng, count, total, limit, skew):
    if count == 2:
        one = jax.random.randint(rng, (), max(1, total - limit), min(limit, total - 1) + 1)
        return jnp.stack([one, total - one])
    sizes = jnp.asarray(profile(count, total, limit, skew), jnp.int32)
    couples = (count - 1) // 2
    source_of, receiver = sizes[1:1 + 2 * couples:2], sizes[2:2 + 2 * couples:2]
    room = jnp.minimum(source_of - 1, limit - receiver)
    shifted = jax.random.randint(jax.random.fold_in(rng, 1), (couples,), 0, 1 << 20) % (room + 1)
    sizes = sizes.at[1:1 + 2 * couples:2].set(source_of - shifted).at[2:2 + 2 * couples:2].set(receiver + shifted)
    return sizes[jax.random.permutation(jax.random.fold_in(rng, 2), count)]


def centred(own_key, extent, spread, bound, split=(), kind=jnp.bfloat16):
    array = spread * jax.random.normal(own_key, extent, jnp.float32)
    if split:
        array = array * block_scale(own_key, extent, split, -0.22, 0.18)
    return jnp.clip(array, -bound, bound).astype(kind)


def setup_inputs(seed: int = 0) -> dict:
    streams_of = jax.random.split(jax.random.key(seed), 13)
    tokens = centred(streams_of[0], (SEQS, SEQ_LEN, D), 1.0, 6.0, ((0, 2), (1, 4)))
    segments = jax.vmap(lambda own: jnp.searchsorted(jnp.cumsum(ragged(own, DOCS, SEQ_LEN, SEQ_LEN // 2, 1)), jnp.arange(SEQ_LEN), side="right"))(jax.random.split(streams_of[1], SEQS)).reshape((SEQS, SEQ_LEN)).astype(jnp.int32)
    cotangent = centred(streams_of[2], (SEQS, SEQ_LEN, D), 1.0, 6.0, ((0, 2), (1, 4)))
    first_gain = jnp.clip(1.0 + 0.18 * jax.random.normal(streams_of[3], (LAYERS, D), jnp.float32), 0.1, 1.9)
    first_bias = centred(streams_of[4], (LAYERS, D), 0.3, 1.5, (), jnp.float32)
    qkv_weight = centred(streams_of[5], (LAYERS, D, 3, D), D ** -0.5, 0.125, ((1, 8), (3, 4)))
    qkv_bias = centred(streams_of[6], (LAYERS, 3, D), 0.5, 2.5, ((2, 4),), jnp.float32)
    out_weight = centred(streams_of[7], (LAYERS, D, D), (D // 64) ** -0.5, 1.0, ((1, 8), (2, 4)))
    second_gain = jnp.clip(1.0 + 0.18 * jax.random.normal(streams_of[8], (LAYERS, D), jnp.float32), 0.1, 1.9)
    second_bias = centred(streams_of[9], (LAYERS, D), 0.3, 1.5, (), jnp.float32)
    gate_up_weight = centred(streams_of[10], (LAYERS, D, 2, FF), D ** -0.5, 0.125, ((1, 8), (3, 4)))
    down_weight = centred(streams_of[11], (LAYERS, D, FF), FF ** -0.5, 0.078125, ((1, 8), (2, 4)))
    return dict(tokens=tokens, segments=segments, cotangent=cotangent, first_gain=first_gain, first_bias=first_bias, qkv_weight=qkv_weight, qkv_bias=qkv_bias, out_weight=out_weight, second_gain=second_gain, second_bias=second_bias, gate_up_weight=gate_up_weight, down_weight=down_weight)


NORM_EPS = 1e-05
MASK_FILL = -1e+30
PRECISE = lax.Precision.HIGHEST

@jax.custom_vjp
def low(v):
    return lax.optimization_barrier(v.astype(jnp.bfloat16)).astype(jnp.float32)

@jax.custom_vjp
def low_back(v):
    return v

def low_keep(v):
    return (low(v), None)

def low_pass(kept, grad):
    return (grad,)

def back_keep(v):
    return (v, None)

def back_low(kept, grad):
    return (low(grad),)
low.defvjp(low_keep, low_pass)
low_back.defvjp(back_keep, back_low)

def layer_norm(values, gain_vec, offset):
    center = values - lax.optimization_barrier(jnp.mean(values, axis=-1, keepdims=True))
    inverse = lax.rsqrt(lax.optimization_barrier(jnp.mean(center * center, axis=-1, keepdims=True)) + NORM_EPS)
    return center * inverse * gain_vec + offset

def frequencies():
    return jnp.exp(jnp.arange(ROT // 2, dtype=jnp.float32) * (-2.0 * math.log(10000.0) / ROT))

def rotate(tensor, cosine_table, sine_table):
    half_rot = ROT // 2
    first_part = tensor[..., :half_rot]
    second_part = tensor[..., half_rot:ROT]
    cos_b = cosine_table[:, None, :]
    sin_b = sine_table[:, None, :]
    return jnp.concatenate([first_part * cos_b - second_part * sin_b, second_part * cos_b + first_part * sin_b, tensor[..., ROT:]], axis=-1)

def geometry(segment_row):
    places = jnp.arange(SEQ_LEN, dtype=jnp.int32)
    starts = lax.optimization_barrier(jnp.sum((segment_row[None, :] < segment_row[:, None]).astype(jnp.int32), axis=1))
    angles = (places - starts).astype(jnp.float32)[:, None] * frequencies()[None, :]
    allowed = (segment_row[:, None] == segment_row[None, :]) & (places[None, :] <= places[:, None])
    return (jnp.cos(angles), jnp.sin(angles), allowed)

def one_layer(values, cosine_table, sine_table, allowed, gain_one, bias_one, w_qkv, b_qkv, w_out, gain_two, bias_two, w_gate_up, w_down):
    head_shape = (SEQ_LEN, HEADS, HEAD)
    normed_one = low(layer_norm(values, gain_one, bias_one))
    projected = low_back(jnp.einsum('sd,dcf->scf', normed_one, w_qkv, precision=PRECISE) + b_qkv[None])
    queries = low(rotate(projected[:, 0].reshape(head_shape), cosine_table, sine_table))
    keys_rot = low(rotate(projected[:, 1].reshape(head_shape), cosine_table, sine_table))
    values_h = low(projected[:, 2].reshape(head_shape))
    scores = low_back(jnp.einsum('qhe,khe->hqk', queries, keys_rot, precision=PRECISE) * (1.0 / math.sqrt(HEAD)))
    scores = jnp.where(allowed[None], scores, MASK_FILL)
    highest = lax.optimization_barrier(jnp.max(scores, axis=-1, keepdims=True))
    exponent = jnp.exp(scores - highest)
    probabilities = low(exponent / lax.optimization_barrier(jnp.sum(exponent, axis=-1, keepdims=True)))
    mixed_heads = jnp.einsum('hqk,khe->qhe', probabilities, values_h, precision=PRECISE).reshape(SEQ_LEN, D)
    mixed_heads = low(low_back(mixed_heads))
    attended = low_back(jnp.einsum('si,oi->so', mixed_heads, w_out, precision=PRECISE))
    middle = values + attended
    normed_two = low(layer_norm(middle, gain_two, bias_two))
    gate_up = low_back(jnp.einsum('sd,dcf->scf', normed_two, w_gate_up, precision=PRECISE))
    hidden = low(jax.nn.silu(gate_up[:, 0]) * gate_up[:, 1])
    branch = low_back(jnp.einsum('sf,df->sd', hidden, w_down, precision=PRECISE))
    return middle + branch

def forward_seq(values, cosine_table, sine_table, allowed, params):
    for layer_no in range(LAYERS):
        values = one_layer(values, cosine_table, sine_table, allowed, *[param_arr[layer_no] for param_arr in params])
    return values

def reference(tokens, segments, cotangent, first_gain, first_bias, qkv_weight, qkv_bias, out_weight, second_gain, second_bias, gate_up_weight, down_weight):
    params = tuple((array_in.astype(jnp.float32) for array_in in (first_gain, first_bias, qkv_weight, qkv_bias, out_weight, second_gain, second_bias, gate_up_weight, down_weight)))
    zero_grads = tuple((jnp.zeros_like(array_in) for array_in in params))

    def one_seq(totals, sequence_item):
        values, segment_row, cot_row = sequence_item
        cosine_table, sine_table, allowed = geometry(segment_row)

        def run_layers(inputs, *weight_list):
            return forward_seq(inputs, cosine_table, sine_table, allowed, weight_list)
        result, pullback = jax.vjp(run_layers, values.astype(jnp.float32), *params)
        gradients = pullback(cot_row.astype(jnp.float32))
        totals = tuple((running + fresh for running, fresh in zip(totals, gradients[1:])))
        return (totals, (result.astype(jnp.bfloat16), gradients[0]))
    totals, (outputs, input_grads) = lax.scan(one_seq, zero_grads, (tokens, segments, cotangent))
    return (outputs, input_grads, totals[0], totals[1], totals[2], totals[3], totals[4], totals[5], totals[6], totals[7], totals[8])
```

```python
import math

import jax
import jax.numpy as jnp
from jax import lax
from jax.sharding import Mesh
from jax.sharding import PartitionSpec as P

HEAD = 64
ROT = 16
LAYERS = 2
NORM_EPS = 1e-05
MASK_FILL = -1e30
LOW = jnp.bfloat16
F32 = jnp.float32


def dot(a, b, dims):
    return lax.dot_general(a, b, (dims, ((), ())), preferred_element_type=F32)


def nn(a, b):
    return dot(a, b, ((1,), (0,)))


def nt(a, b):
    return dot(a, b, ((1,), (1,)))


def tn(a, b):
    return dot(a, b, ((0,), (0,)))


def normalize(values):
    center = values - jnp.mean(values, axis=-1, keepdims=True)
    inverse = lax.rsqrt(jnp.mean(center * center, axis=-1, keepdims=True) + NORM_EPS)
    return center * inverse, inverse


def norm_back(upstream, normed, inverse, gain_vec):
    scaled = upstream * gain_vec
    return inverse * (
        scaled
        - jnp.mean(scaled, axis=-1, keepdims=True)
        - normed * jnp.mean(scaled * normed, axis=-1, keepdims=True)
    )


def make_program(n_dp, n_chi, n_clo, n_mp):
    dp_bits = [("dp", 1 << k) for k in range(int(math.log2(n_dp)))]
    chi_bits = [("chi", 1 << k) for k in range(int(math.log2(n_chi)))]
    group_bits = chi_bits + dp_bits
    n_groups = n_dp * n_chi
    sizes = {"dp": n_dp, "chi": n_chi, "clo": n_clo, "mp": n_mp}

    def swap(value, axis, bit):
        return lax.ppermute(value, axis, [(i, i ^ bit) for i in range(sizes[axis])])

    def bit_set(axis, bit):
        return (lax.axis_index(axis) & bit) != 0

    def relative(value, axis):
        rest = value.shape[:axis]
        width = value.shape[axis]
        tail = value.shape[axis + 1 :]
        for k, (name, bit) in enumerate(group_bits):
            inner = width // n_groups << k
            parts = value.reshape(rest + (width // (2 * inner), 2, inner) + tail)
            flipped = jnp.flip(parts, len(rest) + 1)
            value = jnp.where(bit_set(name, bit), flipped, parts).reshape(
                rest + (width,) + tail
            )
        return value

    def gather_half(part, order):
        blocks = {0: part}
        for k in order:
            name, bit = group_bits[k]
            fresh = {r | (1 << k): swap(block, name, bit) for r, block in blocks.items()}
            blocks.update(fresh)
        return [blocks[r] for r in range(n_groups)]

    def reduce_half(blocks, order):
        blocks = dict(enumerate(blocks))
        for k in order:
            name, bit = group_bits[k]
            for r in [r for r in blocks if r & (1 << k)]:
                moved = swap(blocks.pop(r).astype(LOW), name, bit)
                blocks[r ^ (1 << k)] = blocks[r ^ (1 << k)] + moved.astype(F32)
        return blocks[0]

    up_order = list(range(len(group_bits)))
    down_order = up_order[::-1]

    def fetch(low_cols, high_cols):
        odd = bit_set("clo", 1)
        keep = jnp.where(odd, high_cols, low_cols)
        other = swap(jnp.where(odd, low_cols, high_cols), "clo", 1)
        first, second = jnp.where(odd, other, keep), jnp.where(odd, keep, other)
        first = gather_half(first, up_order)
        second = gather_half(second, down_order)
        return jnp.concatenate([x for pair in zip(first, second) for x in pair], axis=0)

    def spread(grad):
        rows = grad.shape[0] // (2 * n_groups)
        parts = [grad[i * rows : (i + 1) * rows] for i in range(2 * n_groups)]
        first = reduce_half(parts[0::2], down_order)
        second = reduce_half(parts[1::2], up_order)
        odd = bit_set("clo", 1)
        keep = jnp.where(odd, second, first)
        other = swap(jnp.where(odd, first, second).astype(LOW), "clo", 1).astype(F32)
        return jnp.where(odd, other, keep), jnp.where(odd, keep, other)

    def token_gather(own):
        half = [own] + [swap(own, "mp", r) for r in range(1, n_mp)]
        half = jnp.concatenate(half, axis=0)
        return jnp.concatenate([half, swap(half, "clo", 1)], axis=0)

    def token_reduce(partial):
        rows = partial.shape[0] // 2
        moved = swap(partial[rows:].astype(LOW), "clo", 1)
        half = partial[:rows] + moved.astype(F32)
        own = rows // n_mp
        total = half[:own]
        for r in range(1, n_mp):
            total = total + swap(half[r * own : (r + 1) * own].astype(LOW), "mp", r).astype(F32)
        return total

    def own_tokens(value):
        seqs, block, width = value.shape
        sub = block * n_chi // n_mp
        per_block = block // sub
        place = lax.axis_index("mp") % per_block
        mine = lax.dynamic_slice_in_dim(value, place * sub, sub, 1)
        chi = lax.axis_index("chi")
        here = lax.dynamic_index_in_dim(mine, chi, 0, keepdims=False)
        there = swap(lax.dynamic_index_in_dim(mine, 1 - chi, 0, keepdims=False), "chi", 1)
        return jnp.where(lax.axis_index("mp") // per_block == chi, here, there)

    def tokens_out(own, block):
        sub, width = own.shape
        per_block = block // sub
        chi, mp = lax.axis_index("chi"), lax.axis_index("mp")
        parts = jnp.stack([own] + [swap(own, "mp", r) for r in range(1, n_mp)])
        parts = parts.reshape(n_chi, per_block, sub, width)
        parts = jnp.where(mp % per_block == 1, jnp.flip(parts, 1), parts)
        parts = parts.reshape(n_chi, block, width)
        here = (mp // per_block) == chi
        mine = jnp.where(here, parts[0], parts[1])
        moved = swap(jnp.where(here, parts[1], parts[0]), "chi", 1)
        return jnp.where(chi == 0, jnp.stack([mine, moved]), jnp.stack([moved, mine]))

    def on_device(
        tokens, segments, cotangent, first_gain, first_bias, qkv_weight, qkv_bias,
        out_weight, second_gain, second_bias, gate_up_weight, down_weight,
    ):
        n_seq, block, width = tokens.shape
        rows_dev = qkv_weight.shape[1]
        half_in = qkv_weight.shape[3] // 2
        half_ff = down_weight.shape[2] // 2
        heads = half_in // HEAD
        total = block * n_chi * n_clo
        sub = total // (n_clo * n_mp)
        mp, clo, chi = (lax.axis_index(a) for a in ("mp", "clo", "chi"))

        x_own = relative(own_tokens(tokens), 1).astype(F32)
        dx = relative(own_tokens(cotangent), 1)

        weights = []
        for l in range(LAYERS):
            qkv = qkv_weight[l]
            gu = gate_up_weight[l]
            weights.append(
                (
                    fetch(
                        qkv[:, :, :half_in].reshape(rows_dev, -1),
                        qkv[:, :, half_in:].reshape(rows_dev, -1),
                    ),
                    fetch(out_weight[l][:, :half_in], out_weight[l][:, half_in:]),
                    fetch(
                        gu[:, :, :half_ff].reshape(rows_dev, -1),
                        gu[:, :, half_ff:].reshape(rows_dev, -1),
                    ),
                    fetch(down_weight[l][:, :half_ff], down_weight[l][:, half_ff:]),
                )
            )
        gains = relative(
            jnp.stack([first_gain, first_bias, second_gain, second_bias]), 2
        )
        half_bias = jnp.where(clo == 1, qkv_bias[:, :, half_in:], qkv_bias[:, :, :half_in])

        there = swap(lax.dynamic_index_in_dim(segments, 1 - chi, 0, keepdims=False), "chi", 1)
        here = lax.dynamic_index_in_dim(segments, chi, 0, keepdims=False)
        pair = jnp.stack([jnp.where(chi == 0, here, there), jnp.where(chi == 0, there, here)])
        other = swap(pair, "clo", 1)
        whole = jnp.stack(
            [jnp.where(clo == 0, pair, other), jnp.where(clo == 0, other, pair)], axis=1
        ).reshape(total)
        core_of = jnp.arange(n_clo, dtype=jnp.int32) ^ clo
        mp_of = jnp.arange(n_mp, dtype=jnp.int32) ^ mp
        per_block = block // sub
        place = (
            (mp_of // per_block * (n_clo * block) + mp_of % per_block * sub)[None, :, None]
            + (core_of * block)[:, None, None]
            + jnp.arange(sub, dtype=jnp.int32)[None, None, :]
        ).reshape(total)
        match = place[:, None] == jnp.arange(total, dtype=jnp.int32)[None, :]
        seg = jnp.sum(jnp.where(match, whole[None, :], 0), axis=1)
        starts = jnp.sum((seg[None, :] < seg[:, None]).astype(jnp.int32), axis=1)
        freq = jnp.exp(
            jnp.arange(ROT // 2, dtype=F32) * (-2.0 * math.log(10000.0) / ROT)
        )
        angles = (place - starts).astype(F32)[:, None] * freq[None, :]
        cos_t, sin_t = jnp.cos(angles)[:, None, :], jnp.sin(angles)[:, None, :]
        allowed = (seg[:, None] == seg[None, :]) & (place[None, :] <= place[:, None])

        def rotate(value, sign):
            a, b = value[..., : ROT // 2], value[..., ROT // 2 : ROT]
            return jnp.concatenate(
                [a * cos_t - sign * b * sin_t, b * cos_t + sign * a * sin_t, value[..., ROT:]],
                axis=-1,
            )

        scale = 1.0 / math.sqrt(HEAD)

        def scores_of(q, k):
            s = jnp.einsum("qhe,khe->hqk", q, k, preferred_element_type=F32) * scale
            return jnp.where(allowed[None], s, MASK_FILL)

        saved = []
        for l in range(LAYERS):
            w_qkv, w_out, w_gu, w_down = weights[l]
            n1, inv1 = normalize(x_own)
            h1 = token_gather((n1 * gains[0, l] + gains[1, l]).astype(LOW))
            p = nn(h1, w_qkv).reshape(total, 3, heads, HEAD) + half_bias[l].reshape(
                1, 3, heads, HEAD
            )
            q = rotate(p[:, 0], 1.0).astype(LOW)
            k = rotate(p[:, 1], 1.0).astype(LOW)
            v = p[:, 2].astype(LOW)
            s = scores_of(q, k)
            top = jnp.max(s, axis=-1, keepdims=True)
            e = jnp.exp(s - top)
            den = jnp.sum(e, axis=-1, keepdims=True)
            log_total = top + jnp.log(den)
            w = (e / den).astype(LOW)
            o = jnp.einsum("hqk,khe->qhe", w, v, preferred_element_type=F32)
            o = o.reshape(total, half_in).astype(LOW)
            y_own = x_own + token_reduce(nt(o, w_out))
            n2, inv2 = normalize(y_own)
            h2 = token_gather((n2 * gains[2, l] + gains[3, l]).astype(LOW))
            gu = nn(h2, w_gu)
            g, u = gu[:, :half_ff], gu[:, half_ff:]
            z = (jax.nn.silu(g) * u).astype(LOW)
            x_own = y_own + token_reduce(nt(z, w_down))
            saved.append((h1, n1, inv1, q, k, v, log_total, o, h2, n2, inv2, gu, z))

        activations = tokens_out(relative(x_own.astype(LOW), 1), block)

        dx = dx.astype(F32)
        weight_grads = [None] * LAYERS
        small_grads = [None] * LAYERS
        for l in reversed(range(LAYERS)):
            w_qkv, w_out, w_gu, w_down = weights[l]
            h1, n1, inv1, q, k, v, log_total, o, h2, n2, inv2, gu, z = saved[l]
            dm = token_gather(dx.astype(LOW))
            dz = nn(dm, w_down)
            g, u = gu[:, :half_ff], gu[:, half_ff:]
            sig = jax.nn.sigmoid(g)
            dg = dz * u * sig * (1.0 + g * (1.0 - sig))
            du = dz * g * sig
            dp2 = jnp.concatenate([dg.astype(LOW), du.astype(LOW)], axis=1)
            dh2 = token_reduce(nt(dp2, w_gu))
            g_down = spread(tn(dm, z))
            g_gu = spread(tn(h2, dp2))
            dy = dx + norm_back(dh2, n2, inv2, gains[2, l])
            da = token_gather(dy.astype(LOW))
            do = nn(da, w_out).astype(LOW).reshape(total, heads, HEAD)
            prob = jnp.exp(scores_of(q, k) - log_total)
            dw = jnp.einsum("qhe,khe->hqk", do, v, preferred_element_type=F32)
            dv = jnp.einsum("hqk,qhe->khe", prob.astype(LOW), do, preferred_element_type=F32)
            ds = (prob * (dw - jnp.sum(prob * dw, axis=-1, keepdims=True))).astype(LOW)
            dq = jnp.einsum("hqk,khe->qhe", ds, k, preferred_element_type=F32) * scale
            dk = jnp.einsum("hqk,qhe->khe", ds, q, preferred_element_type=F32) * scale
            dp1 = jnp.stack([rotate(dq, -1.0), rotate(dk, -1.0), dv], axis=1).astype(LOW)
            dp1 = dp1.reshape(total, 3 * half_in)
            dh1 = token_reduce(nt(dp1, w_qkv))
            g_out = spread(tn(da, o))
            g_qkv = spread(tn(h1, dp1))
            dx = dy + norm_back(dh1, n1, inv1, gains[0, l])
            weight_grads[l] = (g_qkv, g_out, g_gu, g_down)
            small_grads[l] = (
                jnp.sum(dh1 * n1, axis=0),
                jnp.sum(dh1, axis=0),
                jnp.sum(dh2 * n2, axis=0),
                jnp.sum(dh2, axis=0),
                jnp.sum(dp1.astype(F32), axis=0),
            )
        tokens_grad = tokens_out(relative(dx.astype(LOW), 1), block).astype(F32)

        norms = relative(
            jnp.stack([jnp.stack([small_grads[l][i] for l in range(LAYERS)]) for i in range(4)]), 2
        )
        bias = jnp.stack([small_grads[l][4] for l in range(LAYERS)]).reshape(LAYERS, 3, half_in)
        for name, bit in [("mp", 1 << k) for k in range(int(math.log2(n_mp)))] + [("clo", 1)]:
            norms = norms + swap(norms, name, bit)
        for name, bit in group_bits:
            norms = norms + swap(norms, name, bit)
            bias = bias + swap(bias, name, bit)
        bias_other = swap(bias, "clo", 1)
        bias = jnp.concatenate(
            [jnp.where(clo == 0, bias, bias_other), jnp.where(clo == 0, bias_other, bias)], axis=2
        )

        def joined(i, parts):
            return jnp.stack(
                [
                    jnp.concatenate(
                        [
                            piece.reshape((rows_dev,) + parts + (-1,))
                            for piece in weight_grads[l][i]
                        ],
                        axis=-1,
                    )
                    for l in range(LAYERS)
                ]
            )

        return (
            activations, tokens_grad, norms[0], norms[1], joined(0, (3,)), bias,
            joined(1, ()), norms[2], norms[3], joined(2, (2,)), joined(3, ()),
        )

    return on_device


def solution(mesh):
    n_dp, n_ctx, n_mp = (mesh.shape[a] for a in ("dp", "ctx", "mp"))
    n_clo = 2
    n_chi = n_ctx // n_clo
    fine = Mesh(mesh.devices.reshape(n_dp, n_chi, n_clo, n_mp), ("dp", "chi", "clo", "mp"))
    rows = ("dp", "chi", "clo")
    ctx = ("chi", "clo")
    return jax.shard_map(
        make_program(n_dp, n_chi, n_clo, n_mp),
        mesh=fine,
        in_specs=(
            P("dp", ctx, None),
            P("dp", ctx),
            P("dp", ctx, None),
            P(),
            P(),
            P(None, rows, None, "mp"),
            P(None, None, "mp"),
            P(None, rows, "mp"),
            P(),
            P(),
            P(None, rows, None, "mp"),
            P(None, rows, "mp"),
        ),
        out_specs=(
            P("dp", ctx, None),
            P("dp", ctx, None),
            P(),
            P(),
            P(None, rows, None, "mp"),
            P(None, None, "mp"),
            P(None, rows, "mp"),
            P(),
            P(),
            P(None, rows, None, "mp"),
            P(None, rows, "mp"),
        ),
        check_vma=False,
    )
```

```python
import functools
import math

import jax
import jax.numpy as jnp
from jax import lax
from jax.experimental import pallas as pl
from jax.experimental.pallas import tpu as pltpu
from jax.sharding import Mesh
from jax.sharding import PartitionSpec as P

HEAD = 64
ROT = 16
LAYERS = 2
NORM_EPS = 1e-05
MASK_FILL = -1e30
LOW = jnp.bfloat16
F32 = jnp.float32
VMEM_LIMIT = 44 * 1024 * 1024
ANY = pl.BlockSpec(memory_space=pl.ANY)
VMEM = pl.BlockSpec(memory_space=pltpu.VMEM)


def dot(a, b, dims):
    return lax.dot_general(a, b, (dims, ((), ())), preferred_element_type=F32)


def nn(a, b):
    return dot(a, b, ((1,), (0,)))


def nt(a, b):
    return dot(a, b, ((1,), (1,)))


def tn(a, b):
    return dot(a, b, ((0,), (0,)))


def shape(dims, kind):
    return jax.ShapeDtypeStruct(dims, kind)


def call(body, n_any, args, outs, scratch, flops):
    moved = sum(a.size * a.dtype.itemsize for a in args)
    moved += sum(math.prod(o.shape) * jnp.dtype(o.dtype).itemsize for o in outs)
    return pl.pallas_call(
        body,
        out_shape=tuple(outs),
        in_specs=[ANY] * n_any + [VMEM] * (len(args) - n_any),
        out_specs=tuple([VMEM] * len(outs)),
        scratch_shapes=scratch,
        compiler_params=pltpu.CompilerParams(vmem_limit_bytes=VMEM_LIMIT),
        cost_estimate=pl.CostEstimate(flops=flops, bytes_accessed=moved, transcendentals=0),
    )(*args)


def into_rows(pieces, whole, sems, first):
    copies, row = [], 0
    for i, piece in enumerate(pieces):
        rows = piece.shape[0]
        copies.append(
            pltpu.make_async_copy(piece, whole.at[pl.ds(row, rows)], sems.at[first + i])
        )
        row += rows
    return copies


def start_all(copies):
    for c in copies:
        c.start()


def wait_all(copies):
    for c in copies:
        c.wait()


def rolled(value, cos_t, sa, sb, sign):
    width = value.shape[1]
    ahead = pltpu.roll(value, width - ROT // 2, 1)
    behind = pltpu.roll(value, ROT // 2, 1)
    return value * cos_t + sign * (ahead * sa + behind * sb)


def allowed_of(pc, sc, pr, sr):
    return (sc == sr) & (pr <= pc)


def put_halves(tile, cols, own_ref, send_ref):
    half = own_ref.shape[0]
    own_ref[:, cols] = tile[:half]
    send_ref[:, cols] = tile[half:].astype(LOW)


def softmax_of(q_h, k, allowed, scale):
    s = jnp.where(allowed, nt(q_h, k) * scale, MASK_FILL)
    top = jnp.max(s, axis=-1, keepdims=True)
    e = jnp.exp(s - top)
    return e / jnp.sum(e, axis=-1, keepdims=True)


def attn_forward(n_h, n_w, heads, *refs):
    h_parts, w_parts, refs = refs[:n_h], refs[n_h : n_h + n_w], refs[n_h + n_w :]
    bias, pc, sc, pr, sr, cos_t, sa, sb = refs[:8]
    q_o, k_o, v_o, o_o, own_o, send_o, h_s, w_s, acc, sems = refs[8:]
    width = heads * HEAD
    copies = into_rows(h_parts, h_s, sems, 0)
    w_copies = into_rows(w_parts, w_s, sems, n_h)
    start_all(copies + w_copies)
    wait_all(copies)
    block = w_s.shape[0] // (n_w // 2)
    for r in range(n_w // 2):
        wait_all(w_copies[2 * r : 2 * r + 2])
        rows = slice(r * block, (r + 1) * block)
        for c in range(3):
            cols = slice(c * width, (c + 1) * width)
            part = nn(h_s[:, rows], w_s[rows, cols])
            acc[:, cols] = part + (bias[:, cols] if r == 0 else acc[:, cols])
    q_o[...] = rolled(acc[:, :width], cos_t[...], sa[...], sb[...], 1.0).astype(LOW)
    k_o[...] = rolled(acc[:, width : 2 * width], cos_t[...], sa[...], sb[...], 1.0).astype(LOW)
    v_o[...] = acc[:, 2 * width :].astype(LOW)
    lane = lax.broadcasted_iota(jnp.int32, (1, width), 1) // HEAD
    allowed = allowed_of(pc[...], sc[...], pr[...], sr[...])
    k, v, q = k_o[...], v_o[...], q_o[...]
    zero = jnp.zeros((), LOW)
    o = None
    for h in range(heads):
        mine = lane == h
        w = softmax_of(jnp.where(mine, q, zero), k, allowed, 1.0 / math.sqrt(HEAD))
        part = nn(w.astype(LOW), jnp.where(mine, v, zero))
        o = part if o is None else o + part
    o_o[...] = o.astype(LOW)
    o = o_o[...]
    for r in range(n_w // 2):
        rows = slice(r * block, (r + 1) * block)
        put_halves(nt(o, w_s[rows, 3 * width :]), rows, own_o, send_o)


def attn_backward(n_h, n_w, heads, *refs):
    d_parts, w_parts, refs = refs[:n_h], refs[n_h : n_h + n_w], refs[n_h + n_w :]
    q_i, k_i, v_i, pc, sc, pr, sr, cos_t, sa, sb = refs[:10]
    dp_o, bias_o, own_o, send_o, d_s, w_s, acc, sems = refs[10:]
    width = heads * HEAD
    copies = into_rows(d_parts, d_s, sems, 0)
    w_copies = into_rows(w_parts, w_s, sems, n_h)
    start_all(copies + w_copies)
    wait_all(copies)
    block = w_s.shape[0] // (n_w // 2)
    for r in range(n_w // 2):
        wait_all(w_copies[2 * r : 2 * r + 2])
        rows = slice(r * block, (r + 1) * block)
        part = nn(d_s[:, rows], w_s[rows, 3 * width :])
        acc[...] = part if r == 0 else acc[...] + part
    do = acc[...].astype(LOW)
    q, k, v = q_i[...], k_i[...], v_i[...]
    lane = lax.broadcasted_iota(jnp.int32, (1, width), 1) // HEAD
    allowed = allowed_of(pc[...], sc[...], pr[...], sr[...])
    zero = jnp.zeros((), LOW)
    scale = 1.0 / math.sqrt(HEAD)
    dq = dk = dv = None
    for h in range(heads):
        mine = lane == h
        q_h = jnp.where(mine, q, zero)
        do_h = jnp.where(mine, do, zero)
        w = softmax_of(q_h, k, allowed, scale)
        dw = nt(do_h, v)
        ds = (w * (dw - jnp.sum(w * dw, axis=-1, keepdims=True))).astype(LOW)
        dv_h = tn(w.astype(LOW), do_h)
        dq_h = nn(ds, jnp.where(mine, k, zero))
        dk_h = tn(ds, q_h)
        dq, dk, dv = (
            (dq_h, dk_h, dv_h) if h == 0 else (dq + dq_h, dk + dk_h, dv + dv_h)
        )
    dp_o[:, :width] = rolled(dq * scale, cos_t[...], sa[...], sb[...], -1.0).astype(LOW)
    dp_o[:, width : 2 * width] = rolled(
        dk * scale, cos_t[...], sa[...], sb[...], -1.0
    ).astype(LOW)
    dp_o[:, 2 * width :] = dv.astype(LOW)
    bias_o[...] = jnp.sum(dp_o[...].astype(F32), axis=0, keepdims=True)
    for r in range(n_w // 2):
        rows = slice(r * block, (r + 1) * block)
        put_halves(nt(dp_o[...], w_s[rows, : 3 * width]), rows, own_o, send_o)


def to_front(value, units):
    return value[:, units : 2 * units]


def mlp_forward(n_h, n_w, *refs):
    h_parts, w_parts, refs = refs[:n_h], refs[n_h : n_h + n_w], refs[n_h + n_w :]
    gu_o, z_o, own_o, send_o, h_s, w_s, sems = refs
    units = z_o.shape[1]
    copies = into_rows(h_parts, h_s, sems, 0)
    w_copies = into_rows(w_parts, w_s, sems, n_h)
    start_all(copies + w_copies)
    wait_all(copies)
    block = w_s.shape[0] // (n_w // 2)
    for r in range(n_w // 2):
        wait_all(w_copies[2 * r : 2 * r + 2])
        rows = slice(r * block, (r + 1) * block)
        part = nn(h_s[:, rows], w_s[rows, : 2 * units])
        gu_o[...] = part if r == 0 else gu_o[...] + part
    g = gu_o[:, :units]
    u = to_front(gu_o, units)
    z_o[...] = (g * u / (1.0 + jnp.exp(-g))).astype(LOW)
    z = z_o[...]
    for r in range(n_w // 2):
        rows = slice(r * block, (r + 1) * block)
        put_halves(nt(z, w_s[rows, 2 * units :]), rows, own_o, send_o)


def mlp_backward(n_h, n_w, *refs):
    d_parts, w_parts, refs = refs[:n_h], refs[n_h : n_h + n_w], refs[n_h + n_w :]
    gu_i, dp_o, own_o, send_o, d_s, w_s, acc, sems = refs
    units = acc.shape[1]
    copies = into_rows(d_parts, d_s, sems, 0)
    w_copies = into_rows(w_parts, w_s, sems, n_h)
    start_all(copies + w_copies)
    wait_all(copies)
    block = w_s.shape[0] // (n_w // 2)
    for r in range(n_w // 2):
        wait_all(w_copies[2 * r : 2 * r + 2])
        rows = slice(r * block, (r + 1) * block)
        part = nn(d_s[:, rows], w_s[rows, 2 * units :])
        acc[...] = part if r == 0 else acc[...] + part
    g = gu_i[:, :units]
    u = to_front(gu_i, units)
    sig = 1.0 / (1.0 + jnp.exp(-g))
    dz = acc[...]
    dp_o[:, :units] = (dz * u * sig * (1.0 + g * (1.0 - sig))).astype(LOW)
    dp_o[:, units:] = (dz * g * sig).astype(LOW)
    dp = dp_o[...]
    for r in range(n_w // 2):
        rows = slice(r * block, (r + 1) * block)
        put_halves(nt(dp, w_s[rows, : 2 * units]), rows, own_o, send_o)


def weight_grads(n_h, n_w, *refs):
    a_parts, b_parts, refs = refs[:n_h], refs[n_h : 2 * n_h], refs[2 * n_h :]
    da, db = refs[:2]
    outs, (a_s, b_s, sems) = refs[2 : 2 + n_w], refs[2 + n_w :]
    copies = into_rows(a_parts, a_s, sems, 0) + into_rows(b_parts, b_s, sems, n_h)
    start_all(copies)
    wait_all(copies)
    block = a_s.shape[1] // (n_w // 2)
    half = block // 2
    split = da.shape[1]
    for r in range(n_w // 2):
        cols = slice(r * block, (r + 1) * block)
        first = tn(a_s[:, cols], da[...]).astype(LOW)
        second = tn(b_s[:, cols], db[...]).astype(LOW)
        for i in range(2):
            rows = slice(i * half, (i + 1) * half)
            outs[2 * r + i][:, :split] = first[rows]
            outs[2 * r + i][:, split:] = second[rows]


def middle(own_i, moved_i, own_o, *sends):
    rows = own_o.shape[0]
    own_o[...] = own_i[:rows] + moved_i[:rows].astype(F32)
    for r, send in enumerate(sends):
        at = slice((r + 1) * rows, (r + 2) * rows)
        send[...] = (own_i[at] + moved_i[at].astype(F32)).astype(LOW)


def norm_of(value):
    center = value - jnp.mean(value, axis=-1, keepdims=True)
    inverse = lax.rsqrt(jnp.mean(center * center, axis=-1, keepdims=True) + NORM_EPS)
    return center * inverse, inverse


def norm_forward(x_i, gain, offset, *refs):
    terms, (x_o, h_o) = refs[:-2], refs[-2:]
    x = x_i[...]
    for t in terms:
        x = x + t[...].astype(F32)
    x_o[...] = x
    h_o[...] = (norm_of(x)[0] * gain[...] + offset[...]).astype(LOW)


def norm_backward(dx_i, y_i, gain, *refs):
    terms, (dy_o, low_o, small_o) = refs[:-3], refs[-3:]
    dh = terms[0][...]
    for t in terms[1:]:
        dh = dh + t[...].astype(F32)
    n, inverse = norm_of(y_i[...])
    small_o[0:1] = jnp.sum(dh * n, axis=0, keepdims=True)
    small_o[1:2] = jnp.sum(dh, axis=0, keepdims=True)
    scaled = dh * gain[...]
    dy = dx_i[...] + inverse * (
        scaled
        - jnp.mean(scaled, axis=-1, keepdims=True)
        - n * jnp.mean(scaled * n, axis=-1, keepdims=True)
    )
    dy_o[...] = dy
    low_o[...] = dy.astype(LOW)


def log2(n):
    return n.bit_length() - 1


def make_program(n_dp, n_chi, n_clo, n_mp):
    group_bits = [("chi", 1 << k) for k in range(log2(n_chi))]
    group_bits += [("dp", 1 << k) for k in range(log2(n_dp))]
    n_groups = n_dp * n_chi
    n_pieces = 2 * n_groups
    sizes = {"dp": n_dp, "chi": n_chi, "clo": n_clo, "mp": n_mp}
    up_order = list(range(len(group_bits)))
    down_order = up_order[::-1]

    def swap(value, axis, bit):
        return lax.ppermute(value, axis, [(i, i ^ bit) for i in range(sizes[axis])])

    def relative(value):
        block = value.shape[-1] // n_groups
        me = lax.axis_index("dp") * n_chi + lax.axis_index("chi")
        parts = [
            lax.dynamic_slice_in_dim(value, (me ^ r) * block, block, value.ndim - 1)
            for r in range(n_groups)
        ]
        return jnp.concatenate(parts, axis=-1)

    def gather_weights(low_cols, high_cols):
        odd = lax.axis_index("clo") == 1
        keep = jnp.where(odd, high_cols, low_cols)
        other = swap(jnp.where(odd, low_cols, high_cols), "clo", 1)
        a = {0: jnp.where(odd, other, keep)}
        b = {0: jnp.where(odd, keep, other)}
        for ka, kb in zip(up_order, down_order):
            for have, k in ((a, ka), (b, kb)):
                fresh = {r | (1 << k): swap(have[r], *group_bits[k]) for r in list(have)}
                have.update(fresh)
        return [x for r in range(n_groups) for x in (a[r], b[r])]

    def spread(pieces):
        a, b = dict(enumerate(pieces[0::2])), dict(enumerate(pieces[1::2]))
        for ka, kb in zip(down_order, up_order):
            for have, k in ((a, ka), (b, kb)):
                for r in [r for r in have if r & (1 << k)]:
                    moved = swap(have.pop(r), *group_bits[k])
                    to = r ^ (1 << k)
                    have[to] = (have[to].astype(F32) + moved.astype(F32)).astype(LOW)
        odd = lax.axis_index("clo") == 1
        keep = jnp.where(odd, b[0], a[0])
        other = swap(jnp.where(odd, a[0], b[0]), "clo", 1)
        return jnp.where(odd, other, keep), jnp.where(odd, keep, other)

    def token_gather(own):
        half = [own] + [swap(own, "mp", r) for r in range(1, n_mp)]
        return half + [swap(part, "clo", 1) for part in half]

    def token_reduce(own_half, send_half):
        rows, width = own_half.shape
        sub = rows // n_mp
        moved = swap(send_half, "clo", 1)
        outs = [shape((sub, width), F32)] + [shape((sub, width), LOW)] * (n_mp - 1)
        parts = call(middle, 0, [own_half, moved], outs, [], rows * width)
        return [parts[0]] + [swap(parts[r], "mp", r) for r in range(1, n_mp)]

    def own_tokens(value):
        seqs, block, width = value.shape
        sub = block * n_chi // n_mp
        per_block = block // sub
        place = lax.axis_index("mp") % per_block
        mine = lax.dynamic_slice_in_dim(value, place * sub, sub, 1)
        chi = lax.axis_index("chi")
        here = lax.dynamic_index_in_dim(mine, chi, 0, keepdims=False)
        there = swap(lax.dynamic_index_in_dim(mine, 1 - chi, 0, keepdims=False), "chi", 1)
        return jnp.where(lax.axis_index("mp") // per_block == chi, here, there)

    def tokens_out(own, block):
        sub, width = own.shape
        per_block = block // sub
        chi, mp = lax.axis_index("chi"), lax.axis_index("mp")
        parts = jnp.stack([own] + [swap(own, "mp", r) for r in range(1, n_mp)])
        parts = parts.reshape(n_chi, per_block, sub, width)
        parts = jnp.where(mp % per_block == 1, jnp.flip(parts, 1), parts)
        parts = parts.reshape(n_chi, block, width)
        here = (mp // per_block) == chi
        mine = jnp.where(here, parts[0], parts[1])
        moved = swap(jnp.where(here, parts[1], parts[0]), "chi", 1)
        return jnp.where(chi == 0, jnp.stack([mine, moved]), jnp.stack([moved, mine]))

    def on_device(
        tokens, segments, cotangent, first_gain, first_bias, qkv_weight, qkv_bias,
        out_weight, second_gain, second_bias, gate_up_weight, down_weight,
    ):
        n_seq, block, width = tokens.shape
        rows_dev = qkv_weight.shape[1]
        half_in = qkv_weight.shape[3] // 2
        half_ff = down_weight.shape[2] // 2
        heads = half_in // HEAD
        total = block * n_chi * n_clo
        half_total = total // n_clo
        sub = half_total // n_mp
        n_parts = n_clo * n_mp
        mp, clo, chi = (lax.axis_index(a) for a in ("mp", "clo", "chi"))
        attn_cols, mlp_cols = 4 * half_in, 3 * half_ff

        x_own = relative(own_tokens(tokens)).astype(F32)

        def halves(l, which):
            lo, hi = (slice(None, half_in), slice(half_in, None)), (
                slice(None, half_ff),
                slice(half_ff, None),
            )
            out = []
            for i in range(2):
                if which == 0:
                    parts = [qkv_weight[l, :, c, lo[i]] for c in range(3)]
                    parts.append(out_weight[l, :, lo[i]])
                else:
                    parts = [gate_up_weight[l, :, c, hi[i]] for c in range(2)]
                    parts.append(down_weight[l, :, hi[i]])
                out.append(jnp.concatenate(parts, axis=1))
            return out

        weights = [
            (gather_weights(*halves(l, 0)), gather_weights(*halves(l, 1))) for l in range(LAYERS)
        ]
        dx = relative(own_tokens(cotangent))
        gains = relative(jnp.stack([first_gain, first_bias, second_gain, second_bias]))
        half_bias = jnp.where(clo == 1, qkv_bias[:, :, half_in:], qkv_bias[:, :, :half_in])
        half_bias = half_bias.reshape(LAYERS, 1, 3 * half_in)

        there = swap(lax.dynamic_index_in_dim(segments, 1 - chi, 0, keepdims=False), "chi", 1)
        here = lax.dynamic_index_in_dim(segments, chi, 0, keepdims=False)
        pair = jnp.stack([jnp.where(chi == 0, here, there), jnp.where(chi == 0, there, here)])
        other = swap(pair, "clo", 1)
        whole = jnp.stack(
            [jnp.where(clo == 0, pair, other), jnp.where(clo == 0, other, pair)], axis=1
        ).reshape(total)
        core_of = jnp.arange(n_clo, dtype=jnp.int32) ^ clo
        mp_of = jnp.arange(n_mp, dtype=jnp.int32) ^ mp
        per_block = block // sub
        place = (
            (mp_of // per_block * (n_clo * block) + mp_of % per_block * sub)[None, :, None]
            + (core_of * block)[:, None, None]
            + jnp.arange(sub, dtype=jnp.int32)[None, None, :]
        ).reshape(total)
        match = place[:, None] == jnp.arange(total, dtype=jnp.int32)[None, :]
        seg = jnp.sum(jnp.where(match, whole[None, :], 0), axis=1)
        starts = jnp.sum((seg[None, :] < seg[:, None]).astype(jnp.int32), axis=1)
        freq = jnp.exp(
            jnp.arange(ROT // 2, dtype=F32) * (-2.0 * math.log(10000.0) / ROT)
        )
        angles = freq[:, None] * (place - starts).astype(F32)[None, :]
        cos_t, sin_t = jnp.cos(angles).T, jnp.sin(angles).T
        zeros = jnp.zeros((total, ROT // 2), F32)
        tail = jnp.zeros((total, HEAD - ROT), F32)
        tables = [
            jnp.tile(jnp.concatenate(parts, axis=1), (1, heads))
            for parts in (
                (cos_t, cos_t, tail + 1.0),
                (-sin_t, zeros, tail),
                (zeros, sin_t, tail),
            )
        ]
        geometry = [place[:, None], seg[:, None], place[None, :], seg[None, :]] + tables

        act = shape((total, half_in), LOW)
        reduced = [shape((half_total, width), F32), shape((half_total, width), LOW)]
        n_w = n_pieces
        sems = pltpu.SemaphoreType.DMA((n_parts + n_w,))
        h_scratch = pltpu.VMEM((total, width), LOW)

        def mm(*dims):
            return 2 * math.prod(dims)

        def norm(x, gain, offset, terms):
            outs = [shape(x.shape, F32), shape(x.shape, LOW)]
            return call(norm_forward, 0, [x, gain[None], offset[None]] + terms, outs, [], 10 * x.size)

        def norm_back(dx, y, gain, terms):
            outs = [shape(y.shape, F32), shape(y.shape, LOW), shape((2, width), F32)]
            return call(norm_backward, 0, [dx, y, gain[None]] + terms, outs, [], 20 * y.size)

        def grads(a_parts, b_parts, da, db, cols):
            outs = [shape((width // n_w, cols), LOW)] * n_w
            return call(
                functools.partial(weight_grads, n_parts, n_w),
                2 * n_parts,
                a_parts + b_parts + [da, db],
                outs,
                [h_scratch, h_scratch, pltpu.SemaphoreType.DMA((2 * n_parts,))],
                mm(total, width, cols),
            )

        saved = []
        terms = []
        for l in range(LAYERS):
            w_attn, w_mlp = weights[l]
            x_own, h = norm(x_own, gains[0, l], gains[1, l], terms)
            h1 = token_gather(h)
            q, k, v, o, own, send = call(
                functools.partial(attn_forward, n_parts, n_w, heads),
                n_parts + n_w,
                h1 + w_attn + [half_bias[l]] + geometry,
                [act] * 4 + reduced,
                [
                    h_scratch,
                    pltpu.VMEM((width, attn_cols), LOW),
                    pltpu.VMEM((total, 3 * half_in), F32),
                    sems,
                ],
                mm(total, width, attn_cols) + 2 * mm(heads, total, total, 2 * half_in),
            )
            y_own, h = norm(x_own, gains[2, l], gains[3, l], token_reduce(own, send))
            h2 = token_gather(h)
            gu, z, own, send = call(
                functools.partial(mlp_forward, n_parts, n_w),
                n_parts + n_w,
                h2 + w_mlp,
                [shape((total, 2 * half_ff), F32), shape((total, half_ff), LOW)] + reduced,
                [h_scratch, pltpu.VMEM((width, mlp_cols), LOW), sems],
                mm(total, width, mlp_cols),
            )
            saved.append((x_own, h1, q, k, v, o, y_own, h2, gu, z))
            x_own, terms = y_own, token_reduce(own, send)
        for t in terms:
            x_own = x_own + t.astype(F32)
        activations = tokens_out(relative(x_own.astype(LOW)), block)

        low = dx
        dx = dx.astype(F32)
        weight_out = [None] * LAYERS
        small_out = [None] * LAYERS
        for l in reversed(range(LAYERS)):
            w_attn, w_mlp = weights[l]
            x_own, h1, q, k, v, o, y_own, h2, gu, z = saved[l]
            dm = token_gather(low)
            dp2, own, send = call(
                functools.partial(mlp_backward, n_parts, n_w),
                n_parts + n_w,
                dm + w_mlp + [gu],
                [shape((total, 2 * half_ff), LOW)] + reduced,
                [
                    h_scratch,
                    pltpu.VMEM((width, mlp_cols), LOW),
                    pltpu.VMEM((total, half_ff), F32),
                    sems,
                ],
                mm(total, width, mlp_cols),
            )
            terms = token_reduce(own, send)
            g_mlp = spread(grads(h2, dm, dp2, z, mlp_cols))
            dy, low, small_two = norm_back(dx, y_own, gains[2, l], terms)
            da = token_gather(low)
            dp1, bias_grad, own, send = call(
                functools.partial(attn_backward, n_parts, n_w, heads),
                n_parts + n_w,
                da + w_attn + [q, k, v] + geometry,
                [shape((total, 3 * half_in), LOW), shape((1, 3 * half_in), F32)] + reduced,
                [
                    h_scratch,
                    pltpu.VMEM((width, attn_cols), LOW),
                    pltpu.VMEM((total, half_in), F32),
                    sems,
                ],
                mm(total, width, attn_cols) + 5 * mm(heads, total, total, half_in),
            )
            terms = token_reduce(own, send)
            g_attn = spread(grads(h1, da, dp1, o, attn_cols))
            dx, low, small_one = norm_back(dy, x_own, gains[0, l], terms)
            weight_out[l] = (g_attn, g_mlp)
            small_out[l] = (small_one, small_two, bias_grad)
        tokens_grad = tokens_out(relative(low), block).astype(F32)

        norms = relative(
            jnp.stack([jnp.concatenate(small_out[l][:2], axis=0) for l in range(LAYERS)], axis=1)
        )
        bias = jnp.stack([small_out[l][2] for l in range(LAYERS)]).reshape(LAYERS, 3, half_in)
        for k in range(log2(n_mp)):
            norms = norms + swap(norms, "mp", 1 << k)
        norms = norms + swap(norms, "clo", 1)
        for name, bit in group_bits:
            norms = norms + swap(norms, name, bit)
            bias = bias + swap(bias, name, bit)
        bias_other = swap(bias, "clo", 1)
        bias = jnp.concatenate(
            [jnp.where(clo == 0, bias, bias_other), jnp.where(clo == 0, bias_other, bias)], axis=2
        )

        def columns(which, first, count, parts):
            layers = []
            for l in range(LAYERS):
                pieces = [
                    piece[:, first : first + count].reshape((rows_dev,) + parts + (-1,))
                    for piece in weight_out[l][which]
                ]
                layers.append(jnp.concatenate(pieces, axis=-1).astype(F32))
            return jnp.stack(layers)

        return (
            activations, tokens_grad, norms[0], norms[1],
            columns(0, 0, 3 * half_in, (3,)), bias,
            columns(0, 3 * half_in, half_in, ()), norms[2], norms[3],
            columns(1, 0, 2 * half_ff, (2,)), columns(1, 2 * half_ff, half_ff, ()),
        )

    return on_device


def solution(mesh):
    n_dp, n_ctx, n_mp = (mesh.shape[a] for a in ("dp", "ctx", "mp"))
    n_clo = 2
    n_chi = n_ctx // n_clo
    fine = Mesh(mesh.devices.reshape(n_dp, n_chi, n_clo, n_mp), ("dp", "chi", "clo", "mp"))
    rows = ("dp", "chi", "clo")
    ctx = ("chi", "clo")
    token_spec = P("dp", ctx, None)
    four, three = P(None, rows, None, "mp"), P(None, rows, "mp")
    bias_spec = P(None, None, "mp")
    return jax.shard_map(
        make_program(n_dp, n_chi, n_clo, n_mp),
        mesh=fine,
        in_specs=(
            token_spec, P("dp", ctx), token_spec, P(), P(), four, bias_spec, three, P(), P(),
            four, three,
        ),
        out_specs=(
            token_spec, token_spec, P(), P(), four, bias_spec, three, P(), P(), four, three,
        ),
        check_vma=False,
    )
```

```python
import functools
import math

import jax
import jax.numpy as jnp
from jax import lax
from jax.experimental import pallas as pl
from jax.experimental.pallas import tpu as pltpu
from jax.sharding import Mesh
from jax.sharding import PartitionSpec as P

HEAD = 64
ROT = 16
LAYERS = 2
NORM_EPS = 1e-05
MASK_FILL = -1e30
LOW = jnp.bfloat16
F32 = jnp.float32
VMEM_LIMIT = 44 * 1024 * 1024
HBM = pl.BlockSpec(memory_space=pltpu.HBM)
VMEM = pl.BlockSpec(memory_space=pltpu.VMEM)


def dot(a, b, dims):
    return lax.dot_general(a, b, (dims, ((), ())), preferred_element_type=F32)


def nn(a, b):
    return dot(a, b, ((1,), (0,)))


def nt(a, b):
    return dot(a, b, ((1,), (1,)))


def tn(a, b):
    return dot(a, b, ((0,), (0,)))


def shape(dims, kind):
    return jax.ShapeDtypeStruct(dims, kind)


def call(body, n_hbm, args, outs, scratch, flops, hbm_outs=0):
    moved = sum(a.size * a.dtype.itemsize for a in args)
    moved += sum(math.prod(o.shape) * jnp.dtype(o.dtype).itemsize for o in outs)
    return pl.pallas_call(
        body,
        out_shape=tuple(outs),
        in_specs=[HBM] * n_hbm + [VMEM] * (len(args) - n_hbm),
        out_specs=tuple([HBM] * hbm_outs + [VMEM] * (len(outs) - hbm_outs)),
        scratch_shapes=scratch,
        compiler_params=pltpu.CompilerParams(vmem_limit_bytes=VMEM_LIMIT),
        cost_estimate=pl.CostEstimate(flops=flops, bytes_accessed=moved, transcendentals=0),
    )(*args)


def into_rows(pieces, whole, sems, first):
    copies, row = [], 0
    for i, piece in enumerate(pieces):
        rows = piece.shape[0]
        copies.append(
            pltpu.make_async_copy(piece, whole.at[pl.ds(row, rows)], sems.at[first + i])
        )
        row += rows
    return copies


def weights_into(pieces, whole, sems, first):
    me = lax.axis_index("clo")
    copies = []
    for i, piece in enumerate(pieces):
        rows = piece.shape[0]
        at = (i // 2 * 2) * rows + (me ^ (i % 2)) * rows
        to = whole.at[pl.ds(pl.multiple_of(at, rows), rows)]
        copies.append(pltpu.make_async_copy(piece, to, sems.at[first + i]))
    return copies


def start_all(copies):
    for c in copies:
        c.start()


def wait_all(copies):
    for c in copies:
        c.wait()


def rolled(value, tables, sign):
    cos_t, ahead_t, behind_t = tables[0], tables[1], tables[2]
    slabs = []
    for at in range(0, value.shape[1], 128):
        x = value[:, at : at + 128]
        ahead = pltpu.roll(x, 128 - ROT // 2, 1)
        behind = pltpu.roll(x, ROT // 2, 1)
        slabs.append(x * cos_t + sign * (ahead * ahead_t + behind * behind_t))
    return jnp.concatenate(slabs, axis=1).astype(LOW)


def allowed_of(column, row):
    return (column[:, 0:1] == row[0:1]) & (row[1:2] <= column[:, 1:2])


def put_halves(tile, cols, own_ref, send_ref):
    half = own_ref.shape[0]
    own_ref[:, cols] = tile[:half]
    send_ref[:, cols] = tile[half:].astype(LOW)


def softmax_of(q_h, k, allowed, scale):
    s = jnp.where(allowed, nt(q_h, k) * scale, MASK_FILL)
    top = jnp.max(s, axis=-1, keepdims=True)
    e = jnp.exp(s - top)
    return e / jnp.sum(e, axis=-1, keepdims=True)


def load(pairs, sems, first):
    return [
        pltpu.make_async_copy(src, dst, sems.at[first + i]) for i, (src, dst) in enumerate(pairs)
    ]


def block_rows(w_s, n_w, w_copies=None):
    block = w_s.shape[0] // (n_w // 2)
    for r in range(n_w // 2):
        if w_copies is not None:
            wait_all(w_copies[2 * r : 2 * r + 2])
        yield r, slice(r * block, (r + 1) * block)


def attn_forward(n_h, n_w, heads, *refs):
    h_parts, w_parts, refs = refs[:n_h], refs[n_h : n_h + n_w], refs[n_h + n_w :]
    tables, column, row, bias = refs[:4]
    q_o, k_o, v_o, o_o, own_o, send_o, h_s, w_s, acc, tab, col, sems = refs[4:]
    width = heads * HEAD
    copies = into_rows(h_parts, h_s, sems, 0)
    w_copies = weights_into(w_parts, w_s, sems, n_h)
    extra = load([(tables, tab), (column, col)], sems, n_h + n_w)
    start_all(copies + w_copies + extra)
    wait_all(copies)
    for r, rows in block_rows(w_s, n_w, w_copies):
        for c in range(3):
            cols = slice(c * width, (c + 1) * width)
            part = nn(h_s[:, rows], w_s[rows, cols])
            acc[:, cols] = part + (bias[:, cols] if r == 0 else acc[:, cols])
    wait_all(extra)
    q_o[...] = rolled(acc[:, :width], tab, 1.0)
    k_o[...] = rolled(acc[:, width : 2 * width], tab, 1.0)
    v_o[...] = acc[:, 2 * width :].astype(LOW)
    lane = lax.broadcasted_iota(jnp.int32, (1, width), 1) // HEAD
    allowed = allowed_of(col, row)
    k, v, q = k_o[...], v_o[...], q_o[...]
    zero = jnp.zeros((), LOW)
    o = None
    for h in range(heads):
        mine = lane == h
        w = softmax_of(jnp.where(mine, q, zero), k, allowed, 1.0 / math.sqrt(HEAD))
        part = nn(w.astype(LOW), jnp.where(mine, v, zero))
        o = part if o is None else o + part
    o_o[...] = o.astype(LOW)
    o = o_o[...]
    for r, rows in block_rows(w_s, n_w):
        put_halves(nt(o, w_s[rows, 3 * width :]), rows, own_o, send_o)


def attn_backward(n_h, n_w, heads, *refs):
    d_parts, w_parts, refs = refs[:n_h], refs[n_h : n_h + n_w], refs[n_h + n_w :]
    q_i, k_i, v_i, tables, column, row = refs[:6]
    dp_o, bias_o, own_o, send_o, d_s, w_s, acc, qkv, tab, col, sems = refs[6:]
    width = heads * HEAD
    copies = into_rows(d_parts, d_s, sems, 0)
    w_copies = weights_into(w_parts, w_s, sems, n_h)
    extra = load(
        [(q_i, qkv.at[0]), (k_i, qkv.at[1]), (v_i, qkv.at[2]), (tables, tab), (column, col)],
        sems,
        n_h + n_w,
    )
    start_all(copies + w_copies + extra)
    wait_all(copies)
    for r, rows in block_rows(w_s, n_w, w_copies):
        part = nn(d_s[:, rows], w_s[rows, 3 * width :])
        acc[...] = part if r == 0 else acc[...] + part
    do = acc[...].astype(LOW)
    wait_all(extra)
    q, k, v = qkv[0], qkv[1], qkv[2]
    lane = lax.broadcasted_iota(jnp.int32, (1, width), 1) // HEAD
    allowed = allowed_of(col, row)
    zero = jnp.zeros((), LOW)
    scale = 1.0 / math.sqrt(HEAD)
    dq = dk = dv = None
    for h in range(heads):
        mine = lane == h
        q_h = jnp.where(mine, q, zero)
        do_h = jnp.where(mine, do, zero)
        w = softmax_of(q_h, k, allowed, scale)
        dw = nt(do_h, v)
        ds = (w * (dw - jnp.sum(w * dw, axis=-1, keepdims=True))).astype(LOW)
        dv_h = tn(w.astype(LOW), do_h)
        dq_h = nn(ds, jnp.where(mine, k, zero))
        dk_h = tn(ds, q_h)
        dq, dk, dv = (
            (dq_h, dk_h, dv_h) if h == 0 else (dq + dq_h, dk + dk_h, dv + dv_h)
        )
    dp_o[:, :width] = rolled(dq * scale, tab, -1.0)
    dp_o[:, width : 2 * width] = rolled(dk * scale, tab, -1.0)
    dp_o[:, 2 * width :] = dv.astype(LOW)
    dp = dp_o[...]
    bias_o[...] = jnp.sum(dp.astype(F32), axis=0, keepdims=True)
    for r, rows in block_rows(w_s, n_w):
        put_halves(nt(dp, w_s[rows, : 3 * width]), rows, own_o, send_o)


def mlp_forward(n_h, n_w, *refs):
    h_parts, w_parts, refs = refs[:n_h], refs[n_h : n_h + n_w], refs[n_h + n_w :]
    gu_o, z_o, own_o, send_o, h_s, w_s, sems = refs
    units = z_o.shape[1]
    copies = into_rows(h_parts, h_s, sems, 0)
    w_copies = weights_into(w_parts, w_s, sems, n_h)
    start_all(copies + w_copies)
    wait_all(copies)
    for r, rows in block_rows(w_s, n_w, w_copies):
        part = nn(h_s[:, rows], w_s[rows, : 2 * units])
        gu_o[...] = part if r == 0 else gu_o[...] + part
    g = gu_o[:, :units]
    u = gu_o[:, units:]
    z_o[...] = (g * u / (1.0 + jnp.exp(-g))).astype(LOW)
    z = z_o[...]
    for r, rows in block_rows(w_s, n_w):
        put_halves(nt(z, w_s[rows, 2 * units : 3 * units]), rows, own_o, send_o)


def mlp_backward(n_h, n_w, *refs):
    d_parts, w_parts, refs = refs[:n_h], refs[n_h : n_h + n_w], refs[n_h + n_w :]
    gu_i, dp_o, own_o, send_o, d_s, w_s, acc, gu, sems = refs
    units = acc.shape[1]
    copies = into_rows(d_parts, d_s, sems, 0)
    w_copies = weights_into(w_parts, w_s, sems, n_h)
    extra = load([(gu_i, gu)], sems, n_h + n_w)
    start_all(copies + w_copies + extra)
    wait_all(copies)
    for r, rows in block_rows(w_s, n_w, w_copies):
        part = nn(d_s[:, rows], w_s[rows, 2 * units : 3 * units])
        acc[...] = part if r == 0 else acc[...] + part
    wait_all(extra)
    g = gu[:, :units]
    u = gu[:, units:]
    sig = 1.0 / (1.0 + jnp.exp(-g))
    dz = acc[...]
    dp_o[:, :units] = (dz * u * sig * (1.0 + g * (1.0 - sig))).astype(LOW)
    dp_o[:, units:] = (dz * g * sig).astype(LOW)
    dp = dp_o[...]
    for r, rows in block_rows(w_s, n_w):
        put_halves(nt(dp, w_s[rows, : 2 * units]), rows, own_o, send_o)


def weight_grads(n_h, n_w, *refs):
    a_parts, b_parts, refs = refs[:n_h], refs[n_h : 2 * n_h], refs[2 * n_h :]
    da_i, db_i = refs[:2]
    outs, (a_s, b_s, da_s, db_s, sems) = refs[2 : 2 + n_w], refs[2 + n_w :]
    copies = into_rows(a_parts, a_s, sems, 0) + into_rows(b_parts, b_s, sems, n_h)
    copies += load([(da_i, da_s), (db_i, db_s)], sems, 2 * n_h)
    start_all(copies)
    wait_all(copies)
    block = a_s.shape[1] // (n_w // 2)
    half = block // 2
    split, end = da_s.shape[1], da_s.shape[1] + db_s.shape[1]
    swapped = lax.axis_index("clo") == 1
    for r in range(n_w // 2):
        cols = slice(r * block, (r + 1) * block)
        first = tn(a_s[:, cols], da_s[...]).astype(LOW)
        second = tn(b_s[:, cols], db_s[...]).astype(LOW)
        for i in range(2):
            here, there = slice(i * half, (i + 1) * half), slice((1 - i) * half, (2 - i) * half)
            out = outs[2 * r + i]
            out[:, :split] = jnp.where(swapped, first[there], first[here])
            out[:, split:end] = jnp.where(swapped, second[there], second[here])
            if end < out.shape[1]:
                out[:, end:] = jnp.zeros((half, out.shape[1] - end), LOW)


def cut_columns(*refs):
    qkv, out, keep, send, sems = refs
    width = keep.shape[1] // 4
    me = lax.axis_index("clo")
    copies = []
    for to, core in ((keep, me), (send, 1 - me)):
        cols = pl.ds(pl.multiple_of(core * width, 128), width)
        for c in range(4):
            src = out.at[:, cols] if c == 3 else qkv.at[c, :, cols]
            dst = to.at[:, pl.ds(c * width, width)]
            copies.append(pltpu.make_async_copy(src, dst, sems.at[len(copies)]))
    start_all(copies)
    wait_all(copies)


def middle(own_i, moved_i, own_o, *sends):
    rows = own_o.shape[0]
    own_o[...] = own_i[:rows] + moved_i[:rows].astype(F32)
    for r, send in enumerate(sends):
        at = slice((r + 1) * rows, (r + 2) * rows)
        send[...] = (own_i[at] + moved_i[at].astype(F32)).astype(LOW)


def norm_of(value):
    center = value - jnp.mean(value, axis=-1, keepdims=True)
    inverse = lax.rsqrt(jnp.mean(center * center, axis=-1, keepdims=True) + NORM_EPS)
    return center * inverse, inverse


def norm_forward(x_i, gain, offset, *refs):
    terms, (x_o, h_o) = refs[:-2], refs[-2:]
    x = x_i[...]
    for t in terms:
        x = x + t[...].astype(F32)
    x_o[...] = x
    h_o[...] = (norm_of(x)[0] * gain[...] + offset[...]).astype(LOW)


def norm_backward(dx_i, y_i, gain, *refs):
    terms, (dy_o, low_o, small_o) = refs[:-3], refs[-3:]
    dh = terms[0][...]
    for t in terms[1:]:
        dh = dh + t[...].astype(F32)
    n, inverse = norm_of(y_i[...])
    small_o[0:1] = jnp.sum(dh * n, axis=0, keepdims=True)
    small_o[1:2] = jnp.sum(dh, axis=0, keepdims=True)
    scaled = dh * gain[...]
    dy = dx_i[...] + inverse * (
        scaled
        - jnp.mean(scaled, axis=-1, keepdims=True)
        - n * jnp.mean(scaled * n, axis=-1, keepdims=True)
    )
    dy_o[...] = dy
    low_o[...] = dy.astype(LOW)


def log2(n):
    return n.bit_length() - 1


def make_program(n_dp, n_chi, n_clo, n_mp):
    group_bits = [("chi", 1 << k) for k in range(log2(n_chi))]
    group_bits += [("dp", 1 << k) for k in range(log2(n_dp))]
    n_groups = n_dp * n_chi
    n_pieces = 2 * n_groups
    sizes = {"dp": n_dp, "chi": n_chi, "clo": n_clo, "mp": n_mp}
    up_order = list(range(len(group_bits)))
    down_order = up_order[::-1]

    def swap(value, axis, bit):
        return lax.ppermute(value, axis, [(i, i ^ bit) for i in range(sizes[axis])])

    def relative(value):
        block = value.shape[-1] // n_groups
        me = lax.axis_index("dp") * n_chi + lax.axis_index("chi")
        parts = [
            lax.dynamic_slice_in_dim(value, (me ^ r) * block, block, value.ndim - 1)
            for r in range(n_groups)
        ]
        return jnp.concatenate(parts, axis=-1)

    def gather_weights(keep, send):
        a, b = {0: keep}, {0: swap(send, "clo", 1)}
        for ka, kb in zip(up_order, down_order):
            for have, k in ((a, ka), (b, kb)):
                fresh = {r | (1 << k): swap(have[r], *group_bits[k]) for r in list(have)}
                have.update(fresh)
        return [x for r in range(n_groups) for x in (a[r], b[r])]

    def spread(pieces):
        a, b = dict(enumerate(pieces[0::2])), dict(enumerate(pieces[1::2]))
        for ka, kb in zip(down_order, up_order):
            for have, k in ((a, ka), (b, kb)):
                for r in [r for r in have if r & (1 << k)]:
                    moved = swap(have.pop(r), *group_bits[k])
                    to = r ^ (1 << k)
                    have[to] = (have[to].astype(F32) + moved.astype(F32)).astype(LOW)
        return a[0], swap(b[0], "clo", 1)

    def token_gather(own):
        half = [own] + [swap(own, "mp", r) for r in range(1, n_mp)]
        return half + [swap(part, "clo", 1) for part in half]

    def token_reduce(own_half, send_half):
        rows, width = own_half.shape
        sub = rows // n_mp
        moved = swap(send_half, "clo", 1)
        outs = [shape((sub, width), F32)] + [shape((sub, width), LOW)] * (n_mp - 1)
        parts = call(middle, 0, [own_half, moved], outs, [], rows * width)
        return [parts[0]] + [swap(parts[r], "mp", r) for r in range(1, n_mp)]

    def own_tokens(value):
        seqs, block, width = value.shape
        sub = block * n_chi // n_mp
        per_block = block // sub
        place = lax.axis_index("mp") % per_block
        mine = lax.dynamic_slice_in_dim(value, place * sub, sub, 1)
        chi = lax.axis_index("chi")
        here = lax.dynamic_index_in_dim(mine, chi, 0, keepdims=False)
        there = swap(lax.dynamic_index_in_dim(mine, 1 - chi, 0, keepdims=False), "chi", 1)
        return jnp.where(lax.axis_index("mp") // per_block == chi, here, there)

    def tokens_out(own, block):
        sub, width = own.shape
        per_block = block // sub
        chi, mp = lax.axis_index("chi"), lax.axis_index("mp")
        parts = jnp.stack([own] + [swap(own, "mp", r) for r in range(1, n_mp)])
        parts = parts.reshape(n_chi, per_block, sub, width)
        parts = jnp.where(mp % per_block == 1, jnp.flip(parts, 1), parts)
        parts = parts.reshape(n_chi, block, width)
        here = (mp // per_block) == chi
        mine = jnp.where(here, parts[0], parts[1])
        moved = swap(jnp.where(here, parts[1], parts[0]), "chi", 1)
        return jnp.where(chi == 0, jnp.stack([mine, moved]), jnp.stack([moved, mine]))

    def on_device(
        tokens, segments, cotangent, first_gain, first_bias, qkv_weight, qkv_bias,
        out_weight, second_gain, second_bias, gate_up_weight, down_weight,
    ):
        n_seq, block, width = tokens.shape
        rows_dev = qkv_weight.shape[1]
        half_in = qkv_weight.shape[3] // 2
        half_ff = down_weight.shape[2] // 2
        heads = half_in // HEAD
        total = block * n_chi * n_clo
        half_total = total // n_clo
        sub = half_total // n_mp
        n_parts = n_clo * n_mp
        mp, clo, chi = (lax.axis_index(a) for a in ("mp", "clo", "chi"))
        x_own = relative(own_tokens(tokens)).astype(F32)

        pad = -(3 * half_ff) % 128
        attn_cols, mlp_cols = 4 * half_in, 3 * half_ff + pad

        def attn_columns(l):
            view = jnp.transpose(qkv_weight[l], (1, 0, 2))
            outs = [shape((rows_dev, attn_cols), LOW)] * 2
            return call(
                cut_columns, 2, [view, out_weight[l]], outs,
                [pltpu.SemaphoreType.DMA((8,))], 0, hbm_outs=2,
            )

        def mlp_columns(l):
            gu, down = jnp.transpose(gate_up_weight[l], (1, 0, 2)), down_weight[l]
            low = [gu[0, :, :half_ff], gu[1, :, :half_ff], down[:, :half_ff]]
            high = [gu[0, :, half_ff:], gu[1, :, half_ff:], down[:, half_ff:]]
            fill = [jnp.zeros((rows_dev, pad), LOW)] if pad else []
            low, high = jnp.concatenate(low + fill, axis=1), jnp.concatenate(high + fill, axis=1)
            return jnp.where(clo == 1, high, low), jnp.where(clo == 1, low, high)

        weights = [[None, None] for l in range(LAYERS)]
        ready = None
        for l in range(LAYERS):
            for i, columns_of in enumerate((attn_columns, mlp_columns)):
                keep, send = columns_of(l)
                if ready is not None:
                    keep, send, _ = lax.optimization_barrier((keep, send, ready))
                weights[l][i] = gather_weights(keep, send)
                ready = weights[l][i][2]
        dx = relative(own_tokens(cotangent))
        gains = relative(jnp.stack([first_gain, first_bias, second_gain, second_bias]))
        half_bias = jnp.where(clo == 1, qkv_bias[:, :, half_in:], qkv_bias[:, :, :half_in])
        half_bias = half_bias.reshape(LAYERS, 1, 3 * half_in)

        there = swap(lax.dynamic_index_in_dim(segments, 1 - chi, 0, keepdims=False), "chi", 1)
        here = lax.dynamic_index_in_dim(segments, chi, 0, keepdims=False)
        pair = jnp.stack([jnp.where(chi == 0, here, there), jnp.where(chi == 0, there, here)])
        other = swap(pair, "clo", 1)
        whole = jnp.stack(
            [jnp.where(clo == 0, pair, other), jnp.where(clo == 0, other, pair)], axis=1
        ).reshape(total)
        core_of = jnp.arange(n_clo, dtype=jnp.int32) ^ clo
        mp_of = jnp.arange(n_mp, dtype=jnp.int32) ^ mp
        per_block = block // sub
        place = (
            (mp_of // per_block * (n_clo * block) + mp_of % per_block * sub)[None, :, None]
            + (core_of * block)[:, None, None]
            + jnp.arange(sub, dtype=jnp.int32)[None, None, :]
        ).reshape(total)
        match = place[:, None] == jnp.arange(total, dtype=jnp.int32)[None, :]
        seg = jnp.sum(jnp.where(match, whole[None, :], 0), axis=1)
        starts = jnp.sum((seg[None, :] < seg[:, None]).astype(jnp.int32), axis=1)
        freq = jnp.exp(
            jnp.arange(ROT // 2, dtype=F32) * (-2.0 * math.log(10000.0) / ROT)
        )
        angles = freq[:, None] * (place - starts).astype(F32)[None, :]
        cos_t, sin_t = jnp.cos(angles).T, jnp.sin(angles).T
        zeros = jnp.zeros((total, ROT // 2), F32)
        tail = jnp.zeros((total, HEAD - ROT), F32)
        per_slab = 128 // HEAD
        tables = jnp.stack(
            [
                jnp.tile(jnp.concatenate(parts, axis=1), (1, per_slab))
                for parts in (
                    (cos_t, cos_t, tail + 1.0),
                    (-sin_t, zeros, tail),
                    (zeros, sin_t, tail),
                )
            ]
        )
        row = jnp.stack([seg, place])
        geometry = [tables, row.T, row]
        geometry_scratch = [
            pltpu.VMEM((3, total, 128), F32),
            pltpu.VMEM((total, 2), jnp.int32),
        ]

        act = shape((total, half_in), LOW)
        reduced = [shape((half_total, width), F32), shape((half_total, width), LOW)]
        n_w = n_pieces
        sems = pltpu.SemaphoreType.DMA((n_parts + n_w + 5,))
        h_scratch = pltpu.VMEM((total, width), LOW)

        def mm(*dims):
            return 2 * math.prod(dims)

        def norm(x, gain, offset, terms):
            outs = [shape(x.shape, F32), shape(x.shape, LOW)]
            return call(norm_forward, 0, [x, gain[None], offset[None]] + terms, outs, [], 10 * x.size)

        def norm_back(dx, y, gain, terms):
            outs = [shape(y.shape, F32), shape(y.shape, LOW), shape((2, width), F32)]
            return call(norm_backward, 0, [dx, y, gain[None]] + terms, outs, [], 20 * y.size)

        def grads(a_parts, b_parts, da, db, cols):
            outs = [shape((width // n_w, cols), LOW)] * n_w
            return call(
                functools.partial(weight_grads, n_parts, n_w),
                2 * n_parts + 2,
                a_parts + b_parts + [da, db],
                outs,
                [
                    h_scratch,
                    h_scratch,
                    pltpu.VMEM(da.shape, LOW),
                    pltpu.VMEM(db.shape, LOW),
                    pltpu.SemaphoreType.DMA((2 * n_parts + 2,)),
                ],
                mm(total, width, cols),
            )

        saved = []
        terms = []
        for l in range(LAYERS):
            w_attn, w_mlp = weights[l]
            x_own, h = norm(x_own, gains[0, l], gains[1, l], terms)
            h1 = token_gather(h)
            q, k, v, o, own, send = call(
                functools.partial(attn_forward, n_parts, n_w, heads),
                n_parts + n_w + 2,
                h1 + w_attn + geometry + [half_bias[l]],
                [act] * 4 + reduced,
                [
                    h_scratch,
                    pltpu.VMEM((width, attn_cols), LOW),
                    pltpu.VMEM((total, 3 * half_in), F32),
                ]
                + geometry_scratch
                + [sems],
                mm(total, width, attn_cols) + 2 * mm(heads, total, total, 2 * half_in),
            )
            y_own, h = norm(x_own, gains[2, l], gains[3, l], token_reduce(own, send))
            h2 = token_gather(h)
            gu, z, own, send = call(
                functools.partial(mlp_forward, n_parts, n_w),
                n_parts + n_w,
                h2 + w_mlp,
                [shape((total, 2 * half_ff), F32), shape((total, half_ff), LOW)] + reduced,
                [h_scratch, pltpu.VMEM((width, mlp_cols), LOW), sems],
                mm(total, width, mlp_cols),
            )
            saved.append((x_own, h1, q, k, v, o, y_own, h2, gu, z))
            x_own, terms = y_own, token_reduce(own, send)
        for t in terms:
            x_own = x_own + t.astype(F32)
        activations = tokens_out(relative(x_own.astype(LOW)), block)

        low = dx
        dx = dx.astype(F32)
        weight_out = [None] * LAYERS
        small_out = [None] * LAYERS
        for l in reversed(range(LAYERS)):
            w_attn, w_mlp = weights[l]
            x_own, h1, q, k, v, o, y_own, h2, gu, z = saved[l]
            dm = token_gather(low)
            dp2, own, send = call(
                functools.partial(mlp_backward, n_parts, n_w),
                n_parts + n_w + 1,
                dm + w_mlp + [gu],
                [shape((total, 2 * half_ff), LOW)] + reduced,
                [
                    h_scratch,
                    pltpu.VMEM((width, mlp_cols), LOW),
                    pltpu.VMEM((total, half_ff), F32),
                    pltpu.VMEM(gu.shape, F32),
                    sems,
                ],
                mm(total, width, mlp_cols),
            )
            terms = token_reduce(own, send)
            g_mlp = spread(grads(h2, dm, dp2, z, mlp_cols))
            dy, low, small_two = norm_back(dx, y_own, gains[2, l], terms)
            da = token_gather(low)
            dp1, bias_grad, own, send = call(
                functools.partial(attn_backward, n_parts, n_w, heads),
                n_parts + n_w + 5,
                da + w_attn + [q, k, v] + geometry,
                [shape((total, 3 * half_in), LOW), shape((1, 3 * half_in), F32)] + reduced,
                [
                    h_scratch,
                    pltpu.VMEM((width, attn_cols), LOW),
                    pltpu.VMEM((total, half_in), F32),
                    pltpu.VMEM((3, total, half_in), LOW),
                ]
                + geometry_scratch
                + [sems],
                mm(total, width, attn_cols) + 5 * mm(heads, total, total, half_in),
            )
            terms = token_reduce(own, send)
            g_attn = spread(grads(h1, da, dp1, o, attn_cols))
            dx, low, small_one = norm_back(dy, x_own, gains[0, l], terms)
            weight_out[l] = (g_attn, g_mlp)
            small_out[l] = (small_one, small_two, bias_grad)
        tokens_grad = tokens_out(relative(low), block).astype(F32)

        norms = relative(
            jnp.stack([jnp.concatenate(small_out[l][:2], axis=0) for l in range(LAYERS)], axis=1)
        )
        bias = jnp.stack([small_out[l][2] for l in range(LAYERS)]).reshape(LAYERS, 3, half_in)
        for k in range(log2(n_mp)):
            norms = norms + swap(norms, "mp", 1 << k)
        norms = norms + swap(norms, "clo", 1)
        for name, bit in group_bits:
            norms = norms + swap(norms, name, bit)
            bias = bias + swap(bias, name, bit)
        bias_other = swap(bias, "clo", 1)
        bias = jnp.concatenate(
            [jnp.where(clo == 0, bias, bias_other), jnp.where(clo == 0, bias_other, bias)], axis=2
        )

        def columns(which, first, count, parts):
            layers = []
            for l in range(LAYERS):
                mine, others = (
                    piece[:, first : first + count].reshape((rows_dev,) + parts + (-1,))
                    for piece in weight_out[l][which]
                )
                low = jnp.where(clo == 0, mine, others)
                high = jnp.where(clo == 0, others, mine)
                layers.append(jnp.concatenate([low, high], axis=-1).astype(F32))
            return jnp.stack(layers)

        return (
            activations, tokens_grad, norms[0], norms[1],
            columns(0, 0, 3 * half_in, (3,)), bias,
            columns(0, 3 * half_in, half_in, ()), norms[2], norms[3],
            columns(1, 0, 2 * half_ff, (2,)), columns(1, 2 * half_ff, half_ff, ()),
        )

    return on_device


def solution(mesh):
    n_dp, n_ctx, n_mp = (mesh.shape[a] for a in ("dp", "ctx", "mp"))
    n_clo = 2
    n_chi = n_ctx // n_clo
    fine = Mesh(mesh.devices.reshape(n_dp, n_chi, n_clo, n_mp), ("dp", "chi", "clo", "mp"))
    rows = ("dp", "chi", "clo")
    ctx = ("chi", "clo")
    token_spec = P("dp", ctx, None)
    four, three = P(None, rows, None, "mp"), P(None, rows, "mp")
    bias_spec = P(None, None, "mp")
    return jax.shard_map(
        make_program(n_dp, n_chi, n_clo, n_mp),
        mesh=fine,
        in_specs=(
            token_spec, P("dp", ctx), token_spec, P(), P(), four, bias_spec, three, P(), P(),
            four, three,
        ),
        out_specs=(
            token_spec, token_spec, P(), P(), four, bias_spec, three, P(), P(), four, three,
        ),
        check_vma=False,
    )
```

```python
import functools
import math

import jax
import jax.numpy as jnp
from jax import lax
from jax.experimental import pallas as pl
from jax.experimental.layout import Layout, with_layout_constraint
from jax.experimental.pallas import tpu as pltpu
from jax.sharding import Mesh
from jax.sharding import PartitionSpec as P

HEAD = 64
ROT = 16
LAYERS = 2
NORM_EPS = 1e-05
MASK_FILL = -1e30
LOW = jnp.bfloat16
F32 = jnp.float32
MIB = 1024 * 1024
BLOCK = 512
HBM = pl.BlockSpec(memory_space=pltpu.HBM)
ANY = pl.BlockSpec(memory_space=pl.ANY)
VMEM = pl.BlockSpec(memory_space=pltpu.VMEM)


def dot(a, b, dims):
    return lax.dot_general(a, b, (dims, ((), ())), preferred_element_type=F32)


def nn(a, b):
    return dot(a, b, ((1,), (0,)))


def nt(a, b):
    return dot(a, b, ((1,), (1,)))


def tn(a, b):
    return dot(a, b, ((0,), (0,)))


def shape(dims, kind):
    return jax.ShapeDtypeStruct(dims, kind)


def call(body, n_hbm, args, outs, scratch, flops, hbm_outs=0, n_any=0, limit=32):
    moved = sum(a.size * a.dtype.itemsize for a in args)
    moved += sum(math.prod(o.shape) * jnp.dtype(o.dtype).itemsize for o in outs)
    return pl.pallas_call(
        body,
        out_shape=tuple(outs),
        in_specs=[ANY] * n_any + [HBM] * (n_hbm - n_any) + [VMEM] * (len(args) - n_hbm),
        out_specs=tuple([HBM] * hbm_outs + [VMEM] * (len(outs) - hbm_outs)),
        scratch_shapes=scratch,
        compiler_params=pltpu.CompilerParams(vmem_limit_bytes=limit * MIB),
        cost_estimate=pl.CostEstimate(flops=flops, bytes_accessed=moved, transcendentals=0),
    )(*args)


def into_rows(pieces, whole, sems, first):
    copies, row = [], 0
    for i, piece in enumerate(pieces):
        rows = piece.shape[0]
        copies.append(
            pltpu.make_async_copy(piece, whole.at[pl.ds(row, rows)], sems.at[first + i])
        )
        row += rows
    return copies


def weights_into(weights, whole, sems, first):
    rows, width = whole.shape
    cols = pl.ds(pl.multiple_of(lax.axis_index("clo") * width, 128), width)
    copies = []
    for at in range(0, rows, BLOCK):
        src, dst = weights.at[pl.ds(at, BLOCK), cols], whole.at[pl.ds(at, BLOCK)]
        copies.append(pltpu.make_async_copy(src, dst, sems.at[first + len(copies)]))
    return copies


def start_all(copies):
    for c in copies:
        c.start()


def wait_all(copies):
    for c in copies:
        c.wait()


def rolled(value, tables, sign):
    cos_t, ahead_t, behind_t = tables[0], tables[1], tables[2]
    slabs = []
    for at in range(0, value.shape[1], 128):
        x = value[:, at : at + 128]
        ahead = pltpu.roll(x, 128 - ROT // 2, 1)
        behind = pltpu.roll(x, ROT // 2, 1)
        slabs.append(x * cos_t + sign * (ahead * ahead_t + behind * behind_t))
    return jnp.concatenate(slabs, axis=1).astype(LOW)


def allowed_of(column, row):
    return (column[:, 0:1] == row[0:1]) & (row[1:2] <= column[:, 1:2])


def put_halves(tile, cols, own_ref, send_ref):
    half = own_ref.shape[0]
    own_ref[:, cols] = tile[:half]
    send_ref[:, cols] = tile[half:].astype(LOW)


def softmax_of(q_h, k, allowed, scale):
    s = jnp.where(allowed, nt(q_h, k) * scale, MASK_FILL)
    top = jnp.max(s, axis=-1, keepdims=True)
    e = jnp.exp(s - top)
    return e / jnp.sum(e, axis=-1, keepdims=True)


def load(pairs, sems, first):
    return [
        pltpu.make_async_copy(src, dst, sems.at[first + i]) for i, (src, dst) in enumerate(pairs)
    ]


def block_rows(w_s, w_copies=None):
    for i, at in enumerate(range(0, w_s.shape[0], BLOCK)):
        if w_copies is not None:
            w_copies[i].wait()
        yield i, slice(at, at + BLOCK)


def attn_forward(n_h, heads, *refs):
    h_parts, weights, refs = refs[:n_h], refs[n_h], refs[n_h + 1 :]
    tables, column, row, bias = refs[:4]
    full_o, q_o, k_o, v_o, o_o, own_o, send_o, h_s, w_s, acc, tab, col, sems = refs[4:]
    width = heads * HEAD
    copies = into_rows(h_parts, h_s, sems, 0)
    w_copies = weights_into(weights, w_s, sems, n_h)
    extra = load([(tables, tab), (column, col)], sems, n_h + len(w_copies))
    start_all(copies + w_copies + extra)
    wait_all(copies)
    whole = pltpu.make_async_copy(h_s, full_o, sems.at[0])
    whole.start()
    for r, rows in block_rows(w_s, w_copies):
        for c in range(3):
            cols = slice(c * width, (c + 1) * width)
            part = nn(h_s[:, rows], w_s[rows, cols])
            acc[:, cols] = part + (bias[:, cols] if r == 0 else acc[:, cols])
    wait_all(extra)
    q_o[...] = rolled(acc[:, :width], tab, 1.0)
    k_o[...] = rolled(acc[:, width : 2 * width], tab, 1.0)
    v_o[...] = acc[:, 2 * width :].astype(LOW)
    lane = lax.broadcasted_iota(jnp.int32, (1, width), 1) // HEAD
    allowed = allowed_of(col, row)
    k, v, q = k_o[...], v_o[...], q_o[...]
    zero = jnp.zeros((), LOW)
    o = None
    for h in range(heads):
        mine = lane == h
        w = softmax_of(jnp.where(mine, q, zero), k, allowed, 1.0 / math.sqrt(HEAD))
        part = nn(w.astype(LOW), jnp.where(mine, v, zero))
        o = part if o is None else o + part
    o_o[...] = o.astype(LOW)
    o = o_o[...]
    for r, rows in block_rows(w_s):
        put_halves(nt(o, w_s[rows, 3 * width :]), rows, own_o, send_o)
    whole.wait()


def attn_backward(n_h, heads, *refs):
    d_parts, weights, refs = refs[:n_h], refs[n_h], refs[n_h + 1 :]
    q_i, k_i, v_i, tables, column, row = refs[:6]
    full_o, dp_o, bias_o, own_o, send_o, d_s, w_s, acc, qkv, tab, col, sems = refs[6:]
    width = heads * HEAD
    copies = into_rows(d_parts, d_s, sems, 0)
    w_copies = weights_into(weights, w_s, sems, n_h)
    extra = load(
        [(q_i, qkv.at[0]), (k_i, qkv.at[1]), (v_i, qkv.at[2]), (tables, tab), (column, col)],
        sems,
        n_h + len(w_copies),
    )
    start_all(copies + w_copies + extra)
    wait_all(copies)
    whole = pltpu.make_async_copy(d_s, full_o, sems.at[0])
    whole.start()
    for r, rows in block_rows(w_s, w_copies):
        part = nn(d_s[:, rows], w_s[rows, 3 * width :])
        acc[...] = part if r == 0 else acc[...] + part
    do = acc[...].astype(LOW)
    wait_all(extra)
    q, k, v = qkv[0], qkv[1], qkv[2]
    lane = lax.broadcasted_iota(jnp.int32, (1, width), 1) // HEAD
    allowed = allowed_of(col, row)
    zero = jnp.zeros((), LOW)
    scale = 1.0 / math.sqrt(HEAD)
    dq = dk = dv = None
    for h in range(heads):
        mine = lane == h
        q_h = jnp.where(mine, q, zero)
        do_h = jnp.where(mine, do, zero)
        w = softmax_of(q_h, k, allowed, scale)
        dw = nt(do_h, v)
        ds = (w * (dw - jnp.sum(w * dw, axis=-1, keepdims=True))).astype(LOW)
        dv_h = tn(w.astype(LOW), do_h)
        dq_h = nn(ds, jnp.where(mine, k, zero))
        dk_h = tn(ds, q_h)
        dq, dk, dv = (
            (dq_h, dk_h, dv_h) if h == 0 else (dq + dq_h, dk + dk_h, dv + dv_h)
        )
    dp_o[:, :width] = rolled(dq * scale, tab, -1.0)
    dp_o[:, width : 2 * width] = rolled(dk * scale, tab, -1.0)
    dp_o[:, 2 * width :] = dv.astype(LOW)
    dp = dp_o[...]
    bias_o[...] = jnp.sum(dp.astype(F32), axis=0, keepdims=True)
    for r, rows in block_rows(w_s):
        put_halves(nt(dp, w_s[rows, : 3 * width]), rows, own_o, send_o)
    whole.wait()


def mlp_forward(n_h, *refs):
    h_parts, weights, refs = refs[:n_h], refs[n_h], refs[n_h + 1 :]
    full_o, gu_o, z_o, own_o, send_o, h_s, w_s, sems = refs
    units = z_o.shape[1]
    copies = into_rows(h_parts, h_s, sems, 0)
    w_copies = weights_into(weights, w_s, sems, n_h)
    start_all(copies + w_copies)
    wait_all(copies)
    whole = pltpu.make_async_copy(h_s, full_o, sems.at[0])
    whole.start()
    for r, rows in block_rows(w_s, w_copies):
        part = nn(h_s[:, rows], w_s[rows, : 2 * units])
        gu_o[...] = part if r == 0 else gu_o[...] + part
    g = gu_o[:, :units]
    u = gu_o[:, units:]
    z_o[...] = (g * u / (1.0 + jnp.exp(-g))).astype(LOW)
    z = z_o[...]
    for r, rows in block_rows(w_s):
        put_halves(nt(z, w_s[rows, 2 * units : 3 * units]), rows, own_o, send_o)
    whole.wait()


def mlp_backward(n_h, *refs):
    d_parts, weights, refs = refs[:n_h], refs[n_h], refs[n_h + 1 :]
    gu_i, full_o, dp_o, own_o, send_o, d_s, w_s, acc, gu, sems = refs
    units = acc.shape[1]
    copies = into_rows(d_parts, d_s, sems, 0)
    w_copies = weights_into(weights, w_s, sems, n_h)
    extra = load([(gu_i, gu)], sems, n_h + len(w_copies))
    start_all(copies + w_copies + extra)
    wait_all(copies)
    whole = pltpu.make_async_copy(d_s, full_o, sems.at[0])
    whole.start()
    for r, rows in block_rows(w_s, w_copies):
        part = nn(d_s[:, rows], w_s[rows, 2 * units : 3 * units])
        acc[...] = part if r == 0 else acc[...] + part
    wait_all(extra)
    g = gu[:, :units]
    u = gu[:, units:]
    sig = 1.0 / (1.0 + jnp.exp(-g))
    dz = acc[...]
    dp_o[:, :units] = (dz * u * sig * (1.0 + g * (1.0 - sig))).astype(LOW)
    dp_o[:, units:] = (dz * g * sig).astype(LOW)
    dp = dp_o[...]
    for r, rows in block_rows(w_s):
        put_halves(nt(dp, w_s[rows, : 2 * units]), rows, own_o, send_o)
    whole.wait()


def load_grads(args, a_s, b_s, da_s, db_s, sems):
    copies = load(list(zip(args, (a_s, b_s, da_s, db_s))), sems, 0)
    start_all(copies)
    wait_all(copies)


def weight_grads(*refs):
    out, a_s, b_s, da_s, db_s, slots, sems, out_sems = refs[4:]
    load_grads(refs[:4], a_s, b_s, da_s, db_s, sems)
    split, end = da_s.shape[1], da_s.shape[1] + db_s.shape[1]
    sent = []
    for i, at in enumerate(range(0, a_s.shape[1], BLOCK)):
        cols = slice(at, at + BLOCK)
        slot = slots.at[i % 2]
        if i >= 2:
            sent[i - 2].wait()
        slot[:, :split] = tn(a_s[:, cols], da_s[...]).astype(LOW)
        slot[:, split:end] = tn(b_s[:, cols], db_s[...]).astype(LOW)
        if end < slot.shape[1]:
            slot[:, end:] = jnp.zeros((BLOCK, slot.shape[1] - end), LOW)
        sent.append(pltpu.make_async_copy(slot, out.at[pl.ds(at, BLOCK)], out_sems.at[i]))
        sent[i].start()
    wait_all(sent[-2:])


def weight_pieces(n_groups, n_chi, *refs):
    outs, (a_s, b_s, da_s, db_s, sems) = refs[4:-5], refs[-5:]
    load_grads(refs[:4], a_s, b_s, da_s, db_s, sems)
    block = a_s.shape[1] // n_groups
    half = block // 2
    split, end = da_s.shape[1], da_s.shape[1] + db_s.shape[1]
    swapped = lax.axis_index("clo") == 1
    group = lax.axis_index("dp") * n_chi + lax.axis_index("chi")
    for r in range(n_groups):
        cols = pl.ds(pl.multiple_of((group ^ r) * block, 128), block)
        first = tn(a_s[:, cols], da_s[...]).astype(LOW)
        second = tn(b_s[:, cols], db_s[...]).astype(LOW)
        for i in range(2):
            here, there = slice(i * half, (i + 1) * half), slice((1 - i) * half, (2 - i) * half)
            out = outs[2 * r + i]
            out[:, :split] = jnp.where(swapped, first[there], first[here])
            out[:, split:end] = jnp.where(swapped, second[there], second[here])
            if end < out.shape[1]:
                out[:, end:] = jnp.zeros((half, out.shape[1] - end), LOW)


def order_columns(*refs):
    qkv, out, both, sems = refs
    width = both.shape[1] // 8
    copies = []
    for core in range(2):
        cols = pl.ds(core * width, width)
        for c in range(4):
            src = out.at[:, cols] if c == 3 else qkv.at[c, :, cols]
            dst = both.at[:, pl.ds((4 * core + c) * width, width)]
            copies.append(pltpu.make_async_copy(src, dst, sems.at[len(copies)]))
    start_all(copies)
    wait_all(copies)


def middle(own_i, moved_i, own_o, *sends):
    rows = own_o.shape[0]
    own_o[...] = own_i[:rows] + moved_i[:rows].astype(F32)
    for r, send in enumerate(sends):
        at = slice((r + 1) * rows, (r + 2) * rows)
        send[...] = (own_i[at] + moved_i[at].astype(F32)).astype(LOW)


def norm_of(value):
    center = value - jnp.mean(value, axis=-1, keepdims=True)
    inverse = lax.rsqrt(jnp.mean(center * center, axis=-1, keepdims=True) + NORM_EPS)
    return center * inverse, inverse


def norm_forward(x_i, gain, offset, *refs):
    terms, (x_o, h_o) = refs[:-2], refs[-2:]
    x = x_i[...]
    for t in terms:
        x = x + t[...].astype(F32)
    x_o[...] = x
    h_o[...] = (norm_of(x)[0] * gain[...] + offset[...]).astype(LOW)


def norm_backward(dx_i, y_i, gain, *refs):
    terms, (dy_o, low_o, small_o) = refs[:-3], refs[-3:]
    dh = terms[0][...]
    for t in terms[1:]:
        dh = dh + t[...].astype(F32)
    n, inverse = norm_of(y_i[...])
    small_o[0:1] = jnp.sum(dh * n, axis=0, keepdims=True)
    small_o[1:2] = jnp.sum(dh, axis=0, keepdims=True)
    scaled = dh * gain[...]
    dy = dx_i[...] + inverse * (
        scaled
        - jnp.mean(scaled, axis=-1, keepdims=True)
        - n * jnp.mean(scaled * n, axis=-1, keepdims=True)
    )
    dy_o[...] = dy
    low_o[...] = dy.astype(LOW)


def after(value, event):
    return lax.optimization_barrier((value, event))[0]


def log2(n):
    return n.bit_length() - 1


def reverse_bits(r, bits):
    return sum(((r >> k) & 1) << (bits - 1 - k) for k in range(bits))


def make_program(n_dp, n_chi, n_clo, n_mp):
    group_bits = [("chi", 1 << k) for k in range(log2(n_chi))]
    group_bits += [("dp", 1 << k) for k in range(log2(n_dp))]
    n_groups = n_dp * n_chi
    sizes = {"dp": n_dp, "chi": n_chi, "clo": n_clo, "mp": n_mp}
    up_order = list(range(len(group_bits)))
    down_order = up_order[::-1]

    def swap(value, axis, bit):
        return lax.ppermute(value, axis, [(i, i ^ bit) for i in range(sizes[axis])])

    def spread(pieces):
        a, b = dict(enumerate(pieces[0::2])), dict(enumerate(pieces[1::2]))
        for ka, kb in zip(down_order, up_order):
            for have, k in ((a, ka), (b, kb)):
                for r in [r for r in have if r & (1 << k)]:
                    moved = swap(have.pop(r), *group_bits[k])
                    to = r ^ (1 << k)
                    have[to] = (have[to].astype(F32) + moved.astype(F32)).astype(LOW)
        return a[0], swap(b[0], "clo", 1)

    def mp_gather(own):
        parts = [own]
        for k in reversed(range(log2(n_mp))):
            parts = parts + [swap(part, "mp", 1 << k) for part in parts]
        return [parts[reverse_bits(r, log2(n_mp))] for r in range(n_mp)]

    def token_gather(own):
        half = mp_gather(own)
        return half + [swap(part, "clo", 1) for part in half]

    def token_reduce(own_half, send_half, beside=None, before=None):
        rows, width = own_half.shape
        sub = rows // n_mp
        moved = swap(send_half, "clo", 1)
        if before is not None:
            (own_half, moved), before = lax.optimization_barrier(((own_half, moved), before))
        outs = [shape((sub, width), F32)] + [shape((sub, width), LOW)] * (n_mp - 1)
        parts = call(middle, 0, [own_half, moved], outs, [], rows * width)
        terms = [parts[0]] + [swap(parts[r], "mp", r) for r in range(1, n_mp)]
        result = None
        if beside is not None:
            work, args = beside
            terms, result = lax.optimization_barrier((terms, work(*after(args, parts[0]))))
        return terms, result, before

    def own_tokens(value):
        seqs, block, width = value.shape
        sub = block * n_chi // n_mp
        per_block = block // sub
        place = lax.axis_index("mp") % per_block
        mine = lax.dynamic_slice_in_dim(value, place * sub, sub, 1)
        chi = lax.axis_index("chi")
        here = lax.dynamic_index_in_dim(mine, chi, 0, keepdims=False)
        there = swap(lax.dynamic_index_in_dim(mine, 1 - chi, 0, keepdims=False), "chi", 1)
        return jnp.where(lax.axis_index("mp") // per_block == chi, here, there)

    def to_blocks(held, block):
        chi = lax.axis_index("chi")
        mine = lax.dynamic_slice_in_dim(held, chi * block, block, 0)
        moved = swap(lax.dynamic_slice_in_dim(held, (1 - chi) * block, block, 0), "chi", 1)
        return jnp.where(chi == 0, jnp.stack([mine, moved]), jnp.stack([moved, mine]))

    def by_place(parts):
        sub, width = parts[0].shape
        mp = lax.axis_index("mp")
        parts = jnp.stack(parts)
        for k in range(log2(n_mp)):
            pairs = parts.reshape(n_mp >> (k + 1), 2, 1 << k, sub, width)
            pairs = jnp.where((mp >> k) % 2 == 1, jnp.flip(pairs, 1), pairs)
            parts = pairs.reshape(n_mp, sub, width)
        return parts.reshape(n_mp * sub, width)

    def on_device(
        tokens, segments, cotangent, first_gain, first_bias, qkv_weight, qkv_bias,
        out_weight, second_gain, second_bias, gate_up_weight, down_weight,
    ):
        n_seq, block, width = tokens.shape
        rows_dev = qkv_weight.shape[1]
        half_in = qkv_weight.shape[3] // 2
        half_ff = down_weight.shape[2] // 2
        heads = half_in // HEAD
        total = block * n_chi * n_clo
        half_total = total // n_clo
        sub = half_total // n_mp
        n_parts = n_clo * n_mp
        mp, clo, chi = (lax.axis_index(a) for a in ("mp", "clo", "chi"))
        x_own = own_tokens(tokens).astype(F32)

        pad = -(3 * half_ff) % 128
        attn_cols, mlp_cols = 4 * half_in, 3 * half_ff + pad

        def attn_columns(l):
            view = jnp.transpose(qkv_weight[l], (1, 0, 2))
            outs = [shape((rows_dev, 2 * attn_cols), LOW)]
            args = [view, out_weight[l]]
            sems = [pltpu.SemaphoreType.DMA((8,))]
            return call(order_columns, 2, args, outs, sems, 0, hbm_outs=1)

        def mlp_columns(l):
            gu, down = jnp.transpose(gate_up_weight[l], (1, 0, 2)), down_weight[l]
            fill = jnp.zeros((rows_dev, pad), LOW)
            parts = []
            for cols in (slice(None, half_ff), slice(half_ff, None)):
                parts += [gu[0, :, cols], gu[1, :, cols], down[:, cols], fill]
            return jnp.concatenate(parts, axis=1)

        def gather_weights(own):
            return lax.all_gather(own, ("dp", "chi", "clo"), axis=0, tiled=True)

        weights = []
        for l in range(LAYERS):
            attn = [gather_weights(attn_columns(l)[0])]
            weights.append([attn, gather_weights(mlp_columns(l))])
        dx = own_tokens(cotangent)
        gains = jnp.stack([first_gain, first_bias, second_gain, second_bias])
        half_bias = jnp.where(clo == 1, qkv_bias[:, :, half_in:], qkv_bias[:, :, :half_in])
        half_bias = half_bias.reshape(LAYERS, 1, 3 * half_in)

        there = swap(lax.dynamic_index_in_dim(segments, 1 - chi, 0, keepdims=False), "chi", 1)
        here = lax.dynamic_index_in_dim(segments, chi, 0, keepdims=False)
        pair = jnp.stack([jnp.where(chi == 0, here, there), jnp.where(chi == 0, there, here)])
        other = swap(pair, "clo", 1)
        whole = jnp.stack(
            [jnp.where(clo == 0, pair, other), jnp.where(clo == 0, other, pair)], axis=1
        ).reshape(total)
        core_of = jnp.arange(n_clo, dtype=jnp.int32) ^ clo
        mp_of = jnp.arange(n_mp, dtype=jnp.int32) ^ mp
        per_block = block // sub
        place = (
            (mp_of // per_block * (n_clo * block) + mp_of % per_block * sub)[None, :, None]
            + (core_of * block)[:, None, None]
            + jnp.arange(sub, dtype=jnp.int32)[None, None, :]
        ).reshape(total)
        match = place[:, None] == jnp.arange(total, dtype=jnp.int32)[None, :]
        seg = jnp.sum(jnp.where(match, whole[None, :], 0), axis=1)
        starts = jnp.sum((seg[None, :] < seg[:, None]).astype(jnp.int32), axis=1)
        freq = jnp.exp(
            jnp.arange(ROT // 2, dtype=F32) * (-2.0 * math.log(10000.0) / ROT)
        )
        angles = freq[:, None] * (place - starts).astype(F32)[None, :]
        cos_t, sin_t = jnp.cos(angles).T, jnp.sin(angles).T
        zeros = jnp.zeros((total, ROT // 2), F32)
        tail = jnp.zeros((total, HEAD - ROT), F32)
        per_slab = 128 // HEAD
        tables = jnp.stack(
            [
                jnp.tile(jnp.concatenate(parts, axis=1), (1, per_slab))
                for parts in (
                    (cos_t, cos_t, tail + 1.0),
                    (-sin_t, zeros, tail),
                    (zeros, sin_t, tail),
                )
            ]
        )
        row = jnp.stack([seg, place])
        geometry = [tables, row.T, row]
        geometry_scratch = [
            pltpu.VMEM((3, total, 128), F32),
            pltpu.VMEM((total, 2), jnp.int32),
        ]

        act = shape((total, half_in), LOW)
        reduced = [shape((half_total, width), F32), shape((half_total, width), LOW)]
        sems = pltpu.SemaphoreType.DMA((n_parts + width // BLOCK + 5,))
        h_scratch = pltpu.VMEM((total, width), LOW)

        def mm(*dims):
            return 2 * math.prod(dims)

        def norm(x, gain, offset, terms):
            outs = [shape(x.shape, F32), shape(x.shape, LOW)]
            return call(norm_forward, 0, [x, gain[None], offset[None]] + terms, outs, [], 10 * x.size)

        def norm_back(dx, y, gain, terms):
            outs = [shape(y.shape, F32), shape(y.shape, LOW), shape((2, width), F32)]
            return call(norm_backward, 0, [dx, y, gain[None]] + terms, outs, [], 20 * y.size)

        def grads(a, b, da, db, cols, pieces):
            scratch = [pltpu.VMEM(x.shape, LOW) for x in (a, b, da, db)]
            sems = pltpu.SemaphoreType.DMA((4,))
            if pieces:
                body = functools.partial(weight_pieces, n_groups, n_chi)
                outs = [shape((rows_dev, cols), LOW)] * (2 * n_groups)
                scratch += [sems]
            else:
                body = weight_grads
                outs = [shape((width, cols), LOW)]
                scratch += [pltpu.VMEM((2, BLOCK, cols), LOW), sems]
                scratch += [pltpu.SemaphoreType.DMA((width // BLOCK,))]
            return call(
                body, 4, [a, b, da, db], outs, scratch, mm(total, width, cols),
                hbm_outs=0 if pieces else 1, limit=60,
            )

        def scatter(partial):
            return lax.psum_scatter(partial[0], ("dp", "chi"), scatter_dimension=0, tiled=True)

        def pick(block_sum):
            mine = lax.dynamic_slice_in_dim(block_sum, clo * rows_dev, rows_dev, 0)
            others = lax.dynamic_slice_in_dim(block_sum, (1 - clo) * rows_dev, rows_dev, 0)
            return mine, swap(others, "clo", 1)

        def columns(pieces, first, count, parts):
            mine, others = (
                piece[:, first : first + count].reshape((rows_dev,) + parts + (-1,))
                for piece in pieces
            )
            low = jnp.where(clo == 0, mine, others)
            high = jnp.where(clo == 0, others, mine)
            return jnp.concatenate([low, high], axis=-1).astype(F32)

        def above_zeros(x):
            layout = Layout(major_to_minor=tuple(range(x.ndim + 1)))
            return with_layout_constraint(jnp.stack([jnp.zeros_like(x), x]), layout)

        def attn_out(pieces):
            return (
                columns(pieces, 0, 3 * half_in, (3,)),
                columns(pieces, 3 * half_in, half_in, ()),
            )

        def mlp_out(pieces):
            return (
                columns(pieces, 0, 2 * half_ff, (2,)),
                columns(pieces, 2 * half_ff, half_ff, ()),
            )

        whole = shape((total, width), LOW)
        saved = []
        terms = []
        for l in range(LAYERS):
            w_attn, w_mlp = weights[l]
            x_own, h = norm(x_own, gains[0, l], gains[1, l], terms)
            h1 = token_gather(h)
            h1, q, k, v, o, own, send = call(
                functools.partial(attn_forward, n_parts, heads),
                n_parts + 3,
                h1 + w_attn + geometry + [half_bias[l]],
                [whole] + [act] * 4 + reduced,
                [
                    h_scratch,
                    pltpu.VMEM((width, attn_cols), LOW),
                    pltpu.VMEM((total, 3 * half_in), F32),
                ]
                + geometry_scratch
                + [sems],
                mm(total, width, attn_cols) + 2 * mm(heads, total, total, 2 * half_in),
                n_any=n_parts,
                hbm_outs=1,
                limit=56,
            )
            y_own, h = norm(x_own, gains[2, l], gains[3, l], token_reduce(own, send)[0])
            h2 = token_gather(h)
            h2, gu, z, own, send = call(
                functools.partial(mlp_forward, n_parts),
                n_parts + 1,
                h2 + [w_mlp],
                [whole, shape((total, 2 * half_ff), F32), shape((total, half_ff), LOW)] + reduced,
                [h_scratch, pltpu.VMEM((width, mlp_cols), LOW), sems],
                mm(total, width, mlp_cols),
                n_any=n_parts,
                hbm_outs=1,
            )
            saved.append((x_own, h1, q, k, v, o, y_own, h2, gu, z))
            x_own, terms = y_own, token_reduce(own, send)[0]

        low = dx
        dx = dx.astype(F32)
        small_out = [None] * LAYERS
        done = None
        for l in reversed(range(LAYERS)):
            w_attn, w_mlp = weights[l]
            x_own, h1, q, k, v, o, y_own, h2, gu, z = saved[l]
            parts = token_gather(low)
            dm, dp2, own, send = call(
                functools.partial(mlp_backward, n_parts),
                n_parts + 2,
                parts + [w_mlp, gu],
                [whole, shape((total, 2 * half_ff), LOW)] + reduced,
                [
                    h_scratch,
                    pltpu.VMEM((width, mlp_cols), LOW),
                    pltpu.VMEM((total, half_ff), F32),
                    pltpu.VMEM(gu.shape, F32),
                    sems,
                ],
                mm(total, width, mlp_cols),
                n_any=n_parts,
                hbm_outs=1,
            )
            work = functools.partial(grads, cols=mlp_cols, pieces=False)
            if done is None:
                terms, g_mlp, last = token_reduce(own, send, (work, (h2, dm, dp2, z)), terms)
                x_last = y_own
                for t in last:
                    x_last = x_last + t.astype(F32)
                x_last = mp_gather(x_last.astype(LOW))
            else:
                terms, g_mlp, _ = token_reduce(own, send, (work, (h2, dm, dp2, z)))
            g_mlp = scatter(g_mlp)
            dy, low, small_two = norm_back(dx, y_own, gains[2, l], terms)
            parts = token_gather(low)
            if done is not None:
                late, early = done
                early = [above_zeros(x) for x in mlp_out(pick(early))]
                parts, early = lax.optimization_barrier((parts, early))
            da, dp1, bias_grad, own, send = call(
                functools.partial(attn_backward, n_parts, heads),
                n_parts + 6,
                parts + w_attn + [q, k, v] + geometry,
                [whole, shape((total, 3 * half_in), LOW), shape((1, 3 * half_in), F32)] + reduced,
                [
                    h_scratch,
                    pltpu.VMEM((width, attn_cols), LOW),
                    pltpu.VMEM((total, half_in), F32),
                    pltpu.VMEM((3, total, half_in), LOW),
                ]
                + geometry_scratch
                + [sems],
                mm(total, width, attn_cols) + 5 * mm(heads, total, total, half_in),
                n_any=n_parts,
                hbm_outs=1,
                limit=56,
            )
            work = functools.partial(grads, cols=attn_cols, pieces=False)
            if done is None:
                terms, g_attn, x_last = token_reduce(own, send, (work, (h1, da, dp1, o)), x_last)
                activations = to_blocks(by_place(x_last), block)
                done = (scatter(g_attn), g_mlp)
            else:
                terms, g_attn, _ = token_reduce(own, send, (work, (h1, da, dp1, o)))
                late = [above_zeros(x) for x in attn_out(pick(late))]
                terms, late = lax.optimization_barrier((terms, late))
            dx, low, small_one = norm_back(dy, x_own, gains[0, l], terms)
            small_out[l] = (small_one, small_two, bias_grad)
        parts = mp_gather(low)
        tokens_grad = to_blocks(by_place(parts), block).astype(F32)
        g_mlp, small_out = after((g_mlp, small_out), parts[n_mp // 2])
        g_attn, mlp_last = pick(scatter(g_attn)), mlp_out(pick(g_mlp))
        parts = zip(late + early, attn_out(g_attn) + tuple(mlp_last))
        weight_out = [stack.at[0].set(part) for stack, part in parts]

        norms = jnp.stack(
            [jnp.concatenate(small_out[l][:2], axis=0) for l in range(LAYERS)], axis=1
        )
        bias = jnp.stack([small_out[l][2] for l in range(LAYERS)]).reshape(LAYERS, 3, half_in)
        for k in range(log2(n_mp)):
            norms = norms + swap(norms, "mp", 1 << k)
        norms = norms + swap(norms, "clo", 1)
        for name, bit in group_bits:
            norms = norms + swap(norms, name, bit)
            bias = bias + swap(bias, name, bit)
        bias_other = swap(bias, "clo", 1)
        bias = jnp.concatenate(
            [jnp.where(clo == 0, bias, bias_other), jnp.where(clo == 0, bias_other, bias)], axis=2
        )

        return (
            activations, tokens_grad, norms[0], norms[1],
            weight_out[0], bias, weight_out[1], norms[2], norms[3], weight_out[2], weight_out[3],
        )

    return on_device


def solution(mesh):
    n_dp, n_ctx, n_mp = (mesh.shape[a] for a in ("dp", "ctx", "mp"))
    n_clo = 2
    n_chi = n_ctx // n_clo
    fine = Mesh(mesh.devices.reshape(n_dp, n_chi, n_clo, n_mp), ("dp", "chi", "clo", "mp"))
    rows = ("dp", "chi", "clo")
    ctx = ("chi", "clo")
    token_spec = P("dp", ctx, None)
    four, three = P(None, rows, None, "mp"), P(None, rows, "mp")
    bias_spec = P(None, None, "mp")
    return jax.shard_map(
        make_program(n_dp, n_chi, n_clo, n_mp),
        mesh=fine,
        in_specs=(
            token_spec, P("dp", ctx), token_spec, P(), P(), four, bias_spec, three, P(), P(),
            four, three,
        ),
        out_specs=(
            token_spec, token_spec, P(), P(), four, bias_spec, three, P(), P(), four, three,
        ),
        check_vma=False,
    )
```

```python
import functools
import math

import jax
import jax.numpy as jnp
from jax import lax
from jax.experimental import pallas as pl
from jax.experimental.layout import Layout, with_layout_constraint
from jax.experimental.pallas import tpu as pltpu
from jax.sharding import Mesh
from jax.sharding import PartitionSpec as P

HEAD = 64
ROT = 16
LAYERS = 2
NORM_EPS = 1e-05
MASK_FILL = -1e30
LOW = jnp.bfloat16
F32 = jnp.float32
MIB = 1024 * 1024
BLOCK = 512
HBM = pl.BlockSpec(memory_space=pltpu.HBM)
ANY = pl.BlockSpec(memory_space=pl.ANY)
VMEM = pl.BlockSpec(memory_space=pltpu.VMEM)


def dot(a, b, dims):
    return lax.dot_general(a, b, (dims, ((), ())), preferred_element_type=F32)


def nn(a, b):
    return dot(a, b, ((1,), (0,)))


def nt(a, b):
    return dot(a, b, ((1,), (1,)))


def tn(a, b):
    return dot(a, b, ((0,), (0,)))


def shape(dims, kind):
    return jax.ShapeDtypeStruct(dims, kind)


def call(body, n_hbm, args, outs, scratch, flops, hbm_outs=0, n_any=0, limit=32, aliases=None):
    moved = sum(a.size * a.dtype.itemsize for a in args)
    moved += sum(math.prod(o.shape) * jnp.dtype(o.dtype).itemsize for o in outs)
    return pl.pallas_call(
        body,
        out_shape=tuple(outs),
        in_specs=[ANY] * n_any + [HBM] * (n_hbm - n_any) + [VMEM] * (len(args) - n_hbm),
        out_specs=tuple([HBM] * hbm_outs + [VMEM] * (len(outs) - hbm_outs)),
        scratch_shapes=scratch,
        input_output_aliases=aliases or {},
        compiler_params=pltpu.CompilerParams(vmem_limit_bytes=limit * MIB),
        cost_estimate=pl.CostEstimate(flops=flops, bytes_accessed=moved, transcendentals=0),
    )(*args)


def into_rows(pieces, whole, sems, first):
    copies, row = [], 0
    for i, piece in enumerate(pieces):
        rows = piece.shape[0]
        copies.append(
            pltpu.make_async_copy(piece, whole.at[pl.ds(row, rows)], sems.at[first + i])
        )
        row += rows
    return copies


def weights_into(weights, whole, sems, first):
    rows, width = whole.shape
    cols = pl.ds(pl.multiple_of(lax.axis_index("clo") * width, 128), width)
    copies = []
    for at in range(0, rows, BLOCK):
        src, dst = weights.at[pl.ds(at, BLOCK), cols], whole.at[pl.ds(at, BLOCK)]
        copies.append(pltpu.make_async_copy(src, dst, sems.at[first + len(copies)]))
    return copies


def start_all(copies):
    for c in copies:
        c.start()


def wait_all(copies):
    for c in copies:
        c.wait()


def rolled(value, tables, sign):
    cos_t, ahead_t, behind_t = tables[0], tables[1], tables[2]
    slabs = []
    for at in range(0, value.shape[1], 128):
        x = value[:, at : at + 128]
        ahead = pltpu.roll(x, 128 - ROT // 2, 1)
        behind = pltpu.roll(x, ROT // 2, 1)
        slabs.append(x * cos_t + sign * (ahead * ahead_t + behind * behind_t))
    return jnp.concatenate(slabs, axis=1).astype(LOW)


def allowed_of(column, row):
    return (column[:, 0:1] == row[0:1]) & (row[1:2] <= column[:, 1:2])


def put_halves(tile, cols, own_ref, send_ref):
    half = own_ref.shape[0]
    own_ref[:, cols] = tile[:half]
    send_ref[:, cols] = tile[half:].astype(LOW)


def softmax_of(q_h, k, allowed, scale):
    s = jnp.where(allowed, nt(q_h, k) * scale, MASK_FILL)
    top = jnp.max(s, axis=-1, keepdims=True)
    e = jnp.exp(s - top)
    return e / jnp.sum(e, axis=-1, keepdims=True)


def load(pairs, sems, first):
    return [
        pltpu.make_async_copy(src, dst, sems.at[first + i]) for i, (src, dst) in enumerate(pairs)
    ]


def block_rows(w_s, w_copies=None):
    for i, at in enumerate(range(0, w_s.shape[0], BLOCK)):
        if w_copies is not None:
            w_copies[i].wait()
        yield i, slice(at, at + BLOCK)


def attn_forward(n_h, heads, *refs):
    h_parts, weights, refs = refs[:n_h], refs[n_h], refs[n_h + 1 :]
    tables, column, row, bias = refs[:4]
    full_o, q_o, k_o, v_o, o_o, own_o, send_o, h_s, w_s, acc, tab, col, sems = refs[4:]
    width = heads * HEAD
    copies = into_rows(h_parts, h_s, sems, 0)
    w_copies = weights_into(weights, w_s, sems, n_h)
    extra = load([(tables, tab), (column, col)], sems, n_h + len(w_copies))
    start_all(copies + w_copies + extra)
    wait_all(copies)
    whole = pltpu.make_async_copy(h_s, full_o, sems.at[0])
    whole.start()
    for r, rows in block_rows(w_s, w_copies):
        for c in range(3):
            cols = slice(c * width, (c + 1) * width)
            part = nn(h_s[:, rows], w_s[rows, cols])
            acc[:, cols] = part + (bias[:, cols] if r == 0 else acc[:, cols])
    wait_all(extra)
    q_o[...] = rolled(acc[:, :width], tab, 1.0)
    k_o[...] = rolled(acc[:, width : 2 * width], tab, 1.0)
    v_o[...] = acc[:, 2 * width :].astype(LOW)
    lane = lax.broadcasted_iota(jnp.int32, (1, width), 1) // HEAD
    allowed = allowed_of(col, row)
    k, v, q = k_o[...], v_o[...], q_o[...]
    zero = jnp.zeros((), LOW)
    o = None
    for h in range(heads):
        mine = lane == h
        w = softmax_of(jnp.where(mine, q, zero), k, allowed, 1.0 / math.sqrt(HEAD))
        part = nn(w.astype(LOW), jnp.where(mine, v, zero))
        o = part if o is None else o + part
    o_o[...] = o.astype(LOW)
    o = o_o[...]
    for r, rows in block_rows(w_s):
        put_halves(nt(o, w_s[rows, 3 * width :]), rows, own_o, send_o)
    whole.wait()


def attn_backward(n_h, heads, *refs):
    d_parts, weights, refs = refs[:n_h], refs[n_h], refs[n_h + 1 :]
    q_i, k_i, v_i, tables, column, row = refs[:6]
    full_o, dp_o, bias_o, own_o, send_o, d_s, w_s, acc, qkv, tab, col, sems = refs[6:]
    width = heads * HEAD
    copies = into_rows(d_parts, d_s, sems, 0)
    w_copies = weights_into(weights, w_s, sems, n_h)
    extra = load(
        [(q_i, qkv.at[0]), (k_i, qkv.at[1]), (v_i, qkv.at[2]), (tables, tab), (column, col)],
        sems,
        n_h + len(w_copies),
    )
    start_all(copies + w_copies + extra)
    wait_all(copies)
    whole = pltpu.make_async_copy(d_s, full_o, sems.at[0])
    whole.start()
    for r, rows in block_rows(w_s, w_copies):
        part = nn(d_s[:, rows], w_s[rows, 3 * width :])
        acc[...] = part if r == 0 else acc[...] + part
    do = acc[...].astype(LOW)
    wait_all(extra)
    q, k, v = qkv[0], qkv[1], qkv[2]
    lane = lax.broadcasted_iota(jnp.int32, (1, width), 1) // HEAD
    allowed = allowed_of(col, row)
    zero = jnp.zeros((), LOW)
    scale = 1.0 / math.sqrt(HEAD)
    dq = dk = dv = None
    for h in range(heads):
        mine = lane == h
        q_h = jnp.where(mine, q, zero)
        do_h = jnp.where(mine, do, zero)
        w = softmax_of(q_h, k, allowed, scale)
        dw = nt(do_h, v)
        ds = (w * (dw - jnp.sum(w * dw, axis=-1, keepdims=True))).astype(LOW)
        dv_h = tn(w.astype(LOW), do_h)
        dq_h = nn(ds, jnp.where(mine, k, zero))
        dk_h = tn(ds, q_h)
        dq, dk, dv = (
            (dq_h, dk_h, dv_h) if h == 0 else (dq + dq_h, dk + dk_h, dv + dv_h)
        )
    dp_o[:, :width] = rolled(dq * scale, tab, -1.0)
    dp_o[:, width : 2 * width] = rolled(dk * scale, tab, -1.0)
    dp_o[:, 2 * width :] = dv.astype(LOW)
    dp = dp_o[...]
    bias_o[...] = jnp.sum(dp.astype(F32), axis=0, keepdims=True)
    for r, rows in block_rows(w_s):
        put_halves(nt(dp, w_s[rows, : 3 * width]), rows, own_o, send_o)
    whole.wait()


def mlp_forward(n_h, *refs):
    h_parts, weights, refs = refs[:n_h], refs[n_h], refs[n_h + 1 :]
    full_o, gu_o, z_o, own_o, send_o, h_s, w_s, sems = refs
    units = z_o.shape[1]
    copies = into_rows(h_parts, h_s, sems, 0)
    w_copies = weights_into(weights, w_s, sems, n_h)
    start_all(copies + w_copies)
    wait_all(copies)
    whole = pltpu.make_async_copy(h_s, full_o, sems.at[0])
    whole.start()
    for r, rows in block_rows(w_s, w_copies):
        part = nn(h_s[:, rows], w_s[rows, : 2 * units])
        gu_o[...] = part if r == 0 else gu_o[...] + part
    g = gu_o[:, :units]
    u = gu_o[:, units:]
    z_o[...] = (g * u / (1.0 + jnp.exp(-g))).astype(LOW)
    z = z_o[...]
    for r, rows in block_rows(w_s):
        put_halves(nt(z, w_s[rows, 2 * units : 3 * units]), rows, own_o, send_o)
    whole.wait()


def mlp_backward(n_h, *refs):
    d_parts, weights, refs = refs[:n_h], refs[n_h], refs[n_h + 1 :]
    gu_i, full_o, dp_o, own_o, send_o, d_s, w_s, acc, gu, sems = refs
    units = acc.shape[1]
    copies = into_rows(d_parts, d_s, sems, 0)
    w_copies = weights_into(weights, w_s, sems, n_h)
    extra = load([(gu_i, gu)], sems, n_h + len(w_copies))
    start_all(copies + w_copies + extra)
    wait_all(copies)
    whole = pltpu.make_async_copy(d_s, full_o, sems.at[0])
    whole.start()
    for r, rows in block_rows(w_s, w_copies):
        part = nn(d_s[:, rows], w_s[rows, 2 * units : 3 * units])
        acc[...] = part if r == 0 else acc[...] + part
    wait_all(extra)
    g = gu[:, :units]
    u = gu[:, units:]
    sig = 1.0 / (1.0 + jnp.exp(-g))
    dz = acc[...]
    dp_o[:, :units] = (dz * u * sig * (1.0 + g * (1.0 - sig))).astype(LOW)
    dp_o[:, units:] = (dz * g * sig).astype(LOW)
    dp = dp_o[...]
    for r, rows in block_rows(w_s):
        put_halves(nt(dp, w_s[rows, : 2 * units]), rows, own_o, send_o)
    whole.wait()


def load_grads(args, a_s, b_s, da_s, db_s, sems):
    copies = load(list(zip(args, (a_s, b_s, da_s, db_s))), sems, 0)
    start_all(copies)
    wait_all(copies)


def weight_grads(*refs):
    out, a_s, b_s, da_s, db_s, slots, sems, out_sems = refs[4:]
    load_grads(refs[:4], a_s, b_s, da_s, db_s, sems)
    split, end = da_s.shape[1], da_s.shape[1] + db_s.shape[1]
    sent = []
    for i, at in enumerate(range(0, a_s.shape[1], BLOCK)):
        cols = slice(at, at + BLOCK)
        slot = slots.at[i % 2]
        if i >= 2:
            sent[i - 2].wait()
        slot[:, :split] = tn(a_s[:, cols], da_s[...]).astype(LOW)
        slot[:, split:end] = tn(b_s[:, cols], db_s[...]).astype(LOW)
        if end < slot.shape[1]:
            slot[:, end:] = jnp.zeros((BLOCK, slot.shape[1] - end), LOW)
        sent.append(pltpu.make_async_copy(slot, out.at[pl.ds(at, BLOCK)], out_sems.at[i]))
        sent[i].start()
    wait_all(sent[-2:])


def other_rows(block_sum, out, sem):
    rows = out.shape[0]
    at = (1 - lax.axis_index("clo")) * rows
    copy = pltpu.make_async_copy(
        block_sum.at[pl.ds(pl.multiple_of(at, rows), rows)], out, sem.at[0]
    )
    copy.start()
    copy.wait()


def put_grads(layer, n_old, n_first, *refs):
    block_sum, moved = refs[:2]
    first_o, second_o, mine_s, moved_s, first_s, second_s, sems = refs[2 + n_old :]
    rows = moved.shape[0]
    me = lax.axis_index("clo")
    own = block_sum
    if own.shape[0] > rows:
        own = own.at[pl.ds(pl.multiple_of(me * rows, rows), rows)]
    copies = load([(own, mine_s), (moved, moved_s)], sems, 0)
    start_all(copies)
    wait_all(copies)
    low = jnp.where(me == 0, mine_s[...], moved_s[...])
    high = jnp.where(me == 0, moved_s[...], mine_s[...])
    width = second_s.shape[1] // 2
    out = load([(first_s, first_o.at[layer]), (second_s, second_o.at[layer])], sems, 2)
    for core, part in enumerate((low, high)):
        to = slice(core * width, (core + 1) * width)
        for c in range(n_first):
            first_s[c, :, to] = part[:, c * width : (c + 1) * width].astype(F32)
        second_s[:, to] = part[:, n_first * width : (n_first + 1) * width].astype(F32)
    start_all(out)
    wait_all(out)


def order_columns(*refs):
    qkv, out, both, sems = refs
    width = both.shape[1] // 8
    copies = []
    for core in range(2):
        cols = pl.ds(core * width, width)
        for c in range(4):
            src = out.at[:, cols] if c == 3 else qkv.at[c, :, cols]
            dst = both.at[:, pl.ds((4 * core + c) * width, width)]
            copies.append(pltpu.make_async_copy(src, dst, sems.at[len(copies)]))
    start_all(copies)
    wait_all(copies)


def middle(own_i, moved_i, own_o, *sends):
    rows = own_o.shape[0]
    own_o[...] = own_i[:rows] + moved_i[:rows].astype(F32)
    for r, send in enumerate(sends):
        at = slice((r + 1) * rows, (r + 2) * rows)
        send[...] = (own_i[at] + moved_i[at].astype(F32)).astype(LOW)


def norm_of(value):
    center = value - jnp.mean(value, axis=-1, keepdims=True)
    inverse = lax.rsqrt(jnp.mean(center * center, axis=-1, keepdims=True) + NORM_EPS)
    return center * inverse, inverse


def norm_forward(x_i, gain, offset, *refs):
    terms, (x_o, h_o) = refs[:-2], refs[-2:]
    x = x_i[...]
    for t in terms:
        x = x + t[...].astype(F32)
    x_o[...] = x
    h_o[...] = (norm_of(x)[0] * gain[...] + offset[...]).astype(LOW)


def norm_backward(dx_i, y_i, gain, *refs):
    terms, (dy_o, low_o, small_o) = refs[:-3], refs[-3:]
    dh = terms[0][...]
    for t in terms[1:]:
        dh = dh + t[...].astype(F32)
    n, inverse = norm_of(y_i[...])
    small_o[0:1] = jnp.sum(dh * n, axis=0, keepdims=True)
    small_o[1:2] = jnp.sum(dh, axis=0, keepdims=True)
    scaled = dh * gain[...]
    dy = dx_i[...] + inverse * (
        scaled
        - jnp.mean(scaled, axis=-1, keepdims=True)
        - n * jnp.mean(scaled * n, axis=-1, keepdims=True)
    )
    dy_o[...] = dy
    low_o[...] = dy.astype(LOW)


def after(value, event):
    return lax.optimization_barrier((value, event))[0]


def log2(n):
    return n.bit_length() - 1


def reverse_bits(r, bits):
    return sum(((r >> k) & 1) << (bits - 1 - k) for k in range(bits))


def make_program(n_dp, n_chi, n_clo, n_mp):
    group_bits = [("chi", 1 << k) for k in range(log2(n_chi))]
    group_bits += [("dp", 1 << k) for k in range(log2(n_dp))]
    n_groups = n_dp * n_chi
    sizes = {"dp": n_dp, "chi": n_chi, "clo": n_clo, "mp": n_mp}

    def swap(value, axis, bit):
        return lax.ppermute(value, axis, [(i, i ^ bit) for i in range(sizes[axis])])

    def mp_gather(own):
        parts = [own]
        for k in reversed(range(log2(n_mp))):
            parts = parts + [swap(part, "mp", 1 << k) for part in parts]
        return [parts[reverse_bits(r, log2(n_mp))] for r in range(n_mp)]

    def token_gather(own):
        half = mp_gather(own)
        return half + [swap(part, "clo", 1) for part in half]

    def token_reduce(own_half, send_half, beside=None, before=None):
        rows, width = own_half.shape
        sub = rows // n_mp
        moved = swap(send_half, "clo", 1)
        if before is not None:
            (own_half, moved), before = lax.optimization_barrier(((own_half, moved), before))
        outs = [shape((sub, width), F32)] + [shape((sub, width), LOW)] * (n_mp - 1)
        parts = call(middle, 0, [own_half, moved], outs, [], rows * width)
        terms = [parts[0]] + [swap(parts[r], "mp", r) for r in range(1, n_mp)]
        result = None
        if beside is not None:
            work, args = beside
            terms, result = lax.optimization_barrier((terms, work(*after(args, parts[0]))))
        return terms, result, before

    def own_tokens(value):
        seqs, block, width = value.shape
        sub = block * n_chi // n_mp
        per_block = block // sub
        place = lax.axis_index("mp") % per_block
        mine = lax.dynamic_slice_in_dim(value, place * sub, sub, 1)
        chi = lax.axis_index("chi")
        here = lax.dynamic_index_in_dim(mine, chi, 0, keepdims=False)
        there = swap(lax.dynamic_index_in_dim(mine, 1 - chi, 0, keepdims=False), "chi", 1)
        return jnp.where(lax.axis_index("mp") // per_block == chi, here, there)

    def chi_swap(held, block, extra=None):
        chi = lax.axis_index("chi")
        mine = lax.dynamic_slice_in_dim(held, chi * block, block, 0)
        sent = lax.dynamic_slice_in_dim(held, (1 - chi) * block, block, 0)
        if extra is not None:
            sent = jnp.concatenate([sent, extra], axis=0)
        return mine, swap(sent, "chi", 1)

    def to_blocks(mine, moved, block):
        first = lax.axis_index("chi") == 0
        moved = moved[:block]
        return jnp.where(first, jnp.stack([mine, moved]), jnp.stack([moved, mine]))

    def by_place(parts):
        sub, width = parts[0].shape
        mp = lax.axis_index("mp")
        parts = jnp.stack(parts)
        for k in range(log2(n_mp)):
            pairs = parts.reshape(n_mp >> (k + 1), 2, 1 << k, sub, width)
            pairs = jnp.where((mp >> k) % 2 == 1, jnp.flip(pairs, 1), pairs)
            parts = pairs.reshape(n_mp, sub, width)
        return parts.reshape(n_mp * sub, width)

    def on_device(
        tokens, segments, cotangent, first_gain, first_bias, qkv_weight, qkv_bias,
        out_weight, second_gain, second_bias, gate_up_weight, down_weight,
    ):
        n_seq, block, width = tokens.shape
        rows_dev = qkv_weight.shape[1]
        half_in = qkv_weight.shape[3] // 2
        half_ff = down_weight.shape[2] // 2
        heads = half_in // HEAD
        total = block * n_chi * n_clo
        half_total = total // n_clo
        sub = half_total // n_mp
        n_parts = n_clo * n_mp
        mp, clo, chi = (lax.axis_index(a) for a in ("mp", "clo", "chi"))
        x_own = own_tokens(tokens).astype(F32)

        pad = -(3 * half_ff) % 128
        attn_cols, mlp_cols = 4 * half_in, 3 * half_ff + pad

        def attn_columns(l):
            view = jnp.transpose(qkv_weight[l], (1, 0, 2))
            outs = [shape((rows_dev, 2 * attn_cols), LOW)]
            args = [view, out_weight[l]]
            sems = [pltpu.SemaphoreType.DMA((8,))]
            return call(order_columns, 2, args, outs, sems, 0, hbm_outs=1)

        def mlp_columns(l):
            gu, down = jnp.transpose(gate_up_weight[l], (1, 0, 2)), down_weight[l]
            fill = jnp.zeros((rows_dev, pad), LOW)
            parts = []
            for cols in (slice(None, half_ff), slice(half_ff, None)):
                parts += [gu[0, :, cols], gu[1, :, cols], down[:, cols], fill]
            return jnp.concatenate(parts, axis=1)

        def gather_weights(own):
            return lax.all_gather(own, ("dp", "chi", "clo"), axis=0, tiled=True)

        weights = []
        for l in range(LAYERS):
            attn = [gather_weights(attn_columns(l)[0])]
            weights.append([attn, gather_weights(mlp_columns(l))])
        dx = own_tokens(cotangent)
        gains = jnp.stack([first_gain, first_bias, second_gain, second_bias])
        half_bias = jnp.where(clo == 1, qkv_bias[:, :, half_in:], qkv_bias[:, :, :half_in])
        half_bias = half_bias.reshape(LAYERS, 1, 3 * half_in)

        there = swap(lax.dynamic_index_in_dim(segments, 1 - chi, 0, keepdims=False), "chi", 1)
        here = lax.dynamic_index_in_dim(segments, chi, 0, keepdims=False)
        pair = jnp.stack([jnp.where(chi == 0, here, there), jnp.where(chi == 0, there, here)])
        other = swap(pair, "clo", 1)
        whole = jnp.stack(
            [jnp.where(clo == 0, pair, other), jnp.where(clo == 0, other, pair)], axis=1
        ).reshape(total)
        core_of = jnp.arange(n_clo, dtype=jnp.int32) ^ clo
        mp_of = jnp.arange(n_mp, dtype=jnp.int32) ^ mp
        per_block = block // sub
        place = (
            (mp_of // per_block * (n_clo * block) + mp_of % per_block * sub)[None, :, None]
            + (core_of * block)[:, None, None]
            + jnp.arange(sub, dtype=jnp.int32)[None, None, :]
        ).reshape(total)
        match = place[:, None] == jnp.arange(total, dtype=jnp.int32)[None, :]
        seg = jnp.sum(jnp.where(match, whole[None, :], 0), axis=1)
        starts = jnp.sum((seg[None, :] < seg[:, None]).astype(jnp.int32), axis=1)
        freq = jnp.exp(
            jnp.arange(ROT // 2, dtype=F32) * (-2.0 * math.log(10000.0) / ROT)
        )
        angles = freq[:, None] * (place - starts).astype(F32)[None, :]
        cos_t, sin_t = jnp.cos(angles).T, jnp.sin(angles).T
        zeros = jnp.zeros((total, ROT // 2), F32)
        tail = jnp.zeros((total, HEAD - ROT), F32)
        per_slab = 128 // HEAD
        tables = jnp.stack(
            [
                jnp.tile(jnp.concatenate(parts, axis=1), (1, per_slab))
                for parts in (
                    (cos_t, cos_t, tail + 1.0),
                    (-sin_t, zeros, tail),
                    (zeros, sin_t, tail),
                )
            ]
        )
        row = jnp.stack([seg, place])
        geometry = [tables, row.T, row]
        geometry_scratch = [
            pltpu.VMEM((3, total, 128), F32),
            pltpu.VMEM((total, 2), jnp.int32),
        ]

        act = shape((total, half_in), LOW)
        reduced = [shape((half_total, width), F32), shape((half_total, width), LOW)]
        sems = pltpu.SemaphoreType.DMA((n_parts + width // BLOCK + 5,))
        h_scratch = pltpu.VMEM((total, width), LOW)

        def mm(*dims):
            return 2 * math.prod(dims)

        def norm(x, gain, offset, terms):
            outs = [shape(x.shape, F32), shape(x.shape, LOW)]
            return call(norm_forward, 0, [x, gain[None], offset[None]] + terms, outs, [], 10 * x.size)

        def norm_back(dx, y, gain, terms):
            outs = [shape(y.shape, F32), shape(y.shape, LOW), shape((2, width), F32)]
            return call(norm_backward, 0, [dx, y, gain[None]] + terms, outs, [], 20 * y.size)

        def grads(a, b, da, db, cols):
            scratch = [pltpu.VMEM(x.shape, LOW) for x in (a, b, da, db)]
            scratch += [pltpu.VMEM((2, BLOCK, cols), LOW), pltpu.SemaphoreType.DMA((4,))]
            scratch += [pltpu.SemaphoreType.DMA((width // BLOCK,))]
            outs = [shape((width, cols), LOW)]
            flops = mm(total, width, cols)
            args = [a, b, da, db]
            return call(weight_grads, 4, args, outs, scratch, flops, hbm_outs=1, limit=60)

        def scatter(partial):
            return lax.psum_scatter(partial[0], ("dp", "chi"), scatter_dimension=0, tiled=True)

        def pick(block_sum):
            outs = [shape((rows_dev, block_sum.shape[1]), LOW)]
            sems = [pltpu.SemaphoreType.DMA((1,))]
            others = call(other_rows, 1, [block_sum], outs, sems, 0, hbm_outs=1)[0]
            return block_sum, swap(others, "clo", 1)

        def put(l, sums, n_first, unit, old):
            sums, moved = sums
            first, second = (n_first, rows_dev, 2 * unit), (rows_dev, 2 * unit)
            piece = pltpu.VMEM(moved.shape, LOW)
            return call(
                functools.partial(put_grads, l, len(old), n_first),
                2 + len(old),
                [sums, moved] + old,
                [shape((LAYERS,) + first, F32), shape((LAYERS,) + second, F32)],
                [
                    piece,
                    piece,
                    pltpu.VMEM(first, F32),
                    pltpu.VMEM(second, F32),
                    pltpu.SemaphoreType.DMA((4,)),
                ],
                0,
                hbm_outs=2,
                limit=60,
                aliases={2: 0, 3: 1} if old else None,
            )

        def put_attn(l, sums, old=()):
            return list(put(l, sums, 3, half_in, list(old)))

        def put_mlp(l, sums, old=()):
            return list(put(l, sums, 2, half_ff, list(old)))

        whole = shape((total, width), LOW)
        saved = []
        terms = []
        for l in range(LAYERS):
            w_attn, w_mlp = weights[l]
            x_own, h = norm(x_own, gains[0, l], gains[1, l], terms)
            h1 = token_gather(h)
            h1, q, k, v, o, own, send = call(
                functools.partial(attn_forward, n_parts, heads),
                n_parts + 3,
                h1 + w_attn + geometry + [half_bias[l]],
                [whole] + [act] * 4 + reduced,
                [
                    h_scratch,
                    pltpu.VMEM((width, attn_cols), LOW),
                    pltpu.VMEM((total, 3 * half_in), F32),
                ]
                + geometry_scratch
                + [sems],
                mm(total, width, attn_cols) + 2 * mm(heads, total, total, 2 * half_in),
                n_any=n_parts,
                hbm_outs=1,
                limit=56,
            )
            y_own, h = norm(x_own, gains[2, l], gains[3, l], token_reduce(own, send)[0])
            h2 = token_gather(h)
            if l == 0:
                h2, dm_parts = lax.optimization_barrier((h2, token_gather(dx)))
            h2, gu, z, own, send = call(
                functools.partial(mlp_forward, n_parts),
                n_parts + 1,
                h2 + [w_mlp],
                [whole, shape((total, 2 * half_ff), F32), shape((total, half_ff), LOW)] + reduced,
                [h_scratch, pltpu.VMEM((width, mlp_cols), LOW), sems],
                mm(total, width, mlp_cols),
                n_any=n_parts,
                hbm_outs=1,
            )
            saved.append((x_own, h1, q, k, v, o, y_own, h2, gu, z))
            x_own, terms = y_own, token_reduce(own, send)[0]

        dx = dx.astype(F32)
        small_out = [None] * LAYERS
        done = None
        for l in reversed(range(LAYERS)):
            w_attn, w_mlp = weights[l]
            x_own, h1, q, k, v, o, y_own, h2, gu, z = saved[l]
            parts = dm_parts if done is None else token_gather(low)
            if done is None:
                gu = after(gu, terms[0])
            dm, dp2, own, send = call(
                functools.partial(mlp_backward, n_parts),
                n_parts + 2,
                parts + [w_mlp, gu],
                [whole, shape((total, 2 * half_ff), LOW)] + reduced,
                [
                    h_scratch,
                    pltpu.VMEM((width, mlp_cols), LOW),
                    pltpu.VMEM((total, half_ff), F32),
                    pltpu.VMEM(gu.shape, F32),
                    sems,
                ],
                mm(total, width, mlp_cols),
                n_any=n_parts,
                hbm_outs=1,
            )
            work = functools.partial(grads, cols=mlp_cols)
            if done is None:
                before = terms, work(h2, dm, dp2, z)
                terms, _, (last, g_mlp) = token_reduce(own, send, before=before)
                x_last = y_own
                for t in last:
                    x_last = x_last + t.astype(F32)
                x_last = x_last.astype(LOW)
            else:
                terms, g_mlp, _ = token_reduce(own, send, (work, (h2, dm, dp2, z)))
            g_mlp = scatter(g_mlp)
            dy, low, small_two = norm_back(dx, y_own, gains[2, l], terms)
            parts = token_gather(low)
            if done is not None:
                sums = put_mlp(l + 1, pick(done[1])), put_attn(l + 1, pick(done[0]))
                parts, (mlp_sum, attn_sum) = lax.optimization_barrier((parts, sums))
            da, dp1, bias_grad, own, send = call(
                functools.partial(attn_backward, n_parts, heads),
                n_parts + 6,
                parts + w_attn + [q, k, v] + geometry,
                [whole, shape((total, 3 * half_in), LOW), shape((1, 3 * half_in), F32)] + reduced,
                [
                    h_scratch,
                    pltpu.VMEM((width, attn_cols), LOW),
                    pltpu.VMEM((total, half_in), F32),
                    pltpu.VMEM((3, total, half_in), LOW),
                ]
                + geometry_scratch
                + [sems],
                mm(total, width, attn_cols) + 5 * mm(heads, total, total, half_in),
                n_any=n_parts,
                hbm_outs=1,
                limit=56,
            )
            work = functools.partial(grads, cols=attn_cols)
            if done is None:
                terms, g_attn, _ = token_reduce(own, send, (work, (h1, da, dp1, o)))
                done = (scatter(g_attn), g_mlp)
            else:
                terms, g_attn, _ = token_reduce(own, send, (work, (h1, da, dp1, o)))
            dx, low, small_one = norm_back(dy, x_own, gains[0, l], terms)
            small_out[l] = (small_one, small_two, bias_grad)
        norms = jnp.concatenate([part for l in range(LAYERS) for part in small_out[l][:2]], axis=0)
        bias = jnp.concatenate([small_out[l][2] for l in range(LAYERS)], axis=1)
        rows = -(-bias.size // width)
        bias = jnp.pad(bias, ((0, 0), (0, rows * width - bias.size))).reshape(rows, width)
        parts = mp_gather(jnp.concatenate([low, norms.astype(LOW)], axis=0))
        norms = sum(part[sub:].astype(F32) for part in parts)
        both = jnp.concatenate([norms, bias], axis=0).astype(LOW)
        mine, moved = chi_swap(by_place([part[:sub] for part in parts]), block, both)
        g_mlp, x_last = after((g_mlp, x_last), parts[n_mp // 2])
        g_gu, g_down = put_mlp(0, pick(g_mlp), mlp_sum)
        g_gu = jnp.swapaxes(g_gu, 1, 2)
        g_gu = with_layout_constraint(g_gu, Layout(major_to_minor=(0, 1, 2, 3)))
        x_parts = after(mp_gather(x_last), g_gu)
        x_mine, x_moved = chi_swap(by_place(x_parts), block)
        moved = after(moved, x_parts)
        tokens_grad = to_blocks(mine, moved, block).astype(F32)
        both = both.astype(F32) + moved[block:].astype(F32)
        activations = to_blocks(x_mine, x_moved, block)
        for name, bit in group_bits[1:]:
            both = both + swap(both, name, bit)
        other = swap(both, "clo", 1)
        norms = (both + other)[: 4 * LAYERS].reshape(LAYERS, 4, width)
        mine, others = (
            x[4 * LAYERS :].reshape(-1)[: LAYERS * 3 * half_in].reshape(LAYERS, 3, half_in)
            for x in (both, other)
        )
        low, high = jnp.where(clo == 0, mine, others), jnp.where(clo == 0, others, mine)
        bias = jnp.concatenate([low, high], axis=2)
        norms = [norms[:, i] for i in range(4)]
        g_attn = after(scatter(g_attn), (tokens_grad, activations, g_gu, norms, bias))
        g_qkv, g_out = put_attn(0, pick(g_attn), attn_sum)
        g_qkv = jnp.swapaxes(g_qkv, 1, 2)

        return (
            activations, tokens_grad, norms[0], norms[1],
            g_qkv, bias, g_out, norms[2], norms[3], g_gu, g_down,
        )

    return on_device


def solution(mesh):
    n_dp, n_ctx, n_mp = (mesh.shape[a] for a in ("dp", "ctx", "mp"))
    n_clo = 2
    n_chi = n_ctx // n_clo
    fine = Mesh(mesh.devices.reshape(n_dp, n_chi, n_clo, n_mp), ("dp", "chi", "clo", "mp"))
    rows = ("dp", "chi", "clo")
    ctx = ("chi", "clo")
    token_spec = P("dp", ctx, None)
    four, three = P(None, rows, None, "mp"), P(None, rows, "mp")
    bias_spec = P(None, None, "mp")
    return jax.shard_map(
        make_program(n_dp, n_chi, n_clo, n_mp),
        mesh=fine,
        in_specs=(
            token_spec, P("dp", ctx), token_spec, P(), P(), four, bias_spec, three, P(), P(),
            four, three,
        ),
        out_specs=(
            token_spec, token_spec, P(), P(), four, bias_spec, three, P(), P(), four, three,
        ),
        check_vma=False,
    )
```

```python
import functools
import math

import jax
import jax.numpy as jnp
from jax import lax
from jax.experimental import pallas as pl
from jax.experimental.layout import Layout, with_layout_constraint
from jax.experimental.pallas import tpu as pltpu
from jax.sharding import Mesh
from jax.sharding import PartitionSpec as P

HEAD = 64
ROT = 16
LAYERS = 2
NORM_EPS = 1e-05
MASK_FILL = -1e30
LOW = jnp.bfloat16
F32 = jnp.float32
MIB = 1024 * 1024
BLOCK = 512
HBM = pl.BlockSpec(memory_space=pltpu.HBM)
ANY = pl.BlockSpec(memory_space=pl.ANY)
VMEM = pl.BlockSpec(memory_space=pltpu.VMEM)


def dot(a, b, dims):
    return lax.dot_general(a, b, (dims, ((), ())), preferred_element_type=F32)


def nn(a, b):
    return dot(a, b, ((1,), (0,)))


def nt(a, b):
    return dot(a, b, ((1,), (1,)))


def tn(a, b):
    return dot(a, b, ((0,), (0,)))


def shape(dims, kind):
    return jax.ShapeDtypeStruct(dims, kind)


def call(body, n_hbm, args, outs, scratch, flops, hbm_outs=0, n_any=0, limit=32, aliases=None):
    moved = sum(a.size * a.dtype.itemsize for a in args)
    moved += sum(math.prod(o.shape) * jnp.dtype(o.dtype).itemsize for o in outs)
    return pl.pallas_call(
        body,
        out_shape=tuple(outs),
        in_specs=[ANY] * n_any + [HBM] * (n_hbm - n_any) + [VMEM] * (len(args) - n_hbm),
        out_specs=tuple([HBM] * hbm_outs + [VMEM] * (len(outs) - hbm_outs)),
        scratch_shapes=scratch,
        input_output_aliases=aliases or {},
        compiler_params=pltpu.CompilerParams(vmem_limit_bytes=limit * MIB),
        cost_estimate=pl.CostEstimate(flops=flops, bytes_accessed=moved, transcendentals=0),
    )(*args)


def into_rows(pieces, whole, sems, first):
    copies, row = [], 0
    for i, piece in enumerate(pieces):
        rows = piece.shape[0]
        copies.append(
            pltpu.make_async_copy(piece, whole.at[pl.ds(row, rows)], sems.at[first + i])
        )
        row += rows
    return copies


def weights_into(weights, whole, sems, first):
    rows, width = whole.shape
    cols = pl.ds(pl.multiple_of(lax.axis_index("clo") * width, 128), width)
    copies = []
    for at in range(0, rows, BLOCK):
        src, dst = weights.at[pl.ds(at, BLOCK), cols], whole.at[pl.ds(at, BLOCK)]
        copies.append(pltpu.make_async_copy(src, dst, sems.at[first + len(copies)]))
    return copies


def start_all(copies):
    for c in copies:
        c.start()


def wait_all(copies):
    for c in copies:
        c.wait()


def rolled(value, tables, sign):
    cos_t, ahead_t, behind_t = tables[0], tables[1], tables[2]
    slabs = []
    for at in range(0, value.shape[1], 128):
        x = value[:, at : at + 128]
        ahead = pltpu.roll(x, 128 - ROT // 2, 1)
        behind = pltpu.roll(x, ROT // 2, 1)
        slabs.append(x * cos_t + sign * (ahead * ahead_t + behind * behind_t))
    return jnp.concatenate(slabs, axis=1).astype(LOW)


def allowed_of(column, row):
    return (column[:, 0:1] == row[0:1]) & (row[1:2] <= column[:, 1:2])


def put_halves(tile, cols, own_ref, send_ref):
    half = own_ref.shape[0]
    own_ref[:, cols] = tile[:half].astype(LOW)
    send_ref[:, cols] = tile[half:].astype(LOW)


def softmax_of(q_h, k, allowed, scale):
    s = jnp.where(allowed, nt(q_h * scale, k), MASK_FILL)
    top = jnp.max(s, axis=-1, keepdims=True)
    e = jnp.exp(s - top)
    return e * (1.0 / jnp.sum(e, axis=-1, keepdims=True))


def load(pairs, sems, first):
    return [
        pltpu.make_async_copy(src, dst, sems.at[first + i]) for i, (src, dst) in enumerate(pairs)
    ]


def block_rows(w_s, w_copies=None):
    for i, at in enumerate(range(0, w_s.shape[0], BLOCK)):
        if w_copies is not None:
            w_copies[i].wait()
        yield i, slice(at, at + BLOCK)


def attn_forward(n_h, heads, *refs):
    h_parts, weights, refs = refs[:n_h], refs[n_h], refs[n_h + 1 :]
    tables, column, row, bias = refs[:4]
    full_o, q_o, k_o, v_o, o_o, own_o, send_o, h_s, w_s, acc, tab, col, sems = refs[4:]
    width = heads * HEAD
    copies = into_rows(h_parts, h_s, sems, 0)
    w_copies = weights_into(weights, w_s, sems, n_h)
    extra = load([(tables, tab), (column, col)], sems, n_h + len(w_copies))
    start_all(copies + w_copies + extra)
    wait_all(copies)
    whole = pltpu.make_async_copy(h_s, full_o, sems.at[0])
    whole.start()
    for r, rows in block_rows(w_s, w_copies):
        for c in range(3):
            cols = slice(c * width, (c + 1) * width)
            part = nn(h_s[:, rows], w_s[rows, cols])
            acc[:, cols] = part + (bias[:, cols] if r == 0 else acc[:, cols])
    wait_all(extra)
    q_o[...] = rolled(acc[:, :width], tab, 1.0)
    k_o[...] = rolled(acc[:, width : 2 * width], tab, 1.0)
    v_o[...] = acc[:, 2 * width :].astype(LOW)
    lane = lax.broadcasted_iota(jnp.int32, (1, width), 1) // HEAD
    allowed = allowed_of(col, row)
    k, v, q = k_o[...], v_o[...], q_o[...]
    zero = jnp.zeros((), LOW)
    o = None
    for h in range(heads):
        mine = lane == h
        w = softmax_of(jnp.where(mine, q, zero), k, allowed, LOW(1.0 / math.sqrt(HEAD)))
        part = nn(w.astype(LOW), jnp.where(mine, v, zero))
        o = part if o is None else o + part
    o_o[...] = o.astype(LOW)
    o = o_o[...]
    for r, rows in block_rows(w_s):
        put_halves(nt(o, w_s[rows, 3 * width :]), rows, own_o, send_o)
    whole.wait()


def attn_backward(n_h, heads, *refs):
    d_parts, weights, refs = refs[:n_h], refs[n_h], refs[n_h + 1 :]
    q_i, k_i, v_i, tables, column, row = refs[:6]
    full_o, dp_o, bias_o, own_o, send_o, d_s, w_s, acc, qkv, tab, col, sems = refs[6:]
    width = heads * HEAD
    copies = into_rows(d_parts, d_s, sems, 0)
    w_copies = weights_into(weights, w_s, sems, n_h)
    extra = load(
        [(q_i, qkv.at[0]), (k_i, qkv.at[1]), (v_i, qkv.at[2]), (tables, tab), (column, col)],
        sems,
        n_h + len(w_copies),
    )
    start_all(copies + w_copies + extra)
    wait_all(copies)
    whole = pltpu.make_async_copy(d_s, full_o, sems.at[0])
    whole.start()
    for r, rows in block_rows(w_s, w_copies):
        part = nn(d_s[:, rows], w_s[rows, 3 * width :])
        acc[...] = part if r == 0 else acc[...] + part
    do = acc[...].astype(LOW)
    wait_all(extra)
    q, k, v = qkv[0], qkv[1], qkv[2]
    lane = lax.broadcasted_iota(jnp.int32, (1, width), 1) // HEAD
    allowed = allowed_of(col, row)
    zero = jnp.zeros((), LOW)
    scale = 1.0 / math.sqrt(HEAD)
    dq = dk = dv = None
    for h in range(heads):
        mine = lane == h
        q_h = jnp.where(mine, q, zero)
        do_h = jnp.where(mine, do, zero)
        w = softmax_of(q_h, k, allowed, LOW(scale))
        dw = nt(do_h, v)
        ds = (w * (dw - jnp.sum(w * dw, axis=-1, keepdims=True))).astype(LOW)
        dv_h = tn(w.astype(LOW), do_h)
        dq_h = nn(ds, jnp.where(mine, k, zero))
        dk_h = tn(ds, q_h)
        dq, dk, dv = (
            (dq_h, dk_h, dv_h) if h == 0 else (dq + dq_h, dk + dk_h, dv + dv_h)
        )
    dp_o[:, :width] = rolled(dq * scale, tab, -1.0)
    dp_o[:, width : 2 * width] = rolled(dk * scale, tab, -1.0)
    dp_o[:, 2 * width :] = dv.astype(LOW)
    dp = dp_o[...]
    bias_o[...] = jnp.sum(dp.astype(F32), axis=0, keepdims=True)
    for r, rows in block_rows(w_s):
        put_halves(nt(dp, w_s[rows, : 3 * width]), rows, own_o, send_o)
    whole.wait()


def mlp_forward(n_h, *refs):
    h_parts, weights, refs = refs[:n_h], refs[n_h], refs[n_h + 1 :]
    full_o, gu_o, z_o, own_o, send_o, h_s, w_s, acc, sems = refs
    units = z_o.shape[1]
    copies = into_rows(h_parts, h_s, sems, 0)
    w_copies = weights_into(weights, w_s, sems, n_h)
    start_all(copies + w_copies)
    wait_all(copies)
    whole = pltpu.make_async_copy(h_s, full_o, sems.at[0])
    whole.start()
    for r, rows in block_rows(w_s, w_copies):
        part = nn(h_s[:, rows], w_s[rows, : 2 * units])
        acc[...] = part if r == 0 else acc[...] + part
    gu_o[...] = acc[...].astype(LOW)
    g = acc[:, :units]
    u = acc[:, units:]
    z_o[...] = (g * u / (1.0 + jnp.exp(-g))).astype(LOW)
    z = z_o[...]
    for r, rows in block_rows(w_s):
        put_halves(nt(z, w_s[rows, 2 * units : 3 * units]), rows, own_o, send_o)
    whole.wait()


def mlp_backward(n_h, *refs):
    d_parts, weights, refs = refs[:n_h], refs[n_h], refs[n_h + 1 :]
    gu_i, full_o, dp_o, own_o, send_o, d_s, w_s, acc, gu, sems = refs
    units = acc.shape[1]
    copies = into_rows(d_parts, d_s, sems, 0)
    w_copies = weights_into(weights, w_s, sems, n_h)
    extra = load([(gu_i, gu)], sems, n_h + len(w_copies))
    start_all(copies + w_copies + extra)
    wait_all(copies)
    whole = pltpu.make_async_copy(d_s, full_o, sems.at[0])
    whole.start()
    for r, rows in block_rows(w_s, w_copies):
        part = nn(d_s[:, rows], w_s[rows, 2 * units : 3 * units])
        acc[...] = part if r == 0 else acc[...] + part
    wait_all(extra)
    g = gu[:, :units].astype(F32)
    u = gu[:, units:].astype(F32)
    sig = 1.0 / (1.0 + jnp.exp(-g))
    dz = acc[...]
    dp_o[:, :units] = (dz * u * sig * (1.0 + g * (1.0 - sig))).astype(LOW)
    dp_o[:, units:] = (dz * g * sig).astype(LOW)
    dp = dp_o[...]
    for r, rows in block_rows(w_s):
        put_halves(nt(dp, w_s[rows, : 2 * units]), rows, own_o, send_o)
    whole.wait()


def load_grads(args, a_s, b_s, da_s, db_s, sems):
    copies = load(list(zip(args, (a_s, b_s, da_s, db_s))), sems, 0)
    start_all(copies)
    wait_all(copies)


def weight_grads(*refs):
    out, a_s, b_s, da_s, db_s, slots, sems, out_sems = refs[4:]
    load_grads(refs[:4], a_s, b_s, da_s, db_s, sems)
    split, end = da_s.shape[1], da_s.shape[1] + db_s.shape[1]
    sent = []
    for i, at in enumerate(range(0, a_s.shape[1], BLOCK)):
        cols = slice(at, at + BLOCK)
        slot = slots.at[i % 2]
        if i >= 2:
            sent[i - 2].wait()
        slot[:, :split] = tn(a_s[:, cols], da_s[...]).astype(LOW)
        slot[:, split:end] = tn(b_s[:, cols], db_s[...]).astype(LOW)
        if end < slot.shape[1]:
            slot[:, end:] = jnp.zeros((BLOCK, slot.shape[1] - end), LOW)
        sent.append(pltpu.make_async_copy(slot, out.at[pl.ds(at, BLOCK)], out_sems.at[i]))
        sent[i].start()
    wait_all(sent[-2:])


def other_rows(block_sum, out, sem):
    rows = out.shape[0]
    at = (1 - lax.axis_index("clo")) * rows
    copy = pltpu.make_async_copy(
        block_sum.at[pl.ds(pl.multiple_of(at, rows), rows)], out, sem.at[0]
    )
    copy.start()
    copy.wait()


def put_grads(layer, n_old, n_first, *refs):
    block_sum, moved = refs[:2]
    first_o, second_o, mine_s, moved_s, first_s, second_s, sems = refs[2 + n_old :]
    rows = moved.shape[0]
    me = lax.axis_index("clo")
    own = block_sum
    if own.shape[0] > rows:
        own = own.at[pl.ds(pl.multiple_of(me * rows, rows), rows)]
    copies = load([(own, mine_s), (moved, moved_s)], sems, 0)
    start_all(copies)
    wait_all(copies)
    low = jnp.where(me == 0, mine_s[...], moved_s[...])
    high = jnp.where(me == 0, moved_s[...], mine_s[...])
    width = second_s.shape[1] // 2
    out = load([(first_s, first_o.at[layer]), (second_s, second_o.at[layer])], sems, 2)
    for core, part in enumerate((low, high)):
        to = slice(core * width, (core + 1) * width)
        for c in range(n_first):
            first_s[c, :, to] = part[:, c * width : (c + 1) * width].astype(F32)
        second_s[:, to] = part[:, n_first * width : (n_first + 1) * width].astype(F32)
    start_all(out)
    wait_all(out)


def order_columns(*refs):
    qkv, out, both, sems = refs
    width = both.shape[1] // 8
    copies = []
    for core in range(2):
        cols = pl.ds(core * width, width)
        for c in range(4):
            src = out.at[:, cols] if c == 3 else qkv.at[c, :, cols]
            dst = both.at[:, pl.ds((4 * core + c) * width, width)]
            copies.append(pltpu.make_async_copy(src, dst, sems.at[len(copies)]))
    start_all(copies)
    wait_all(copies)


def middle(own_i, moved_i, own_o, *sends):
    rows = own_o.shape[0]
    own_o[...] = own_i[:rows].astype(F32) + moved_i[:rows].astype(F32)
    for r, send in enumerate(sends):
        at = slice((r + 1) * rows, (r + 2) * rows)
        send[...] = (own_i[at].astype(F32) + moved_i[at].astype(F32)).astype(LOW)


def norm_of(value):
    center = value - jnp.mean(value, axis=-1, keepdims=True)
    inverse = lax.rsqrt(jnp.mean(center * center, axis=-1, keepdims=True) + NORM_EPS)
    return center * inverse, inverse


def norm_forward(x_i, gain, offset, *refs):
    terms, (x_o, h_o) = refs[:-2], refs[-2:]
    x = x_i[...]
    for t in terms:
        x = x + t[...].astype(F32)
    x_o[...] = x
    h_o[...] = (norm_of(x)[0] * gain[...] + offset[...]).astype(LOW)


def norm_backward(dx_i, y_i, gain, *refs):
    terms, (dy_o, low_o, small_o) = refs[:-3], refs[-3:]
    dh = terms[0][...]
    for t in terms[1:]:
        dh = dh + t[...].astype(F32)
    n, inverse = norm_of(y_i[...])
    small_o[0:1] = jnp.sum(dh * n, axis=0, keepdims=True)
    small_o[1:2] = jnp.sum(dh, axis=0, keepdims=True)
    scaled = dh * gain[...]
    dy = dx_i[...] + inverse * (
        scaled
        - jnp.mean(scaled, axis=-1, keepdims=True)
        - n * jnp.mean(scaled * n, axis=-1, keepdims=True)
    )
    dy_o[...] = dy
    low_o[...] = dy.astype(LOW)


def after(value, event):
    return lax.optimization_barrier((value, event))[0]


def log2(n):
    return n.bit_length() - 1


def reverse_bits(r, bits):
    return sum(((r >> k) & 1) << (bits - 1 - k) for k in range(bits))


def make_program(n_dp, n_chi, n_clo, n_mp):
    group_bits = [("chi", 1 << k) for k in range(log2(n_chi))]
    group_bits += [("dp", 1 << k) for k in range(log2(n_dp))]
    n_groups = n_dp * n_chi
    sizes = {"dp": n_dp, "chi": n_chi, "clo": n_clo, "mp": n_mp}

    def swap(value, axis, bit):
        return lax.ppermute(value, axis, [(i, i ^ bit) for i in range(sizes[axis])])

    def mp_gather(own):
        parts = [own]
        for k in reversed(range(log2(n_mp))):
            parts = parts + [swap(part, "mp", 1 << k) for part in parts]
        return [parts[reverse_bits(r, log2(n_mp))] for r in range(n_mp)]

    def token_gather(own):
        half = mp_gather(own)
        return half + [swap(part, "clo", 1) for part in half]

    def token_reduce(own_half, send_half, beside=None, before=None):
        rows, width = own_half.shape
        sub = rows // n_mp
        if before is not None:
            send_half, before = lax.optimization_barrier((send_half, before))
        moved = swap(send_half, "clo", 1)
        outs = [shape((sub, width), F32)] + [shape((sub, width), LOW)] * (n_mp - 1)
        parts = call(middle, 0, [own_half, moved], outs, [], rows * width)
        terms = [parts[0]] + [swap(parts[r], "mp", r) for r in range(1, n_mp)]
        result = None
        if beside is not None:
            work, args = beside
            terms, result = lax.optimization_barrier((terms, work(*after(args, parts[0]))))
        return terms, result, before

    def own_tokens(value):
        seqs, block, width = value.shape
        sub = block * n_chi // n_mp
        per_block = block // sub
        place = lax.axis_index("mp") % per_block
        mine = lax.dynamic_slice_in_dim(value, place * sub, sub, 1)
        chi = lax.axis_index("chi")
        here = lax.dynamic_index_in_dim(mine, chi, 0, keepdims=False)
        there = swap(lax.dynamic_index_in_dim(mine, 1 - chi, 0, keepdims=False), "chi", 1)
        return jnp.where(lax.axis_index("mp") // per_block == chi, here, there)

    def chi_swap(held, block, extra=None):
        chi = lax.axis_index("chi")
        mine = lax.dynamic_slice_in_dim(held, chi * block, block, 0)
        sent = lax.dynamic_slice_in_dim(held, (1 - chi) * block, block, 0)
        if extra is not None:
            sent = jnp.concatenate([sent, extra], axis=0)
        return mine, swap(sent, "chi", 1)

    def to_blocks(mine, moved, block):
        first = lax.axis_index("chi") == 0
        moved = moved[:block]
        return jnp.where(first, jnp.stack([mine, moved]), jnp.stack([moved, mine]))

    def by_place(parts):
        sub, width = parts[0].shape
        mp = lax.axis_index("mp")
        parts = jnp.stack(parts)
        for k in range(log2(n_mp)):
            pairs = parts.reshape(n_mp >> (k + 1), 2, 1 << k, sub, width)
            pairs = jnp.where((mp >> k) % 2 == 1, jnp.flip(pairs, 1), pairs)
            parts = pairs.reshape(n_mp, sub, width)
        return parts.reshape(n_mp * sub, width)

    def on_device(
        tokens, segments, cotangent, first_gain, first_bias, qkv_weight, qkv_bias,
        out_weight, second_gain, second_bias, gate_up_weight, down_weight,
    ):
        n_seq, block, width = tokens.shape
        rows_dev = qkv_weight.shape[1]
        half_in = qkv_weight.shape[3] // 2
        half_ff = down_weight.shape[2] // 2
        heads = half_in // HEAD
        total = block * n_chi * n_clo
        half_total = total // n_clo
        sub = half_total // n_mp
        n_parts = n_clo * n_mp
        mp, clo, chi = (lax.axis_index(a) for a in ("mp", "clo", "chi"))
        x_own = own_tokens(tokens).astype(F32)

        pad = -(3 * half_ff) % 128
        attn_cols, mlp_cols = 4 * half_in, 3 * half_ff + pad

        def attn_columns(l):
            view = jnp.transpose(qkv_weight[l], (1, 0, 2))
            outs = [shape((rows_dev, 2 * attn_cols), LOW)]
            args = [view, out_weight[l]]
            sems = [pltpu.SemaphoreType.DMA((8,))]
            return call(order_columns, 2, args, outs, sems, 0, hbm_outs=1)

        def mlp_columns(l):
            gu, down = jnp.transpose(gate_up_weight[l], (1, 0, 2)), down_weight[l]
            fill = jnp.zeros((rows_dev, pad), LOW)
            parts = []
            for cols in (slice(None, half_ff), slice(half_ff, None)):
                parts += [gu[0, :, cols], gu[1, :, cols], down[:, cols], fill]
            return jnp.concatenate(parts, axis=1)

        def gather_weights(own):
            return lax.all_gather(own, ("dp", "chi", "clo"), axis=0, tiled=True)

        weights = []
        for l in range(LAYERS):
            attn = [gather_weights(attn_columns(l)[0])]
            weights.append([attn, gather_weights(mlp_columns(l))])
        dx = own_tokens(cotangent)
        gains = jnp.stack([first_gain, first_bias, second_gain, second_bias])
        half_bias = jnp.where(clo == 1, qkv_bias[:, :, half_in:], qkv_bias[:, :, :half_in])
        half_bias = half_bias.reshape(LAYERS, 1, 3 * half_in)

        there = swap(lax.dynamic_index_in_dim(segments, 1 - chi, 0, keepdims=False), "chi", 1)
        here = lax.dynamic_index_in_dim(segments, chi, 0, keepdims=False)
        pair = jnp.stack([jnp.where(chi == 0, here, there), jnp.where(chi == 0, there, here)])
        other = swap(pair, "clo", 1)
        whole = jnp.stack(
            [jnp.where(clo == 0, pair, other), jnp.where(clo == 0, other, pair)], axis=1
        ).reshape(total)
        core_of = jnp.arange(n_clo, dtype=jnp.int32) ^ clo
        mp_of = jnp.arange(n_mp, dtype=jnp.int32) ^ mp
        per_block = block // sub
        place = (
            (mp_of // per_block * (n_clo * block) + mp_of % per_block * sub)[None, :, None]
            + (core_of * block)[:, None, None]
            + jnp.arange(sub, dtype=jnp.int32)[None, None, :]
        ).reshape(total)
        match = place[:, None] == jnp.arange(total, dtype=jnp.int32)[None, :]
        seg = jnp.sum(jnp.where(match, whole[None, :], 0), axis=1)
        starts = jnp.sum((seg[None, :] < seg[:, None]).astype(jnp.int32), axis=1)
        freq = jnp.exp(
            jnp.arange(ROT // 2, dtype=F32) * (-2.0 * math.log(10000.0) / ROT)
        )
        angles = freq[:, None] * (place - starts).astype(F32)[None, :]
        cos_t, sin_t = jnp.cos(angles).T, jnp.sin(angles).T
        zeros = jnp.zeros((total, ROT // 2), F32)
        tail = jnp.zeros((total, HEAD - ROT), F32)
        per_slab = 128 // HEAD
        tables = jnp.stack(
            [
                jnp.tile(jnp.concatenate(parts, axis=1), (1, per_slab))
                for parts in (
                    (cos_t, cos_t, tail + 1.0),
                    (-sin_t, zeros, tail),
                    (zeros, sin_t, tail),
                )
            ]
        )
        row = jnp.stack([seg, place])
        geometry = [tables, row.T, row]
        geometry_scratch = [
            pltpu.VMEM((3, total, 128), F32),
            pltpu.VMEM((total, 2), jnp.int32),
        ]

        act = shape((total, half_in), LOW)
        reduced = [shape((half_total, width), LOW)] * 2
        sems = pltpu.SemaphoreType.DMA((n_parts + width // BLOCK + 5,))
        h_scratch = pltpu.VMEM((total, width), LOW)

        def mm(*dims):
            return 2 * math.prod(dims)

        def norm(x, gain, offset, terms):
            outs = [shape(x.shape, F32), shape(x.shape, LOW)]
            return call(norm_forward, 0, [x, gain[None], offset[None]] + terms, outs, [], 10 * x.size)

        def norm_back(dx, y, gain, terms):
            outs = [shape(y.shape, F32), shape(y.shape, LOW), shape((2, width), F32)]
            return call(norm_backward, 0, [dx, y, gain[None]] + terms, outs, [], 20 * y.size)

        def grads(a, b, da, db, cols):
            scratch = [pltpu.VMEM(x.shape, LOW) for x in (a, b, da, db)]
            scratch += [pltpu.VMEM((2, BLOCK, cols), LOW), pltpu.SemaphoreType.DMA((4,))]
            scratch += [pltpu.SemaphoreType.DMA((width // BLOCK,))]
            outs = [shape((width, cols), LOW)]
            flops = mm(total, width, cols)
            args = [a, b, da, db]
            return call(weight_grads, 4, args, outs, scratch, flops, hbm_outs=1, limit=60)

        def scatter(partial):
            return lax.psum_scatter(partial[0], ("dp", "chi"), scatter_dimension=0, tiled=True)

        def pick(block_sum):
            outs = [shape((rows_dev, block_sum.shape[1]), LOW)]
            sems = [pltpu.SemaphoreType.DMA((1,))]
            others = call(other_rows, 1, [block_sum], outs, sems, 0, hbm_outs=1)[0]
            return block_sum, swap(others, "clo", 1)

        def put(l, sums, n_first, unit, old):
            sums, moved = sums
            first, second = (n_first, rows_dev, 2 * unit), (rows_dev, 2 * unit)
            piece = pltpu.VMEM(moved.shape, LOW)
            return call(
                functools.partial(put_grads, l, len(old), n_first),
                2 + len(old),
                [sums, moved] + old,
                [shape((LAYERS,) + first, F32), shape((LAYERS,) + second, F32)],
                [
                    piece,
                    piece,
                    pltpu.VMEM(first, F32),
                    pltpu.VMEM(second, F32),
                    pltpu.SemaphoreType.DMA((4,)),
                ],
                0,
                hbm_outs=2,
                limit=60,
                aliases={2: 0, 3: 1} if old else None,
            )

        def put_attn(l, sums, old=()):
            return list(put(l, sums, 3, half_in, list(old)))

        def put_mlp(l, sums, old=()):
            return list(put(l, sums, 2, half_ff, list(old)))

        whole = shape((total, width), LOW)
        saved = []
        terms = []
        for l in range(LAYERS):
            w_attn, w_mlp = weights[l]
            x_own, h = norm(x_own, gains[0, l], gains[1, l], terms)
            h1 = token_gather(h)
            h1, q, k, v, o, own, send = call(
                functools.partial(attn_forward, n_parts, heads),
                n_parts + 3,
                h1 + w_attn + geometry + [half_bias[l]],
                [whole] + [act] * 4 + reduced,
                [
                    h_scratch,
                    pltpu.VMEM((width, attn_cols), LOW),
                    pltpu.VMEM((total, 3 * half_in), F32),
                ]
                + geometry_scratch
                + [sems],
                mm(total, width, attn_cols) + 2 * mm(heads, total, total, 2 * half_in),
                n_any=n_parts,
                hbm_outs=1,
                limit=56,
            )
            y_own, h = norm(x_own, gains[2, l], gains[3, l], token_reduce(own, send)[0])
            h2 = token_gather(h)
            if l == 0:
                h2, dm_parts = lax.optimization_barrier((h2, token_gather(dx)))
            h2, gu, z, own, send = call(
                functools.partial(mlp_forward, n_parts),
                n_parts + 1,
                h2 + [w_mlp],
                [whole, shape((total, 2 * half_ff), LOW), shape((total, half_ff), LOW)] + reduced,
                [
                    h_scratch,
                    pltpu.VMEM((width, mlp_cols), LOW),
                    pltpu.VMEM((total, 2 * half_ff), F32),
                    sems,
                ],
                mm(total, width, mlp_cols),
                n_any=n_parts,
                hbm_outs=1,
            )
            saved.append((x_own, h1, q, k, v, o, y_own, h2, gu, z))
            x_own, terms = y_own, token_reduce(own, send)[0]

        dx = dx.astype(F32)
        small_out = [None] * LAYERS
        done = None
        for l in reversed(range(LAYERS)):
            w_attn, w_mlp = weights[l]
            x_own, h1, q, k, v, o, y_own, h2, gu, z = saved[l]
            parts = dm_parts if done is None else token_gather(low)
            if done is None:
                gu = after(gu, terms[0])
            dm, dp2, own, send = call(
                functools.partial(mlp_backward, n_parts),
                n_parts + 2,
                parts + [w_mlp, gu],
                [whole, shape((total, 2 * half_ff), LOW)] + reduced,
                [
                    h_scratch,
                    pltpu.VMEM((width, mlp_cols), LOW),
                    pltpu.VMEM((total, half_ff), F32),
                    pltpu.VMEM(gu.shape, LOW),
                    sems,
                ],
                mm(total, width, mlp_cols),
                n_any=n_parts,
                hbm_outs=1,
            )
            work = functools.partial(grads, cols=mlp_cols)
            if done is None:
                before = terms, work(h2, dm, dp2, z)
                terms, _, (last, g_mlp) = token_reduce(own, send, before=before)
                x_last = y_own
                for t in last:
                    x_last = x_last + t.astype(F32)
                x_last = x_last.astype(LOW)
            else:
                terms, g_mlp, _ = token_reduce(own, send, (work, (h2, dm, dp2, z)))
            g_mlp = scatter(g_mlp)
            dy, low, small_two = norm_back(dx, y_own, gains[2, l], terms)
            parts = token_gather(low)
            if done is not None:
                sums = put_mlp(l + 1, pick(done[1])), put_attn(l + 1, pick(done[0]))
                parts, (mlp_sum, attn_sum) = lax.optimization_barrier((parts, sums))
            da, dp1, bias_grad, own, send = call(
                functools.partial(attn_backward, n_parts, heads),
                n_parts + 6,
                parts + w_attn + [q, k, v] + geometry,
                [whole, shape((total, 3 * half_in), LOW), shape((1, 3 * half_in), F32)] + reduced,
                [
                    h_scratch,
                    pltpu.VMEM((width, attn_cols), LOW),
                    pltpu.VMEM((total, half_in), F32),
                    pltpu.VMEM((3, total, half_in), LOW),
                ]
                + geometry_scratch
                + [sems],
                mm(total, width, attn_cols) + 5 * mm(heads, total, total, half_in),
                n_any=n_parts,
                hbm_outs=1,
                limit=56,
            )
            work = functools.partial(grads, cols=attn_cols)
            if done is None:
                terms, g_attn, _ = token_reduce(own, send, (work, (h1, da, dp1, o)))
                done = (scatter(g_attn), g_mlp)
            else:
                terms, g_attn, _ = token_reduce(own, send, (work, (h1, da, dp1, o)))
            dx, low, small_one = norm_back(dy, x_own, gains[0, l], terms)
            small_out[l] = (small_one, small_two, bias_grad)
        norms = jnp.concatenate([part for l in range(LAYERS) for part in small_out[l][:2]], axis=0)
        bias = jnp.concatenate([small_out[l][2] for l in range(LAYERS)], axis=1)
        rows = -(-bias.size // width)
        bias = jnp.pad(bias, ((0, 0), (0, rows * width - bias.size))).reshape(rows, width)
        parts = mp_gather(jnp.concatenate([low, norms.astype(LOW)], axis=0))
        norms = sum(part[sub:].astype(F32) for part in parts)
        both = jnp.concatenate([norms, bias], axis=0).astype(LOW)
        mine, moved = chi_swap(by_place([part[:sub] for part in parts]), block, both)
        g_mlp, x_last = after((g_mlp, x_last), parts[n_mp // 2])
        g_gu, g_down = put_mlp(0, pick(g_mlp), mlp_sum)
        x_parts = after(mp_gather(x_last), g_gu)
        held = by_place(x_parts)
        x_mine, x_moved = chi_swap(held, block)
        g_gu = jnp.swapaxes(after(g_gu, held), 1, 2)
        g_gu = with_layout_constraint(g_gu, Layout(major_to_minor=(0, 1, 2, 3)))
        moved = after(moved, g_gu)
        tokens_grad = to_blocks(mine, moved, block).astype(F32)
        both = both.astype(F32) + moved[block:].astype(F32)
        activations = to_blocks(x_mine, x_moved, block)
        for name, bit in group_bits[1:]:
            both = both + swap(both, name, bit)
        other = swap(both, "clo", 1)
        norms = (both + other)[: 4 * LAYERS].reshape(LAYERS, 4, width)
        mine, others = (
            x[4 * LAYERS :].reshape(-1)[: LAYERS * 3 * half_in].reshape(LAYERS, 3, half_in)
            for x in (both, other)
        )
        low, high = jnp.where(clo == 0, mine, others), jnp.where(clo == 0, others, mine)
        bias = jnp.concatenate([low, high], axis=2)
        norms = [norms[:, i] for i in range(4)]
        g_attn = after(scatter(g_attn), (tokens_grad, activations, g_gu, norms, bias))
        g_qkv, g_out = put_attn(0, pick(g_attn), attn_sum)
        g_qkv = jnp.swapaxes(g_qkv, 1, 2)

        return (
            activations, tokens_grad, norms[0], norms[1],
            g_qkv, bias, g_out, norms[2], norms[3], g_gu, g_down,
        )

    return on_device


def solution(mesh):
    n_dp, n_ctx, n_mp = (mesh.shape[a] for a in ("dp", "ctx", "mp"))
    n_clo = 2
    n_chi = n_ctx // n_clo
    fine = Mesh(mesh.devices.reshape(n_dp, n_chi, n_clo, n_mp), ("dp", "chi", "clo", "mp"))
    rows = ("dp", "chi", "clo")
    ctx = ("chi", "clo")
    token_spec = P("dp", ctx, None)
    four, three = P(None, rows, None, "mp"), P(None, rows, "mp")
    bias_spec = P(None, None, "mp")
    return jax.shard_map(
        make_program(n_dp, n_chi, n_clo, n_mp),
        mesh=fine,
        in_specs=(
            token_spec, P("dp", ctx), token_spec, P(), P(), four, bias_spec, three, P(), P(),
            four, three,
        ),
        out_specs=(
            token_spec, token_spec, P(), P(), four, bias_spec, three, P(), P(), four, three,
        ),
        check_vma=False,
    )
```

```python
import functools
import math

import jax
import jax.numpy as jnp
from jax import lax
from jax.experimental import pallas as pl
from jax.experimental.layout import Layout, with_layout_constraint
from jax.experimental.pallas import tpu as pltpu
from jax.sharding import Mesh
from jax.sharding import PartitionSpec as P

HEAD = 64
ROT = 16
LAYERS = 2
NORM_EPS = 1e-05
MASK_FILL = -1e30
LOW = jnp.bfloat16
F32 = jnp.float32
MIB = 1024 * 1024
BLOCK = 512
HBM = pl.BlockSpec(memory_space=pltpu.HBM)
ANY = pl.BlockSpec(memory_space=pl.ANY)
VMEM = pl.BlockSpec(memory_space=pltpu.VMEM)


def dot(a, b, dims):
    return lax.dot_general(a, b, (dims, ((), ())), preferred_element_type=F32)


def nn(a, b):
    return dot(a, b, ((1,), (0,)))


def nt(a, b):
    return dot(a, b, ((1,), (1,)))


def tn(a, b):
    return dot(a, b, ((0,), (0,)))


def shape(dims, kind):
    return jax.ShapeDtypeStruct(dims, kind)


def call(body, n_hbm, args, outs, scratch, flops, hbm_outs=0, n_any=0, limit=32, aliases=None):
    moved = sum(a.size * a.dtype.itemsize for a in args)
    moved += sum(math.prod(o.shape) * jnp.dtype(o.dtype).itemsize for o in outs)
    return pl.pallas_call(
        body,
        out_shape=tuple(outs),
        in_specs=[ANY] * n_any + [HBM] * (n_hbm - n_any) + [VMEM] * (len(args) - n_hbm),
        out_specs=tuple([HBM] * hbm_outs + [VMEM] * (len(outs) - hbm_outs)),
        scratch_shapes=scratch,
        input_output_aliases=aliases or {},
        compiler_params=pltpu.CompilerParams(vmem_limit_bytes=limit * MIB),
        cost_estimate=pl.CostEstimate(flops=flops, bytes_accessed=moved, transcendentals=0),
    )(*args)


def into_rows(pieces, whole, sems, first):
    copies, row = [], 0
    for i, piece in enumerate(pieces):
        rows = piece.shape[0]
        copies.append(
            pltpu.make_async_copy(piece, whole.at[pl.ds(row, rows)], sems.at[first + i])
        )
        row += rows
    return copies


def weights_into(weights, whole, sems, first):
    rows, width = whole.shape
    cols = pl.ds(pl.multiple_of(lax.axis_index("clo") * width, 128), width)
    copies = []
    for at in range(0, rows, BLOCK):
        src, dst = weights.at[pl.ds(at, BLOCK), cols], whole.at[pl.ds(at, BLOCK)]
        copies.append(pltpu.make_async_copy(src, dst, sems.at[first + len(copies)]))
    return copies


def start_all(copies):
    for c in copies:
        c.start()


def wait_all(copies):
    for c in copies:
        c.wait()


def rolled(value, tables, sign):
    cos_t, ahead_t, behind_t = tables[0], tables[1], tables[2]
    slabs = []
    for at in range(0, value.shape[1], 128):
        x = value[:, at : at + 128]
        ahead = pltpu.roll(x, 128 - ROT // 2, 1)
        behind = pltpu.roll(x, ROT // 2, 1)
        slabs.append(x * cos_t + sign * (ahead * ahead_t + behind * behind_t))
    return jnp.concatenate(slabs, axis=1).astype(LOW)


def allowed_of(column, row):
    return (column[:, 0:1] == row[0:1]) & (row[1:2] <= column[:, 1:2])


def put_halves(tile, cols, own_ref, send_ref):
    half = own_ref.shape[0]
    own_ref[:, cols] = tile[:half].astype(LOW)
    send_ref[:, cols] = tile[half:].astype(LOW)


def softmax_of(q_h, k, allowed, scale):
    s = jnp.where(allowed, nt(q_h * scale, k), MASK_FILL)
    top = jnp.max(s, axis=-1, keepdims=True)
    e = jnp.exp(s - top)
    return e * (1.0 / jnp.sum(e, axis=-1, keepdims=True))


def load(pairs, sems, first):
    return [
        pltpu.make_async_copy(src, dst, sems.at[first + i]) for i, (src, dst) in enumerate(pairs)
    ]


def block_rows(w_s, w_copies=None):
    for i, at in enumerate(range(0, w_s.shape[0], BLOCK)):
        if w_copies is not None:
            w_copies[i].wait()
        yield i, slice(at, at + BLOCK)


def attn_forward(n_h, heads, *refs):
    h_parts, weights, refs = refs[:n_h], refs[n_h], refs[n_h + 1 :]
    tables, column, row, bias = refs[:4]
    full_o, q_o, k_o, v_o, o_o, own_o, send_o, h_s, w_s, acc, tab, col, sems = refs[4:]
    width = heads * HEAD
    copies = into_rows(h_parts, h_s, sems, 0)
    w_copies = weights_into(weights, w_s, sems, n_h)
    extra = load([(tables, tab), (column, col)], sems, n_h + len(w_copies))
    start_all(copies + w_copies + extra)
    wait_all(copies)
    whole = pltpu.make_async_copy(h_s, full_o, sems.at[0])
    whole.start()
    for r, rows in block_rows(w_s, w_copies):
        for c in range(3):
            cols = slice(c * width, (c + 1) * width)
            part = nn(h_s[:, rows], w_s[rows, cols])
            acc[:, cols] = part + (bias[:, cols] if r == 0 else acc[:, cols])
    wait_all(extra)
    q_o[...] = rolled(acc[:, :width], tab, 1.0)
    k_o[...] = rolled(acc[:, width : 2 * width], tab, 1.0)
    v_o[...] = acc[:, 2 * width :].astype(LOW)
    lane = lax.broadcasted_iota(jnp.int32, (1, width), 1) // HEAD
    allowed = allowed_of(col, row)
    k, v, q = k_o[...], v_o[...], q_o[...]
    zero = jnp.zeros((), LOW)
    o = None
    for h in range(heads):
        mine = lane == h
        w = softmax_of(jnp.where(mine, q, zero), k, allowed, LOW(1.0 / math.sqrt(HEAD)))
        part = nn(w.astype(LOW), jnp.where(mine, v, zero))
        o = part if o is None else o + part
    o_o[...] = o.astype(LOW)
    o = o_o[...]
    for r, rows in block_rows(w_s):
        put_halves(nt(o, w_s[rows, 3 * width :]), rows, own_o, send_o)
    whole.wait()


def attn_backward(n_h, heads, *refs):
    d_parts, weights, refs = refs[:n_h], refs[n_h], refs[n_h + 1 :]
    q_i, k_i, v_i, tables, column, row = refs[:6]
    full_o, dp_o, bias_o, own_o, send_o, d_s, w_s, acc, qkv, tab, col, sems = refs[6:]
    width = heads * HEAD
    copies = into_rows(d_parts, d_s, sems, 0)
    w_copies = weights_into(weights, w_s, sems, n_h)
    extra = load(
        [(q_i, qkv.at[0]), (k_i, qkv.at[1]), (v_i, qkv.at[2]), (tables, tab), (column, col)],
        sems,
        n_h + len(w_copies),
    )
    start_all(copies + w_copies + extra)
    wait_all(copies)
    whole = pltpu.make_async_copy(d_s, full_o, sems.at[0])
    whole.start()
    for r, rows in block_rows(w_s, w_copies):
        part = nn(d_s[:, rows], w_s[rows, 3 * width :])
        acc[...] = part if r == 0 else acc[...] + part
    do = acc[...].astype(LOW)
    wait_all(extra)
    q, k, v = qkv[0], qkv[1], qkv[2]
    lane = lax.broadcasted_iota(jnp.int32, (1, width), 1) // HEAD
    allowed = allowed_of(col, row)
    zero = jnp.zeros((), LOW)
    scale = 1.0 / math.sqrt(HEAD)
    dq = dk = dv = None
    for h in range(heads):
        mine = lane == h
        q_h = jnp.where(mine, q, zero)
        do_h = jnp.where(mine, do, zero)
        w = softmax_of(q_h, k, allowed, LOW(scale))
        dw = nt(do_h, v)
        ds = (w * (dw - jnp.sum(w * dw, axis=-1, keepdims=True))).astype(LOW)
        dv_h = tn(w.astype(LOW), do_h)
        dq_h = nn(ds, jnp.where(mine, k, zero))
        dk_h = tn(ds, q_h)
        dq, dk, dv = (
            (dq_h, dk_h, dv_h) if h == 0 else (dq + dq_h, dk + dk_h, dv + dv_h)
        )
    dp_o[:, :width] = rolled(dq * scale, tab, -1.0)
    dp_o[:, width : 2 * width] = rolled(dk * scale, tab, -1.0)
    dp_o[:, 2 * width :] = dv.astype(LOW)
    dp = dp_o[...]
    bias_o[...] = jnp.sum(dp.astype(F32), axis=0, keepdims=True)
    for r, rows in block_rows(w_s):
        put_halves(nt(dp, w_s[rows, : 3 * width]), rows, own_o, send_o)
    whole.wait()


def mlp_forward(n_h, *refs):
    h_parts, weights, refs = refs[:n_h], refs[n_h], refs[n_h + 1 :]
    full_o, gu_o, z_o, own_o, send_o, h_s, w_s, acc, sems = refs
    units = z_o.shape[1]
    copies = into_rows(h_parts, h_s, sems, 0)
    w_copies = weights_into(weights, w_s, sems, n_h)
    start_all(copies + w_copies)
    wait_all(copies)
    whole = pltpu.make_async_copy(h_s, full_o, sems.at[0])
    whole.start()
    for r, rows in block_rows(w_s, w_copies):
        part = nn(h_s[:, rows], w_s[rows, : 2 * units])
        acc[...] = part if r == 0 else acc[...] + part
    gu_o[...] = acc[...].astype(LOW)
    g = acc[:, :units]
    u = acc[:, units:]
    z_o[...] = (g * u / (1.0 + jnp.exp(-g))).astype(LOW)
    z = z_o[...]
    for r, rows in block_rows(w_s):
        put_halves(nt(z, w_s[rows, 2 * units : 3 * units]), rows, own_o, send_o)
    whole.wait()


def mlp_backward(n_h, *refs):
    d_parts, weights, refs = refs[:n_h], refs[n_h], refs[n_h + 1 :]
    gu_i, full_o, dp_o, own_o, send_o, d_s, w_s, acc, gu, sems = refs
    units = acc.shape[1]
    copies = into_rows(d_parts, d_s, sems, 0)
    w_copies = weights_into(weights, w_s, sems, n_h)
    extra = load([(gu_i, gu)], sems, n_h + len(w_copies))
    start_all(copies + w_copies + extra)
    wait_all(copies)
    whole = pltpu.make_async_copy(d_s, full_o, sems.at[0])
    whole.start()
    for r, rows in block_rows(w_s, w_copies):
        part = nn(d_s[:, rows], w_s[rows, 2 * units : 3 * units])
        acc[...] = part if r == 0 else acc[...] + part
    wait_all(extra)
    g = gu[:, :units].astype(F32)
    u = gu[:, units:].astype(F32)
    sig = 1.0 / (1.0 + jnp.exp(-g))
    dz = acc[...]
    dp_o[:, :units] = (dz * u * sig * (1.0 + g * (1.0 - sig))).astype(LOW)
    dp_o[:, units:] = (dz * g * sig).astype(LOW)
    dp = dp_o[...]
    for r, rows in block_rows(w_s):
        put_halves(nt(dp, w_s[rows, : 2 * units]), rows, own_o, send_o)
    whole.wait()


def load_grads(args, a_s, b_s, da_s, db_s, sems):
    copies = load(list(zip(args, (a_s, b_s, da_s, db_s))), sems, 0)
    start_all(copies)
    wait_all(copies)


def weight_grads(*refs):
    out, a_s, b_s, da_s, db_s, slots, sems, out_sems = refs[4:]
    load_grads(refs[:4], a_s, b_s, da_s, db_s, sems)
    split, end = da_s.shape[1], da_s.shape[1] + db_s.shape[1]
    sent = []
    for i, at in enumerate(range(0, a_s.shape[1], BLOCK)):
        cols = slice(at, at + BLOCK)
        slot = slots.at[i % 2]
        if i >= 2:
            sent[i - 2].wait()
        slot[:, :split] = tn(a_s[:, cols], da_s[...]).astype(LOW)
        slot[:, split:end] = tn(b_s[:, cols], db_s[...]).astype(LOW)
        if end < slot.shape[1]:
            slot[:, end:] = jnp.zeros((BLOCK, slot.shape[1] - end), LOW)
        sent.append(pltpu.make_async_copy(slot, out.at[pl.ds(at, BLOCK)], out_sems.at[i]))
        sent[i].start()
    wait_all(sent[-2:])


def other_rows(block_sum, out, sem):
    rows = out.shape[0]
    at = (1 - lax.axis_index("clo")) * rows
    copy = pltpu.make_async_copy(
        block_sum.at[pl.ds(pl.multiple_of(at, rows), rows)], out, sem.at[0]
    )
    copy.start()
    copy.wait()


def put_grads(layer, n_old, n_first, *refs):
    block_sum, moved = refs[:2]
    first_o, second_o, mine_s, moved_s, first_s, second_s, sems = refs[2 + n_old :]
    rows = moved.shape[0]
    me = lax.axis_index("clo")
    own = block_sum
    if own.shape[0] > rows:
        own = own.at[pl.ds(pl.multiple_of(me * rows, rows), rows)]
    copies = load([(own, mine_s), (moved, moved_s)], sems, 0)
    start_all(copies)
    wait_all(copies)
    low = jnp.where(me == 0, mine_s[...], moved_s[...])
    high = jnp.where(me == 0, moved_s[...], mine_s[...])
    width = second_s.shape[1] // 2
    out = load([(first_s, first_o.at[layer]), (second_s, second_o.at[layer])], sems, 2)
    for core, part in enumerate((low, high)):
        to = slice(core * width, (core + 1) * width)
        for c in range(n_first):
            first_s[c, :, to] = part[:, c * width : (c + 1) * width].astype(F32)
        second_s[:, to] = part[:, n_first * width : (n_first + 1) * width].astype(F32)
    start_all(out)
    wait_all(out)


def order_columns(*refs):
    qkv, out, both, sems = refs
    width = both.shape[1] // 8
    copies = []
    for core in range(2):
        cols = pl.ds(core * width, width)
        for c in range(4):
            src = out.at[:, cols] if c == 3 else qkv.at[c, :, cols]
            dst = both.at[:, pl.ds((4 * core + c) * width, width)]
            copies.append(pltpu.make_async_copy(src, dst, sems.at[len(copies)]))
    start_all(copies)
    wait_all(copies)


def middle(own_i, moved_i, own_o, *sends):
    rows = own_o.shape[0]
    own_o[...] = own_i[:rows].astype(F32) + moved_i[:rows].astype(F32)
    for r, send in enumerate(sends):
        at = slice((r + 1) * rows, (r + 2) * rows)
        send[...] = (own_i[at].astype(F32) + moved_i[at].astype(F32)).astype(LOW)


def norm_of(value):
    center = value - jnp.mean(value, axis=-1, keepdims=True)
    inverse = lax.rsqrt(jnp.mean(center * center, axis=-1, keepdims=True) + NORM_EPS)
    return center * inverse, inverse


def norm_forward(x_i, gain, offset, *refs):
    terms, (x_o, h_o) = refs[:-2], refs[-2:]
    x = x_i[...]
    for t in terms:
        x = x + t[...].astype(F32)
    x_o[...] = x
    h_o[...] = (norm_of(x)[0] * gain[...] + offset[...]).astype(LOW)


def norm_backward(dx_i, y_i, gain, *refs):
    terms, (dy_o, low_o, small_o) = refs[:-3], refs[-3:]
    dh = terms[0][...]
    for t in terms[1:]:
        dh = dh + t[...].astype(F32)
    n, inverse = norm_of(y_i[...])
    small_o[0:1] = jnp.sum(dh * n, axis=0, keepdims=True)
    small_o[1:2] = jnp.sum(dh, axis=0, keepdims=True)
    scaled = dh * gain[...]
    dy = dx_i[...] + inverse * (
        scaled
        - jnp.mean(scaled, axis=-1, keepdims=True)
        - n * jnp.mean(scaled * n, axis=-1, keepdims=True)
    )
    dy_o[...] = dy
    low_o[...] = dy.astype(LOW)


def after(value, event):
    return lax.optimization_barrier((value, event))[0]


def log2(n):
    return n.bit_length() - 1


def reverse_bits(r, bits):
    return sum(((r >> k) & 1) << (bits - 1 - k) for k in range(bits))


def make_program(n_dp, n_chi, n_clo, n_mp):
    group_bits = [("chi", 1 << k) for k in range(log2(n_chi))]
    group_bits += [("dp", 1 << k) for k in range(log2(n_dp))]
    n_groups = n_dp * n_chi
    sizes = {"dp": n_dp, "chi": n_chi, "clo": n_clo, "mp": n_mp}

    def swap(value, axis, bit):
        return lax.ppermute(value, axis, [(i, i ^ bit) for i in range(sizes[axis])])

    def mp_gather(own):
        parts = [own]
        for k in reversed(range(log2(n_mp))):
            parts = parts + [swap(part, "mp", 1 << k) for part in parts]
        return [parts[reverse_bits(r, log2(n_mp))] for r in range(n_mp)]

    def token_gather(own):
        half = mp_gather(own)
        return half + [swap(part, "clo", 1) for part in half]

    def token_reduce(own_half, send_half, beside=None, before=None):
        rows, width = own_half.shape
        sub = rows // n_mp
        if before is not None:
            send_half, before = lax.optimization_barrier((send_half, before))
        moved = swap(send_half, "clo", 1)
        outs = [shape((sub, width), F32)] + [shape((sub, width), LOW)] * (n_mp - 1)
        parts = call(middle, 0, [own_half, moved], outs, [], rows * width)
        terms = [parts[0]] + [swap(parts[r], "mp", r) for r in range(1, n_mp)]
        result = None
        if beside is not None:
            work, args = beside
            terms, result = lax.optimization_barrier((terms, work(*after(args, parts[0]))))
        return terms, result, before

    def own_tokens(value):
        seqs, block, width = value.shape
        sub = block * n_chi // n_mp
        per_block = block // sub
        place = lax.axis_index("mp") % per_block
        mine = lax.dynamic_slice_in_dim(value, place * sub, sub, 1)
        chi = lax.axis_index("chi")
        here = lax.dynamic_index_in_dim(mine, chi, 0, keepdims=False)
        there = swap(lax.dynamic_index_in_dim(mine, 1 - chi, 0, keepdims=False), "chi", 1)
        return jnp.where(lax.axis_index("mp") // per_block == chi, here, there)

    def chi_swap(held, block, extra=None):
        chi = lax.axis_index("chi")
        mine = lax.dynamic_slice_in_dim(held, chi * block, block, 0)
        sent = lax.dynamic_slice_in_dim(held, (1 - chi) * block, block, 0)
        if extra is not None:
            sent = jnp.concatenate([sent, extra], axis=0)
        return mine, swap(sent, "chi", 1)

    def to_blocks(mine, moved, block):
        first = lax.axis_index("chi") == 0
        moved = moved[:block]
        return jnp.where(first, jnp.stack([mine, moved]), jnp.stack([moved, mine]))

    def by_place(parts):
        sub, width = parts[0].shape
        mp = lax.axis_index("mp")
        parts = jnp.stack(parts)
        for k in range(log2(n_mp)):
            pairs = parts.reshape(n_mp >> (k + 1), 2, 1 << k, sub, width)
            pairs = jnp.where((mp >> k) % 2 == 1, jnp.flip(pairs, 1), pairs)
            parts = pairs.reshape(n_mp, sub, width)
        return parts.reshape(n_mp * sub, width)

    def on_device(
        tokens, segments, cotangent, first_gain, first_bias, qkv_weight, qkv_bias,
        out_weight, second_gain, second_bias, gate_up_weight, down_weight,
    ):
        n_seq, block, width = tokens.shape
        rows_dev = qkv_weight.shape[1]
        half_in = qkv_weight.shape[3] // 2
        half_ff = down_weight.shape[2] // 2
        heads = half_in // HEAD
        total = block * n_chi * n_clo
        half_total = total // n_clo
        sub = half_total // n_mp
        n_parts = n_clo * n_mp
        mp, clo, chi = (lax.axis_index(a) for a in ("mp", "clo", "chi"))
        x_own = own_tokens(tokens).astype(F32)

        pad = -(3 * half_ff) % 128
        attn_cols, mlp_cols = 4 * half_in, 3 * half_ff + pad

        def attn_columns(l):
            view = jnp.transpose(qkv_weight[l], (1, 0, 2))
            outs = [shape((rows_dev, 2 * attn_cols), LOW)]
            args = [view, out_weight[l]]
            sems = [pltpu.SemaphoreType.DMA((8,))]
            return call(order_columns, 2, args, outs, sems, 0, hbm_outs=1)

        def mlp_columns(l):
            gu, down = jnp.transpose(gate_up_weight[l], (1, 0, 2)), down_weight[l]
            fill = jnp.zeros((rows_dev, pad), LOW)
            parts = []
            for cols in (slice(None, half_ff), slice(half_ff, None)):
                parts += [gu[0, :, cols], gu[1, :, cols], down[:, cols], fill]
            return jnp.concatenate(parts, axis=1)

        def gather_weights(own):
            return lax.all_gather(own, ("dp", "chi", "clo"), axis=0, tiled=True)

        weights = []
        for l in range(LAYERS):
            attn = [gather_weights(attn_columns(l)[0])]
            weights.append([attn, gather_weights(mlp_columns(l))])
        dx = own_tokens(cotangent)
        gains = jnp.stack([first_gain, first_bias, second_gain, second_bias])
        half_bias = jnp.where(clo == 1, qkv_bias[:, :, half_in:], qkv_bias[:, :, :half_in])
        half_bias = half_bias.reshape(LAYERS, 1, 3 * half_in)

        there = swap(lax.dynamic_index_in_dim(segments, 1 - chi, 0, keepdims=False), "chi", 1)
        here = lax.dynamic_index_in_dim(segments, chi, 0, keepdims=False)
        pair = jnp.stack([jnp.where(chi == 0, here, there), jnp.where(chi == 0, there, here)])
        other = swap(pair, "clo", 1)
        whole = jnp.stack(
            [jnp.where(clo == 0, pair, other), jnp.where(clo == 0, other, pair)], axis=1
        ).reshape(total)
        core_of = jnp.arange(n_clo, dtype=jnp.int32) ^ clo
        mp_of = jnp.arange(n_mp, dtype=jnp.int32) ^ mp
        per_block = block // sub
        place = (
            (mp_of // per_block * (n_clo * block) + mp_of % per_block * sub)[None, :, None]
            + (core_of * block)[:, None, None]
            + jnp.arange(sub, dtype=jnp.int32)[None, None, :]
        ).reshape(total)
        match = place[:, None] == jnp.arange(total, dtype=jnp.int32)[None, :]
        seg = jnp.sum(jnp.where(match, whole[None, :], 0), axis=1)
        starts = jnp.sum((seg[None, :] < seg[:, None]).astype(jnp.int32), axis=1)
        freq = jnp.exp(
            jnp.arange(ROT // 2, dtype=F32) * (-2.0 * math.log(10000.0) / ROT)
        )
        angles = freq[:, None] * (place - starts).astype(F32)[None, :]
        cos_t, sin_t = jnp.cos(angles).T, jnp.sin(angles).T
        zeros = jnp.zeros((total, ROT // 2), F32)
        tail = jnp.zeros((total, HEAD - ROT), F32)
        per_slab = 128 // HEAD
        tables = jnp.stack(
            [
                jnp.tile(jnp.concatenate(parts, axis=1), (1, per_slab))
                for parts in (
                    (cos_t, cos_t, tail + 1.0),
                    (-sin_t, zeros, tail),
                    (zeros, sin_t, tail),
                )
            ]
        )
        row = jnp.stack([seg, place])
        geometry = [tables, row.T, row]
        geometry_scratch = [
            pltpu.VMEM((3, total, 128), F32),
            pltpu.VMEM((total, 2), jnp.int32),
        ]

        act = shape((total, half_in), LOW)
        reduced = [shape((half_total, width), LOW)] * 2
        sems = pltpu.SemaphoreType.DMA((n_parts + width // BLOCK + 5,))
        h_scratch = pltpu.VMEM((total, width), LOW)

        def mm(*dims):
            return 2 * math.prod(dims)

        def norm(x, gain, offset, terms):
            outs = [shape(x.shape, F32), shape(x.shape, LOW)]
            return call(norm_forward, 0, [x, gain[None], offset[None]] + terms, outs, [], 10 * x.size)

        def norm_back(dx, y, gain, terms):
            outs = [shape(y.shape, F32), shape(y.shape, LOW), shape((2, width), F32)]
            return call(norm_backward, 0, [dx, y, gain[None]] + terms, outs, [], 20 * y.size)

        def grads(a, b, da, db, cols):
            scratch = [pltpu.VMEM(x.shape, LOW) for x in (a, b, da, db)]
            scratch += [pltpu.VMEM((2, BLOCK, cols), LOW), pltpu.SemaphoreType.DMA((4,))]
            scratch += [pltpu.SemaphoreType.DMA((width // BLOCK,))]
            outs = [shape((width, cols), LOW)]
            flops = mm(total, width, cols)
            args = [a, b, da, db]
            return call(weight_grads, 4, args, outs, scratch, flops, hbm_outs=1, limit=60)

        def scatter(partial):
            return lax.psum_scatter(partial[0], ("dp", "chi"), scatter_dimension=0, tiled=True)

        def pick(block_sum):
            outs = [shape((rows_dev, block_sum.shape[1]), LOW)]
            sems = [pltpu.SemaphoreType.DMA((1,))]
            others = call(other_rows, 1, [block_sum], outs, sems, 0, hbm_outs=1)[0]
            return block_sum, swap(others, "clo", 1)

        def put(l, sums, n_first, unit, old):
            sums, moved = sums
            first, second = (n_first, rows_dev, 2 * unit), (rows_dev, 2 * unit)
            piece = pltpu.VMEM(moved.shape, LOW)
            return call(
                functools.partial(put_grads, l, len(old), n_first),
                2 + len(old),
                [sums, moved] + old,
                [shape((LAYERS,) + first, F32), shape((LAYERS,) + second, F32)],
                [
                    piece,
                    piece,
                    pltpu.VMEM(first, F32),
                    pltpu.VMEM(second, F32),
                    pltpu.SemaphoreType.DMA((4,)),
                ],
                0,
                hbm_outs=2,
                limit=60,
                aliases={2: 0, 3: 1} if old else None,
            )

        def put_attn(l, sums, old=()):
            return list(put(l, sums, 3, half_in, list(old)))

        def put_mlp(l, sums, old=()):
            return list(put(l, sums, 2, half_ff, list(old)))

        whole = shape((total, width), LOW)
        saved = []
        terms = []
        for l in range(LAYERS):
            w_attn, w_mlp = weights[l]
            x_own, h = norm(x_own, gains[0, l], gains[1, l], terms)
            h1 = token_gather(h)
            h1, q, k, v, o, own, send = call(
                functools.partial(attn_forward, n_parts, heads),
                n_parts + 3,
                h1 + w_attn + geometry + [half_bias[l]],
                [whole] + [act] * 4 + reduced,
                [
                    h_scratch,
                    pltpu.VMEM((width, attn_cols), LOW),
                    pltpu.VMEM((total, 3 * half_in), F32),
                ]
                + geometry_scratch
                + [sems],
                mm(total, width, attn_cols) + 2 * mm(heads, total, total, 2 * half_in),
                n_any=n_parts,
                hbm_outs=1,
                limit=56,
            )
            y_own, h = norm(x_own, gains[2, l], gains[3, l], token_reduce(own, send)[0])
            h2 = token_gather(h)
            if l == 0:
                h2, dm_parts = lax.optimization_barrier((h2, token_gather(dx)))
            h2, gu, z, own, send = call(
                functools.partial(mlp_forward, n_parts),
                n_parts + 1,
                h2 + [w_mlp],
                [whole, shape((total, 2 * half_ff), LOW), shape((total, half_ff), LOW)] + reduced,
                [
                    h_scratch,
                    pltpu.VMEM((width, mlp_cols), LOW),
                    pltpu.VMEM((total, 2 * half_ff), F32),
                    sems,
                ],
                mm(total, width, mlp_cols),
                n_any=n_parts,
                hbm_outs=1,
            )
            saved.append((x_own, h1, q, k, v, o, y_own, h2, gu, z))
            x_own, terms = y_own, token_reduce(own, send)[0]

        dx = dx.astype(F32)
        small_out = [None] * LAYERS
        done = None
        for l in reversed(range(LAYERS)):
            w_attn, w_mlp = weights[l]
            x_own, h1, q, k, v, o, y_own, h2, gu, z = saved[l]
            parts = dm_parts if done is None else token_gather(low)
            if done is None:
                gu = after(gu, terms[0])
            dm, dp2, own, send = call(
                functools.partial(mlp_backward, n_parts),
                n_parts + 2,
                parts + [w_mlp, gu],
                [whole, shape((total, 2 * half_ff), LOW)] + reduced,
                [
                    h_scratch,
                    pltpu.VMEM((width, mlp_cols), LOW),
                    pltpu.VMEM((total, half_ff), F32),
                    pltpu.VMEM(gu.shape, LOW),
                    sems,
                ],
                mm(total, width, mlp_cols),
                n_any=n_parts,
                hbm_outs=1,
            )
            work = functools.partial(grads, cols=mlp_cols)
            if done is None:
                before = terms, work(h2, dm, dp2, z)
                terms, _, (last, g_mlp) = token_reduce(own, send, before=before)
                x_last = y_own
                for t in last:
                    x_last = x_last + t.astype(F32)
                x_last = x_last.astype(LOW)
            else:
                terms, g_mlp, _ = token_reduce(own, send, (work, (h2, dm, dp2, z)))
            g_mlp = scatter(g_mlp)
            dy, low, small_two = norm_back(dx, y_own, gains[2, l], terms)
            parts = token_gather(low)
            if done is not None:
                parts, picked = lax.optimization_barrier((parts, [pick(x) for x in done]))
            da, dp1, bias_grad, own, send = call(
                functools.partial(attn_backward, n_parts, heads),
                n_parts + 6,
                parts + w_attn + [q, k, v] + geometry,
                [whole, shape((total, 3 * half_in), LOW), shape((1, 3 * half_in), F32)] + reduced,
                [
                    h_scratch,
                    pltpu.VMEM((width, attn_cols), LOW),
                    pltpu.VMEM((total, half_in), F32),
                    pltpu.VMEM((3, total, half_in), LOW),
                ]
                + geometry_scratch
                + [sems],
                mm(total, width, attn_cols) + 5 * mm(heads, total, total, half_in),
                n_any=n_parts,
                hbm_outs=1,
                limit=56,
            )
            work = functools.partial(grads, cols=attn_cols)
            beside = work, (h1, da, dp1, o)
            if done is None:
                terms, g_attn, _ = token_reduce(own, send, beside)
                done = (scatter(g_attn), g_mlp)
            else:
                terms, g_attn, x_parts = token_reduce(own, send, beside, mp_gather(x_last))
                x_mine, x_moved = chi_swap(by_place(x_parts), block)
            dx, low, small_one = norm_back(dy, x_own, gains[0, l], terms)
            small_out[l] = (small_one, small_two, bias_grad)
        norms = jnp.concatenate([part for l in range(LAYERS) for part in small_out[l][:2]], axis=0)
        bias = jnp.concatenate([small_out[l][2] for l in range(LAYERS)], axis=1)
        rows = -(-bias.size // width)
        bias = jnp.pad(bias, ((0, 0), (0, rows * width - bias.size))).reshape(rows, width)
        parts = mp_gather(jnp.concatenate([low, norms.astype(LOW)], axis=0))
        sums = put_attn(LAYERS - 1, picked[0]), put_mlp(LAYERS - 1, picked[1])
        parts, sums, x_moved = lax.optimization_barrier((parts, sums, x_moved))
        attn_sum, mlp_sum = sums
        norms = sum(part[sub:].astype(F32) for part in parts)
        both = jnp.concatenate([norms, bias], axis=0).astype(LOW)
        mine, moved = chi_swap(by_place([part[:sub] for part in parts]), block, both)
        g_mlp = after(g_mlp, parts[n_mp // 2])
        g_gu, g_down = put_mlp(0, pick(g_mlp), mlp_sum)
        g_gu = jnp.swapaxes(g_gu, 1, 2)
        g_gu = with_layout_constraint(g_gu, Layout(major_to_minor=(0, 1, 2, 3)))
        moved = after(moved, g_gu)
        tokens_grad = to_blocks(mine, moved, block).astype(F32)
        both = both.astype(F32) + moved[block:].astype(F32)
        activations = to_blocks(x_mine, x_moved, block)
        for name, bit in group_bits[1:]:
            both = both + swap(both, name, bit)
        other = swap(both, "clo", 1)
        norms = (both + other)[: 4 * LAYERS].reshape(LAYERS, 4, width)
        mine, others = (
            x[4 * LAYERS :].reshape(-1)[: LAYERS * 3 * half_in].reshape(LAYERS, 3, half_in)
            for x in (both, other)
        )
        low, high = jnp.where(clo == 0, mine, others), jnp.where(clo == 0, others, mine)
        bias = jnp.concatenate([low, high], axis=2)
        norms = [norms[:, i] for i in range(4)]
        g_attn = after(scatter(g_attn), (tokens_grad, activations, g_gu, norms, bias))
        g_qkv, g_out = put_attn(0, pick(g_attn), attn_sum)
        g_qkv = jnp.swapaxes(g_qkv, 1, 2)

        return (
            activations, tokens_grad, norms[0], norms[1],
            g_qkv, bias, g_out, norms[2], norms[3], g_gu, g_down,
        )

    return on_device


def solution(mesh):
    n_dp, n_ctx, n_mp = (mesh.shape[a] for a in ("dp", "ctx", "mp"))
    n_clo = 2
    n_chi = n_ctx // n_clo
    fine = Mesh(mesh.devices.reshape(n_dp, n_chi, n_clo, n_mp), ("dp", "chi", "clo", "mp"))
    rows = ("dp", "chi", "clo")
    ctx = ("chi", "clo")
    token_spec = P("dp", ctx, None)
    four, three = P(None, rows, None, "mp"), P(None, rows, "mp")
    bias_spec = P(None, None, "mp")
    return jax.shard_map(
        make_program(n_dp, n_chi, n_clo, n_mp),
        mesh=fine,
        in_specs=(
            token_spec, P("dp", ctx), token_spec, P(), P(), four, bias_spec, three, P(), P(),
            four, three,
        ),
        out_specs=(
            token_spec, token_spec, P(), P(), four, bias_spec, three, P(), P(), four, three,
        ),
        check_vma=False,
    )
```

```python
import functools
import math

import jax
import jax.numpy as jnp
from jax import lax
from jax.experimental import pallas as pl
from jax.experimental.layout import Layout, with_layout_constraint
from jax.experimental.pallas import tpu as pltpu
from jax.sharding import Mesh
from jax.sharding import PartitionSpec as P

HEAD = 64
ROT = 16
LAYERS = 2
NORM_EPS = 1e-05
MASK_FILL = -1e30
LOW = jnp.bfloat16
F32 = jnp.float32
MIB = 1024 * 1024
BLOCK = 512
HBM = pl.BlockSpec(memory_space=pltpu.HBM)
ANY = pl.BlockSpec(memory_space=pl.ANY)
VMEM = pl.BlockSpec(memory_space=pltpu.VMEM)


def dot(a, b, dims):
    return lax.dot_general(a, b, (dims, ((), ())), preferred_element_type=F32)


def nn(a, b):
    return dot(a, b, ((1,), (0,)))


def nt(a, b):
    return dot(a, b, ((1,), (1,)))


def tn(a, b):
    return dot(a, b, ((0,), (0,)))


def shape(dims, kind):
    return jax.ShapeDtypeStruct(dims, kind)


def call(body, n_hbm, args, outs, scratch, flops, hbm_outs=0, n_any=0, limit=32, aliases=None):
    moved = sum(a.size * a.dtype.itemsize for a in args)
    moved += sum(math.prod(o.shape) * jnp.dtype(o.dtype).itemsize for o in outs)
    return pl.pallas_call(
        body,
        out_shape=tuple(outs),
        in_specs=[ANY] * n_any + [HBM] * (n_hbm - n_any) + [VMEM] * (len(args) - n_hbm),
        out_specs=tuple([HBM] * hbm_outs + [VMEM] * (len(outs) - hbm_outs)),
        scratch_shapes=scratch,
        input_output_aliases=aliases or {},
        compiler_params=pltpu.CompilerParams(vmem_limit_bytes=limit * MIB),
        cost_estimate=pl.CostEstimate(flops=flops, bytes_accessed=moved, transcendentals=0),
    )(*args)


def into_rows(pieces, whole, sems, first):
    copies, row = [], 0
    for i, piece in enumerate(pieces):
        rows = piece.shape[0]
        copies.append(
            pltpu.make_async_copy(piece, whole.at[pl.ds(row, rows)], sems.at[first + i])
        )
        row += rows
    return copies


def weights_into(weights, whole, sems, first):
    rows, width = whole.shape
    cols = pl.ds(pl.multiple_of(lax.axis_index("clo") * width, 128), width)
    copies = []
    for at in range(0, rows, BLOCK):
        src, dst = weights.at[pl.ds(at, BLOCK), cols], whole.at[pl.ds(at, BLOCK)]
        copies.append(pltpu.make_async_copy(src, dst, sems.at[first + len(copies)]))
    return copies


def shared_tile_into(weights, whole, sems, first):
    rows, width = whole.shape
    main = width - 128
    core = lax.axis_index("clo")
    own = pl.ds(pl.multiple_of(core * width, 128), main)
    copies = []
    for at in range(0, rows, BLOCK):
        block = pl.ds(at, BLOCK)
        for cols, to in ((own, pl.ds(0, main)), (pl.ds(main, 128), pl.ds(main, 128))):
            src, dst = weights.at[block, cols], whole.at[block, to]
            copies.append(pltpu.make_async_copy(src, dst, sems.at[first + len(copies)]))
    return copies


def settle_tile(whole, rows):
    tile = whole[rows, whole.shape[1] - 128 :].astype(F32)
    rolled_tile = pltpu.roll(tile, 64, 1)
    tile = jnp.where(lax.axis_index("clo") == 0, tile, rolled_tile)
    whole[rows, whole.shape[1] - 128 :] = tile.astype(LOW)


def start_all(copies):
    for c in copies:
        c.start()


def wait_all(copies):
    for c in copies:
        c.wait()


def rolled(value, tables, sign):
    cos_t, ahead_t, behind_t = tables[0], tables[1], tables[2]
    slabs = []
    for at in range(0, value.shape[1], 128):
        x = value[:, at : at + 128]
        ahead = pltpu.roll(x, 128 - ROT // 2, 1)
        behind = pltpu.roll(x, ROT // 2, 1)
        slabs.append(x * cos_t + sign * (ahead * ahead_t + behind * behind_t))
    return jnp.concatenate(slabs, axis=1).astype(LOW)


def allowed_of(column, row):
    return (column[:, 0:1] == row[0:1]) & (row[1:2] <= column[:, 1:2])


def put_halves(tile, cols, own_ref, send_ref):
    half = own_ref.shape[0]
    own_ref[:, cols] = tile[:half].astype(LOW)
    send_ref[:, cols] = tile[half:].astype(LOW)


def softmax_of(q_h, k, allowed, scale):
    s = jnp.where(allowed, nt(q_h * scale, k), MASK_FILL)
    top = jnp.max(s, axis=-1, keepdims=True)
    e = jnp.exp(s - top)
    return e * (1.0 / jnp.sum(e, axis=-1, keepdims=True))


def load(pairs, sems, first):
    return [
        pltpu.make_async_copy(src, dst, sems.at[first + i]) for i, (src, dst) in enumerate(pairs)
    ]


def block_rows(w_s, w_copies=None):
    for i, at in enumerate(range(0, w_s.shape[0], BLOCK)):
        if w_copies is not None:
            w_copies[i].wait()
        yield i, slice(at, at + BLOCK)


def attn_forward(n_h, heads, *refs):
    h_parts, weights, refs = refs[:n_h], refs[n_h], refs[n_h + 1 :]
    tables, column, row, bias = refs[:4]
    full_o, q_o, k_o, v_o, o_o, own_o, send_o, h_s, w_s, acc, tab, col, sems = refs[4:]
    width = heads * HEAD
    copies = into_rows(h_parts, h_s, sems, 0)
    w_copies = weights_into(weights, w_s, sems, n_h)
    extra = load([(tables, tab), (column, col)], sems, n_h + len(w_copies))
    start_all(copies + w_copies + extra)
    wait_all(copies)
    whole = pltpu.make_async_copy(h_s, full_o, sems.at[0])
    whole.start()
    for r, rows in block_rows(w_s, w_copies):
        for c in range(3):
            cols = slice(c * width, (c + 1) * width)
            part = nn(h_s[:, rows], w_s[rows, cols])
            acc[:, cols] = part + (bias[:, cols] if r == 0 else acc[:, cols])
    wait_all(extra)
    q_o[...] = rolled(acc[:, :width], tab, 1.0)
    k_o[...] = rolled(acc[:, width : 2 * width], tab, 1.0)
    v_o[...] = acc[:, 2 * width :].astype(LOW)
    lane = lax.broadcasted_iota(jnp.int32, (1, width), 1) // HEAD
    allowed = allowed_of(col, row)
    k, v, q = k_o[...], v_o[...], q_o[...]
    zero = jnp.zeros((), LOW)
    o = None
    for h in range(heads):
        mine = lane == h
        w = softmax_of(jnp.where(mine, q, zero), k, allowed, LOW(1.0 / math.sqrt(HEAD)))
        part = nn(w.astype(LOW), jnp.where(mine, v, zero))
        o = part if o is None else o + part
    o_o[...] = o.astype(LOW)
    o = o_o[...]
    for r, rows in block_rows(w_s):
        put_halves(nt(o, w_s[rows, 3 * width :]), rows, own_o, send_o)
    whole.wait()


def attn_backward(n_h, heads, *refs):
    d_parts, weights, refs = refs[:n_h], refs[n_h], refs[n_h + 1 :]
    q_i, k_i, v_i, tables, column, row = refs[:6]
    full_o, dp_o, bias_o, own_o, send_o, d_s, w_s, acc, qkv, tab, col, sems = refs[6:]
    width = heads * HEAD
    copies = into_rows(d_parts, d_s, sems, 0)
    w_copies = weights_into(weights, w_s, sems, n_h)
    extra = load(
        [(q_i, qkv.at[0]), (k_i, qkv.at[1]), (v_i, qkv.at[2]), (tables, tab), (column, col)],
        sems,
        n_h + len(w_copies),
    )
    start_all(copies + w_copies + extra)
    wait_all(copies)
    whole = pltpu.make_async_copy(d_s, full_o, sems.at[0])
    whole.start()
    for r, rows in block_rows(w_s, w_copies):
        part = nn(d_s[:, rows], w_s[rows, 3 * width :])
        acc[...] = part if r == 0 else acc[...] + part
    do = acc[...].astype(LOW)
    wait_all(extra)
    q, k, v = qkv[0], qkv[1], qkv[2]
    lane = lax.broadcasted_iota(jnp.int32, (1, width), 1) // HEAD
    allowed = allowed_of(col, row)
    zero = jnp.zeros((), LOW)
    scale = 1.0 / math.sqrt(HEAD)
    dq = dk = dv = None
    for h in range(heads):
        mine = lane == h
        q_h = jnp.where(mine, q, zero)
        do_h = jnp.where(mine, do, zero)
        w = softmax_of(q_h, k, allowed, LOW(scale))
        dw = nt(do_h, v)
        ds = (w * (dw - jnp.sum(w * dw, axis=-1, keepdims=True))).astype(LOW)
        dv_h = tn(w.astype(LOW), do_h)
        dq_h = nn(ds, jnp.where(mine, k, zero))
        dk_h = tn(ds, q_h)
        dq, dk, dv = (
            (dq_h, dk_h, dv_h) if h == 0 else (dq + dq_h, dk + dk_h, dv + dv_h)
        )
    dp_o[:, :width] = rolled(dq * scale, tab, -1.0)
    dp_o[:, width : 2 * width] = rolled(dk * scale, tab, -1.0)
    dp_o[:, 2 * width :] = dv.astype(LOW)
    dp = dp_o[...]
    bias_o[...] = jnp.sum(dp.astype(F32), axis=0, keepdims=True)
    for r, rows in block_rows(w_s):
        put_halves(nt(dp, w_s[rows, : 3 * width]), rows, own_o, send_o)
    whole.wait()


def mlp_forward(n_h, *refs):
    h_parts, weights, refs = refs[:n_h], refs[n_h], refs[n_h + 1 :]
    full_o, gu_o, z_o, own_o, send_o, h_s, w_s, acc, sems = refs
    units = z_o.shape[1]
    copies = into_rows(h_parts, h_s, sems, 0)
    w_copies = shared_tile_into(weights, w_s, sems, n_h)
    start_all(copies + w_copies)
    wait_all(copies)
    whole = pltpu.make_async_copy(h_s, full_o, sems.at[0])
    whole.start()
    for r, rows in block_rows(w_s):
        wait_all(w_copies[2 * r : 2 * r + 2])
        settle_tile(w_s, rows)
        part = nn(h_s[:, rows], w_s[rows, : 2 * units])
        acc[...] = part if r == 0 else acc[...] + part
    gu_o[...] = acc[...].astype(LOW)
    g = acc[:, :units]
    u = acc[:, units:]
    z_o[...] = (g * u / (1.0 + jnp.exp(-g))).astype(LOW)
    z = z_o[...]
    for r, rows in block_rows(w_s):
        put_halves(nt(z, w_s[rows, 2 * units : 3 * units]), rows, own_o, send_o)
    whole.wait()


def mlp_backward(n_h, *refs):
    d_parts, weights, refs = refs[:n_h], refs[n_h], refs[n_h + 1 :]
    gu_i, full_o, dp_o, own_o, send_o, d_s, w_s, acc, gu, sems = refs
    units = acc.shape[1]
    copies = into_rows(d_parts, d_s, sems, 0)
    w_copies = shared_tile_into(weights, w_s, sems, n_h)
    extra = load([(gu_i, gu)], sems, n_h + len(w_copies))
    start_all(copies + w_copies + extra)
    wait_all(copies)
    whole = pltpu.make_async_copy(d_s, full_o, sems.at[0])
    whole.start()
    for r, rows in block_rows(w_s):
        wait_all(w_copies[2 * r : 2 * r + 2])
        settle_tile(w_s, rows)
        part = nn(d_s[:, rows], w_s[rows, 2 * units : 3 * units])
        acc[...] = part if r == 0 else acc[...] + part
    wait_all(extra)
    g = gu[:, :units].astype(F32)
    u = gu[:, units:].astype(F32)
    sig = 1.0 / (1.0 + jnp.exp(-g))
    dz = acc[...]
    dp_o[:, :units] = (dz * u * sig * (1.0 + g * (1.0 - sig))).astype(LOW)
    dp_o[:, units:] = (dz * g * sig).astype(LOW)
    dp = dp_o[...]
    for r, rows in block_rows(w_s):
        put_halves(nt(dp, w_s[rows, : 2 * units]), rows, own_o, send_o)
    whole.wait()


def load_grads(args, a_s, b_s, da_s, db_s, sems):
    copies = load(list(zip(args, (a_s, b_s, da_s, db_s))), sems, 0)
    start_all(copies)
    wait_all(copies)


def weight_grads(*refs):
    out, a_s, b_s, da_s, db_s, slots, sems, out_sems = refs[4:]
    load_grads(refs[:4], a_s, b_s, da_s, db_s, sems)
    split, end = da_s.shape[1], da_s.shape[1] + db_s.shape[1]
    sent = []
    for i, at in enumerate(range(0, a_s.shape[1], BLOCK)):
        cols = slice(at, at + BLOCK)
        slot = slots.at[i % 2]
        if i >= 2:
            sent[i - 2].wait()
        slot[:, :split] = tn(a_s[:, cols], da_s[...]).astype(LOW)
        slot[:, split:end] = tn(b_s[:, cols], db_s[...]).astype(LOW)
        if end < slot.shape[1]:
            slot[:, end:] = jnp.zeros((BLOCK, slot.shape[1] - end), LOW)
        sent.append(pltpu.make_async_copy(slot, out.at[pl.ds(at, BLOCK)], out_sems.at[i]))
        sent[i].start()
    wait_all(sent[-2:])


def other_rows(block_sum, out, sem):
    rows = out.shape[0]
    at = (1 - lax.axis_index("clo")) * rows
    copy = pltpu.make_async_copy(
        block_sum.at[pl.ds(pl.multiple_of(at, rows), rows)], out, sem.at[0]
    )
    copy.start()
    copy.wait()


def put_grads(layer, n_old, n_first, *refs):
    block_sum, moved = refs[:2]
    first_o, second_o, mine_s, moved_s, first_s, second_s, sems = refs[2 + n_old :]
    rows = moved.shape[0]
    me = lax.axis_index("clo")
    own = block_sum
    if own.shape[0] > rows:
        own = own.at[pl.ds(pl.multiple_of(me * rows, rows), rows)]
    copies = load([(own, mine_s), (moved, moved_s)], sems, 0)
    start_all(copies)
    wait_all(copies)
    low = jnp.where(me == 0, mine_s[...], moved_s[...])
    high = jnp.where(me == 0, moved_s[...], mine_s[...])
    width = second_s.shape[1] // 2
    out = load([(first_s, first_o.at[layer]), (second_s, second_o.at[layer])], sems, 2)
    for core, part in enumerate((low, high)):
        to = slice(core * width, (core + 1) * width)
        for c in range(n_first):
            first_s[c, :, to] = part[:, c * width : (c + 1) * width].astype(F32)
        second_s[:, to] = part[:, n_first * width : (n_first + 1) * width].astype(F32)
    start_all(out)
    wait_all(out)


def order_columns(*refs):
    qkv, out, both, sems = refs
    width = both.shape[1] // 8
    copies = []
    for core in range(2):
        cols = pl.ds(core * width, width)
        for c in range(4):
            src = out.at[:, cols] if c == 3 else qkv.at[c, :, cols]
            dst = both.at[:, pl.ds((4 * core + c) * width, width)]
            copies.append(pltpu.make_async_copy(src, dst, sems.at[len(copies)]))
    start_all(copies)
    wait_all(copies)


def middle(own_i, moved_i, own_o, *sends):
    rows = own_o.shape[0]
    own_o[...] = own_i[:rows].astype(F32) + moved_i[:rows].astype(F32)
    for r, send in enumerate(sends):
        at = slice((r + 1) * rows, (r + 2) * rows)
        send[...] = (own_i[at].astype(F32) + moved_i[at].astype(F32)).astype(LOW)


def norm_of(value):
    center = value - jnp.mean(value, axis=-1, keepdims=True)
    inverse = lax.rsqrt(jnp.mean(center * center, axis=-1, keepdims=True) + NORM_EPS)
    return center * inverse, inverse


def norm_forward(x_i, gain, offset, *refs):
    terms, (x_o, h_o) = refs[:-2], refs[-2:]
    x = x_i[...]
    for t in terms:
        x = x + t[...].astype(F32)
    x_o[...] = x
    h_o[...] = (norm_of(x)[0] * gain[...] + offset[...]).astype(LOW)


def norm_backward(dx_i, y_i, gain, *refs):
    terms, (dy_o, low_o, small_o) = refs[:-3], refs[-3:]
    dh = terms[0][...]
    for t in terms[1:]:
        dh = dh + t[...].astype(F32)
    n, inverse = norm_of(y_i[...])
    small_o[0:1] = jnp.sum(dh * n, axis=0, keepdims=True)
    small_o[1:2] = jnp.sum(dh, axis=0, keepdims=True)
    scaled = dh * gain[...]
    dy = dx_i[...] + inverse * (
        scaled
        - jnp.mean(scaled, axis=-1, keepdims=True)
        - n * jnp.mean(scaled * n, axis=-1, keepdims=True)
    )
    dy_o[...] = dy
    low_o[...] = dy.astype(LOW)


def after(value, event):
    return lax.optimization_barrier((value, event))[0]


def log2(n):
    return n.bit_length() - 1


def reverse_bits(r, bits):
    return sum(((r >> k) & 1) << (bits - 1 - k) for k in range(bits))


def make_program(n_dp, n_chi, n_clo, n_mp):
    group_bits = [("chi", 1 << k) for k in range(log2(n_chi))]
    group_bits += [("dp", 1 << k) for k in range(log2(n_dp))]
    n_groups = n_dp * n_chi
    sizes = {"dp": n_dp, "chi": n_chi, "clo": n_clo, "mp": n_mp}

    def swap(value, axis, bit):
        return lax.ppermute(value, axis, [(i, i ^ bit) for i in range(sizes[axis])])

    def mp_gather(own):
        parts = [own]
        for k in reversed(range(log2(n_mp))):
            parts = parts + [swap(part, "mp", 1 << k) for part in parts]
        return [parts[reverse_bits(r, log2(n_mp))] for r in range(n_mp)]

    def token_gather(own):
        half = mp_gather(own)
        return half + [swap(part, "clo", 1) for part in half]

    def token_reduce(own_half, send_half, beside=None, before=None):
        rows, width = own_half.shape
        sub = rows // n_mp
        if before is not None:
            send_half, before = lax.optimization_barrier((send_half, before))
        moved = swap(send_half, "clo", 1)
        outs = [shape((sub, width), F32)] + [shape((sub, width), LOW)] * (n_mp - 1)
        parts = call(middle, 0, [own_half, moved], outs, [], rows * width)
        terms = [parts[0]] + [swap(parts[r], "mp", r) for r in range(1, n_mp)]
        result = None
        if beside is not None:
            work, args = beside
            terms, result = lax.optimization_barrier((terms, work(*after(args, parts[0]))))
        return terms, result, before

    def own_tokens(value):
        seqs, block, width = value.shape
        sub = block * n_chi // n_mp
        per_block = block // sub
        place = lax.axis_index("mp") % per_block
        mine = lax.dynamic_slice_in_dim(value, place * sub, sub, 1)
        chi = lax.axis_index("chi")
        here = lax.dynamic_index_in_dim(mine, chi, 0, keepdims=False)
        there = swap(lax.dynamic_index_in_dim(mine, 1 - chi, 0, keepdims=False), "chi", 1)
        return jnp.where(lax.axis_index("mp") // per_block == chi, here, there)

    def chi_swap(held, block, extra=None):
        chi = lax.axis_index("chi")
        mine = lax.dynamic_slice_in_dim(held, chi * block, block, 0)
        sent = lax.dynamic_slice_in_dim(held, (1 - chi) * block, block, 0)
        if extra is not None:
            sent = jnp.concatenate([sent, extra], axis=0)
        return mine, swap(sent, "chi", 1)

    def to_blocks(mine, moved, block):
        first = lax.axis_index("chi") == 0
        moved = moved[:block]
        return jnp.where(first, jnp.stack([mine, moved]), jnp.stack([moved, mine]))

    def by_place(parts):
        sub, width = parts[0].shape
        mp = lax.axis_index("mp")
        parts = jnp.stack(parts)
        for k in range(log2(n_mp)):
            pairs = parts.reshape(n_mp >> (k + 1), 2, 1 << k, sub, width)
            pairs = jnp.where((mp >> k) % 2 == 1, jnp.flip(pairs, 1), pairs)
            parts = pairs.reshape(n_mp, sub, width)
        return parts.reshape(n_mp * sub, width)

    def on_device(
        tokens, segments, cotangent, first_gain, first_bias, qkv_weight, qkv_bias,
        out_weight, second_gain, second_bias, gate_up_weight, down_weight,
    ):
        n_seq, block, width = tokens.shape
        rows_dev = qkv_weight.shape[1]
        half_in = qkv_weight.shape[3] // 2
        half_ff = down_weight.shape[2] // 2
        heads = half_in // HEAD
        total = block * n_chi * n_clo
        half_total = total // n_clo
        sub = half_total // n_mp
        n_parts = n_clo * n_mp
        mp, clo, chi = (lax.axis_index(a) for a in ("mp", "clo", "chi"))
        x_own = own_tokens(tokens).astype(F32)

        pad = -(3 * half_ff) % 128
        attn_cols, mlp_cols = 4 * half_in, 3 * half_ff + pad

        def attn_columns(l):
            view = jnp.transpose(qkv_weight[l], (1, 0, 2))
            outs = [shape((rows_dev, 2 * attn_cols), LOW)]
            args = [view, out_weight[l]]
            sems = [pltpu.SemaphoreType.DMA((8,))]
            return call(order_columns, 2, args, outs, sems, 0, hbm_outs=1)

        def mlp_columns(l):
            gu, down = jnp.transpose(gate_up_weight[l], (1, 0, 2)), down_weight[l]
            cut = half_ff - 64
            parts = [gu[0, :, :half_ff], gu[1, :, :half_ff], down[:, :half_ff]]
            parts += [down[:, half_ff + cut :], gu[0, :, half_ff:], gu[1, :, half_ff:]]
            parts += [down[:, half_ff : half_ff + cut]]
            return jnp.concatenate(parts, axis=1)

        def gather_weights(own):
            return lax.all_gather(own, ("dp", "chi", "clo"), axis=0, tiled=True)

        weights = []
        for l in range(LAYERS):
            attn = [gather_weights(attn_columns(l)[0])]
            weights.append([attn, gather_weights(mlp_columns(l))])
        dx = own_tokens(cotangent)
        gains = jnp.stack([first_gain, first_bias, second_gain, second_bias])
        half_bias = jnp.where(clo == 1, qkv_bias[:, :, half_in:], qkv_bias[:, :, :half_in])
        half_bias = half_bias.reshape(LAYERS, 1, 3 * half_in)

        there = swap(lax.dynamic_index_in_dim(segments, 1 - chi, 0, keepdims=False), "chi", 1)
        here = lax.dynamic_index_in_dim(segments, chi, 0, keepdims=False)
        pair = jnp.stack([jnp.where(chi == 0, here, there), jnp.where(chi == 0, there, here)])
        other = swap(pair, "clo", 1)
        whole = jnp.stack(
            [jnp.where(clo == 0, pair, other), jnp.where(clo == 0, other, pair)], axis=1
        ).reshape(total)
        core_of = jnp.arange(n_clo, dtype=jnp.int32) ^ clo
        mp_of = jnp.arange(n_mp, dtype=jnp.int32) ^ mp
        per_block = block // sub
        place = (
            (mp_of // per_block * (n_clo * block) + mp_of % per_block * sub)[None, :, None]
            + (core_of * block)[:, None, None]
            + jnp.arange(sub, dtype=jnp.int32)[None, None, :]
        ).reshape(total)
        match = place[:, None] == jnp.arange(total, dtype=jnp.int32)[None, :]
        seg = jnp.sum(jnp.where(match, whole[None, :], 0), axis=1)
        starts = jnp.sum((seg[None, :] < seg[:, None]).astype(jnp.int32), axis=1)
        freq = jnp.exp(
            jnp.arange(ROT // 2, dtype=F32) * (-2.0 * math.log(10000.0) / ROT)
        )
        angles = freq[:, None] * (place - starts).astype(F32)[None, :]
        cos_t, sin_t = jnp.cos(angles).T, jnp.sin(angles).T
        zeros = jnp.zeros((total, ROT // 2), F32)
        tail = jnp.zeros((total, HEAD - ROT), F32)
        per_slab = 128 // HEAD
        tables = jnp.stack(
            [
                jnp.tile(jnp.concatenate(parts, axis=1), (1, per_slab))
                for parts in (
                    (cos_t, cos_t, tail + 1.0),
                    (-sin_t, zeros, tail),
                    (zeros, sin_t, tail),
                )
            ]
        )
        row = jnp.stack([seg, place])
        geometry = [tables, row.T, row]
        geometry_scratch = [
            pltpu.VMEM((3, total, 128), F32),
            pltpu.VMEM((total, 2), jnp.int32),
        ]

        act = shape((total, half_in), LOW)
        reduced = [shape((half_total, width), LOW)] * 2
        sems = pltpu.SemaphoreType.DMA((n_parts + 2 * (width // BLOCK) + 5,))
        h_scratch = pltpu.VMEM((total, width), LOW)

        def mm(*dims):
            return 2 * math.prod(dims)

        def norm(x, gain, offset, terms):
            outs = [shape(x.shape, F32), shape(x.shape, LOW)]
            return call(norm_forward, 0, [x, gain[None], offset[None]] + terms, outs, [], 10 * x.size)

        def norm_back(dx, y, gain, terms):
            outs = [shape(y.shape, F32), shape(y.shape, LOW), shape((2, width), F32)]
            return call(norm_backward, 0, [dx, y, gain[None]] + terms, outs, [], 20 * y.size)

        def grads(a, b, da, db, cols):
            scratch = [pltpu.VMEM(x.shape, LOW) for x in (a, b, da, db)]
            scratch += [pltpu.VMEM((2, BLOCK, cols), LOW), pltpu.SemaphoreType.DMA((4,))]
            scratch += [pltpu.SemaphoreType.DMA((width // BLOCK,))]
            outs = [shape((width, cols), LOW)]
            flops = mm(total, width, cols)
            args = [a, b, da, db]
            return call(weight_grads, 4, args, outs, scratch, flops, hbm_outs=1, limit=60)

        def scatter(partial):
            return lax.psum_scatter(partial[0], ("dp", "chi"), scatter_dimension=0, tiled=True)

        def pick(block_sum):
            outs = [shape((rows_dev, block_sum.shape[1]), LOW)]
            sems = [pltpu.SemaphoreType.DMA((1,))]
            others = call(other_rows, 1, [block_sum], outs, sems, 0, hbm_outs=1)[0]
            return block_sum, swap(others, "clo", 1)

        def put(l, sums, n_first, unit, old):
            sums, moved = sums
            first, second = (n_first, rows_dev, 2 * unit), (rows_dev, 2 * unit)
            piece = pltpu.VMEM(moved.shape, LOW)
            return call(
                functools.partial(put_grads, l, len(old), n_first),
                2 + len(old),
                [sums, moved] + old,
                [shape((LAYERS,) + first, F32), shape((LAYERS,) + second, F32)],
                [
                    piece,
                    piece,
                    pltpu.VMEM(first, F32),
                    pltpu.VMEM(second, F32),
                    pltpu.SemaphoreType.DMA((4,)),
                ],
                0,
                hbm_outs=2,
                limit=60,
                aliases={2: 0, 3: 1} if old else None,
            )

        def put_attn(l, sums, old=()):
            return list(put(l, sums, 3, half_in, list(old)))

        def put_mlp(l, sums, old=()):
            return list(put(l, sums, 2, half_ff, list(old)))

        whole = shape((total, width), LOW)
        saved = []
        terms = []
        for l in range(LAYERS):
            w_attn, w_mlp = weights[l]
            x_own, h = norm(x_own, gains[0, l], gains[1, l], terms)
            h1 = token_gather(h)
            h1, q, k, v, o, own, send = call(
                functools.partial(attn_forward, n_parts, heads),
                n_parts + 3,
                h1 + w_attn + geometry + [half_bias[l]],
                [whole] + [act] * 4 + reduced,
                [
                    h_scratch,
                    pltpu.VMEM((width, attn_cols), LOW),
                    pltpu.VMEM((total, 3 * half_in), F32),
                ]
                + geometry_scratch
                + [sems],
                mm(total, width, attn_cols) + 2 * mm(heads, total, total, 2 * half_in),
                n_any=n_parts,
                hbm_outs=1,
                limit=56,
            )
            y_own, h = norm(x_own, gains[2, l], gains[3, l], token_reduce(own, send)[0])
            h2 = token_gather(h)
            if l == 0:
                h2, dm_parts = lax.optimization_barrier((h2, token_gather(dx)))
            h2, gu, z, own, send = call(
                functools.partial(mlp_forward, n_parts),
                n_parts + 1,
                h2 + [w_mlp],
                [whole, shape((total, 2 * half_ff), LOW), shape((total, half_ff), LOW)] + reduced,
                [
                    h_scratch,
                    pltpu.VMEM((width, mlp_cols), LOW),
                    pltpu.VMEM((total, 2 * half_ff), F32),
                    sems,
                ],
                mm(total, width, mlp_cols),
                n_any=n_parts,
                hbm_outs=1,
            )
            saved.append((x_own, h1, q, k, v, o, y_own, h2, gu, z))
            x_own, terms = y_own, token_reduce(own, send)[0]

        dx = dx.astype(F32)
        small_out = [None] * LAYERS
        done = None
        for l in reversed(range(LAYERS)):
            w_attn, w_mlp = weights[l]
            x_own, h1, q, k, v, o, y_own, h2, gu, z = saved[l]
            parts = dm_parts if done is None else token_gather(low)
            if done is None:
                gu = after(gu, terms[0])
            dm, dp2, own, send = call(
                functools.partial(mlp_backward, n_parts),
                n_parts + 2,
                parts + [w_mlp, gu],
                [whole, shape((total, 2 * half_ff), LOW)] + reduced,
                [
                    h_scratch,
                    pltpu.VMEM((width, mlp_cols), LOW),
                    pltpu.VMEM((total, half_ff), F32),
                    pltpu.VMEM(gu.shape, LOW),
                    sems,
                ],
                mm(total, width, mlp_cols),
                n_any=n_parts,
                hbm_outs=1,
            )
            work = functools.partial(grads, cols=mlp_cols)
            if done is None:
                before = terms, work(h2, dm, dp2, z)
                terms, _, (last, g_mlp) = token_reduce(own, send, before=before)
                x_last = y_own
                for t in last:
                    x_last = x_last + t.astype(F32)
                x_last = x_last.astype(LOW)
            else:
                terms, g_mlp, _ = token_reduce(own, send, (work, (h2, dm, dp2, z)))
            g_mlp = scatter(g_mlp)
            dy, low, small_two = norm_back(dx, y_own, gains[2, l], terms)
            parts = token_gather(low)
            if done is not None:
                parts, picked = lax.optimization_barrier((parts, [pick(x) for x in done]))
            da, dp1, bias_grad, own, send = call(
                functools.partial(attn_backward, n_parts, heads),
                n_parts + 6,
                parts + w_attn + [q, k, v] + geometry,
                [whole, shape((total, 3 * half_in), LOW), shape((1, 3 * half_in), F32)] + reduced,
                [
                    h_scratch,
                    pltpu.VMEM((width, attn_cols), LOW),
                    pltpu.VMEM((total, half_in), F32),
                    pltpu.VMEM((3, total, half_in), LOW),
                ]
                + geometry_scratch
                + [sems],
                mm(total, width, attn_cols) + 5 * mm(heads, total, total, half_in),
                n_any=n_parts,
                hbm_outs=1,
                limit=56,
            )
            work = functools.partial(grads, cols=attn_cols)
            beside = work, (h1, da, dp1, o)
            if done is None:
                terms, g_attn, _ = token_reduce(own, send, beside)
                done = (scatter(g_attn), g_mlp)
            else:
                terms, g_attn, x_parts = token_reduce(own, send, beside, mp_gather(x_last))
                x_mine, x_moved = chi_swap(by_place(x_parts), block)
            dx, low, small_one = norm_back(dy, x_own, gains[0, l], terms)
            small_out[l] = (small_one, small_two, bias_grad)
        norms = jnp.concatenate([part for l in range(LAYERS) for part in small_out[l][:2]], axis=0)
        bias = jnp.concatenate([small_out[l][2] for l in range(LAYERS)], axis=1)
        rows = -(-bias.size // width)
        bias = jnp.pad(bias, ((0, 0), (0, rows * width - bias.size))).reshape(rows, width)
        parts = mp_gather(jnp.concatenate([low, norms.astype(LOW)], axis=0))
        sums = put_attn(LAYERS - 1, picked[0]), put_mlp(LAYERS - 1, picked[1])
        parts, sums, x_moved = lax.optimization_barrier((parts, sums, x_moved))
        attn_sum, mlp_sum = sums
        norms = sum(part[sub:].astype(F32) for part in parts)
        both = jnp.concatenate([norms, bias], axis=0).astype(LOW)
        mine, moved = chi_swap(by_place([part[:sub] for part in parts]), block, both)
        g_mlp = after(g_mlp, parts[n_mp // 2])
        g_gu, g_down = put_mlp(0, pick(g_mlp), mlp_sum)
        g_gu = jnp.swapaxes(g_gu, 1, 2)
        g_gu = with_layout_constraint(g_gu, Layout(major_to_minor=(0, 1, 2, 3)))
        moved = after(moved, g_gu)
        tokens_grad = to_blocks(mine, moved, block).astype(F32)
        both = both.astype(F32) + moved[block:].astype(F32)
        activations = to_blocks(x_mine, x_moved, block)
        for name, bit in group_bits[1:]:
            both = both + swap(both, name, bit)
        other = swap(both, "clo", 1)
        norms = (both + other)[: 4 * LAYERS].reshape(LAYERS, 4, width)
        mine, others = (
            x[4 * LAYERS :].reshape(-1)[: LAYERS * 3 * half_in].reshape(LAYERS, 3, half_in)
            for x in (both, other)
        )
        low, high = jnp.where(clo == 0, mine, others), jnp.where(clo == 0, others, mine)
        bias = jnp.concatenate([low, high], axis=2)
        norms = [norms[:, i] for i in range(4)]
        g_attn = after(scatter(g_attn), (tokens_grad, activations, g_gu, norms, bias))
        g_qkv, g_out = put_attn(0, pick(g_attn), attn_sum)
        g_qkv = jnp.swapaxes(g_qkv, 1, 2)

        return (
            activations, tokens_grad, norms[0], norms[1],
            g_qkv, bias, g_out, norms[2], norms[3], g_gu, g_down,
        )

    return on_device


def solution(mesh):
    n_dp, n_ctx, n_mp = (mesh.shape[a] for a in ("dp", "ctx", "mp"))
    n_clo = 2
    n_chi = n_ctx // n_clo
    fine = Mesh(mesh.devices.reshape(n_dp, n_chi, n_clo, n_mp), ("dp", "chi", "clo", "mp"))
    rows = ("dp", "chi", "clo")
    ctx = ("chi", "clo")
    token_spec = P("dp", ctx, None)
    four, three = P(None, rows, None, "mp"), P(None, rows, "mp")
    bias_spec = P(None, None, "mp")
    return jax.shard_map(
        make_program(n_dp, n_chi, n_clo, n_mp),
        mesh=fine,
        in_specs=(
            token_spec, P("dp", ctx), token_spec, P(), P(), four, bias_spec, three, P(), P(),
            four, three,
        ),
        out_specs=(
            token_spec, token_spec, P(), P(), four, bias_spec, three, P(), P(), four, three,
        ),
        check_vma=False,
    )
```

```python
import functools
import math

import jax
import jax.numpy as jnp
from jax import lax
from jax.experimental import pallas as pl
from jax.experimental.layout import Layout, with_layout_constraint
from jax.experimental.pallas import tpu as pltpu
from jax.sharding import Mesh
from jax.sharding import PartitionSpec as P

HEAD = 64
ROT = 16
LAYERS = 2
NORM_EPS = 1e-05
MASK_FILL = -1e30
LOW = jnp.bfloat16
F32 = jnp.float32
MIB = 1024 * 1024
BLOCK = 512
HBM = pl.BlockSpec(memory_space=pltpu.HBM)
ANY = pl.BlockSpec(memory_space=pl.ANY)
VMEM = pl.BlockSpec(memory_space=pltpu.VMEM)


def dot(a, b, dims):
    return lax.dot_general(a, b, (dims, ((), ())), preferred_element_type=F32)


def nn(a, b):
    return dot(a, b, ((1,), (0,)))


def nt(a, b):
    return dot(a, b, ((1,), (1,)))


def tn(a, b):
    return dot(a, b, ((0,), (0,)))


def shape(dims, kind):
    return jax.ShapeDtypeStruct(dims, kind)


def call(body, n_hbm, args, outs, scratch, flops, hbm_outs=0, n_any=0, limit=32, aliases=None):
    moved = sum(a.size * a.dtype.itemsize for a in args)
    moved += sum(math.prod(o.shape) * jnp.dtype(o.dtype).itemsize for o in outs)
    return pl.pallas_call(
        body,
        out_shape=tuple(outs),
        in_specs=[ANY] * n_any + [HBM] * (n_hbm - n_any) + [VMEM] * (len(args) - n_hbm),
        out_specs=tuple([HBM] * hbm_outs + [VMEM] * (len(outs) - hbm_outs)),
        scratch_shapes=scratch,
        input_output_aliases=aliases or {},
        compiler_params=pltpu.CompilerParams(vmem_limit_bytes=limit * MIB),
        cost_estimate=pl.CostEstimate(flops=flops, bytes_accessed=moved, transcendentals=0),
    )(*args)


def into_rows(pieces, whole, sems, first):
    copies, row = [], 0
    for i, piece in enumerate(pieces):
        rows = piece.shape[0]
        copies.append(
            pltpu.make_async_copy(piece, whole.at[pl.ds(row, rows)], sems.at[first + i])
        )
        row += rows
    return copies


def weights_into(weights, whole, sems, first):
    rows, width = whole.shape
    cols = pl.ds(pl.multiple_of(lax.axis_index("clo") * width, 128), width)
    copies = []
    for at in range(0, rows, BLOCK):
        src, dst = weights.at[pl.ds(at, BLOCK), cols], whole.at[pl.ds(at, BLOCK)]
        copies.append(pltpu.make_async_copy(src, dst, sems.at[first + len(copies)]))
    return copies


def shared_tile_into(weights, whole, sems, first):
    rows, width = whole.shape
    main = width - 128
    core = lax.axis_index("clo")
    own = pl.ds(pl.multiple_of(core * width, 128), main)
    copies = []
    for at in range(0, rows, BLOCK):
        block = pl.ds(at, BLOCK)
        for cols, to in ((own, pl.ds(0, main)), (pl.ds(main, 128), pl.ds(main, 128))):
            src, dst = weights.at[block, cols], whole.at[block, to]
            copies.append(pltpu.make_async_copy(src, dst, sems.at[first + len(copies)]))
    return copies


def settle_tile(whole, rows):
    tile = whole[rows, whole.shape[1] - 128 :].astype(F32)
    rolled_tile = pltpu.roll(tile, 64, 1)
    tile = jnp.where(lax.axis_index("clo") == 0, tile, rolled_tile)
    whole[rows, whole.shape[1] - 128 :] = tile.astype(LOW)


def start_all(copies):
    for c in copies:
        c.start()


def wait_all(copies):
    for c in copies:
        c.wait()


def rolled(value, tables, sign):
    cos_t, ahead_t, behind_t = tables[0], tables[1], tables[2]
    slabs = []
    for at in range(0, value.shape[1], 128):
        x = value[:, at : at + 128]
        ahead = pltpu.roll(x, 128 - ROT // 2, 1)
        behind = pltpu.roll(x, ROT // 2, 1)
        slabs.append(x * cos_t + sign * (ahead * ahead_t + behind * behind_t))
    return jnp.concatenate(slabs, axis=1).astype(LOW)


def allowed_of(column, row):
    return (column[:, 0:1] == row[0:1]) & (row[1:2] <= column[:, 1:2])


def put_halves(tile, cols, own_ref, send_ref):
    half = own_ref.shape[0]
    own_ref[:, cols] = tile[:half].astype(LOW)
    send_ref[:, cols] = tile[half:].astype(LOW)


def softmax_of(q_h, k, allowed, scale):
    s = jnp.where(allowed, nt(q_h * scale, k), MASK_FILL)
    top = jnp.max(s, axis=-1, keepdims=True)
    e = jnp.exp(s - top)
    return e * (1.0 / jnp.sum(e, axis=-1, keepdims=True))


def load(pairs, sems, first):
    return [
        pltpu.make_async_copy(src, dst, sems.at[first + i]) for i, (src, dst) in enumerate(pairs)
    ]


def block_rows(w_s, w_copies=None):
    for i, at in enumerate(range(0, w_s.shape[0], BLOCK)):
        if w_copies is not None:
            w_copies[i].wait()
        yield i, slice(at, at + BLOCK)


def attn_forward(n_h, heads, *refs):
    h_parts, weights, refs = refs[:n_h], refs[n_h], refs[n_h + 1 :]
    tables, column, row, bias = refs[:4]
    full_o, q_o, k_o, v_o, o_o, own_o, send_o, h_s, w_s, acc, tab, col, sems = refs[4:]
    width = heads * HEAD
    copies = into_rows(h_parts, h_s, sems, 0)
    w_copies = weights_into(weights, w_s, sems, n_h)
    extra = load([(tables, tab), (column, col)], sems, n_h + len(w_copies))
    start_all(copies + w_copies + extra)
    wait_all(copies)
    whole = pltpu.make_async_copy(h_s, full_o, sems.at[0])
    whole.start()
    for r, rows in block_rows(w_s, w_copies):
        for c in range(3):
            cols = slice(c * width, (c + 1) * width)
            part = nn(h_s[:, rows], w_s[rows, cols])
            acc[:, cols] = part + (bias[:, cols] if r == 0 else acc[:, cols])
    wait_all(extra)
    q_o[...] = rolled(acc[:, :width], tab, 1.0)
    k_o[...] = rolled(acc[:, width : 2 * width], tab, 1.0)
    v_o[...] = acc[:, 2 * width :].astype(LOW)
    lane = lax.broadcasted_iota(jnp.int32, (1, width), 1) // HEAD
    allowed = allowed_of(col, row)
    k, v, q = k_o[...], v_o[...], q_o[...]
    zero = jnp.zeros((), LOW)
    o = None
    for h in range(heads):
        mine = lane == h
        w = softmax_of(jnp.where(mine, q, zero), k, allowed, LOW(1.0 / math.sqrt(HEAD)))
        part = nn(w.astype(LOW), jnp.where(mine, v, zero))
        o = part if o is None else o + part
    o_o[...] = o.astype(LOW)
    o = o_o[...]
    for r, rows in block_rows(w_s):
        put_halves(nt(o, w_s[rows, 3 * width :]), rows, own_o, send_o)
    whole.wait()


def attn_backward(n_h, heads, *refs):
    d_parts, weights, refs = refs[:n_h], refs[n_h], refs[n_h + 1 :]
    q_i, k_i, v_i, tables, column, row = refs[:6]
    full_o, dp_o, bias_o, own_o, send_o, d_s, w_s, acc, qkv, tab, col, sems = refs[6:]
    width = heads * HEAD
    copies = into_rows(d_parts, d_s, sems, 0)
    w_copies = weights_into(weights, w_s, sems, n_h)
    extra = load(
        [(q_i, qkv.at[0]), (k_i, qkv.at[1]), (v_i, qkv.at[2]), (tables, tab), (column, col)],
        sems,
        n_h + len(w_copies),
    )
    start_all(copies + w_copies + extra)
    wait_all(copies)
    whole = pltpu.make_async_copy(d_s, full_o, sems.at[0])
    whole.start()
    for r, rows in block_rows(w_s, w_copies):
        part = nn(d_s[:, rows], w_s[rows, 3 * width :])
        acc[...] = part if r == 0 else acc[...] + part
    do = acc[...].astype(LOW)
    wait_all(extra)
    q, k, v = qkv[0], qkv[1], qkv[2]
    lane = lax.broadcasted_iota(jnp.int32, (1, width), 1) // HEAD
    allowed = allowed_of(col, row)
    zero = jnp.zeros((), LOW)
    scale = 1.0 / math.sqrt(HEAD)
    dq = dk = dv = None
    for h in range(heads):
        mine = lane == h
        q_h = jnp.where(mine, q, zero)
        do_h = jnp.where(mine, do, zero)
        w = softmax_of(q_h, k, allowed, LOW(scale))
        dw = nt(do_h, v)
        ds = (w * (dw - jnp.sum(w * dw, axis=-1, keepdims=True))).astype(LOW)
        dv_h = tn(w.astype(LOW), do_h)
        dq_h = nn(ds, jnp.where(mine, k, zero))
        dk_h = tn(ds, q_h)
        dq, dk, dv = (
            (dq_h, dk_h, dv_h) if h == 0 else (dq + dq_h, dk + dk_h, dv + dv_h)
        )
    dp_o[:, :width] = rolled(dq * scale, tab, -1.0)
    dp_o[:, width : 2 * width] = rolled(dk * scale, tab, -1.0)
    dp_o[:, 2 * width :] = dv.astype(LOW)
    dp = dp_o[...]
    bias_o[...] = jnp.sum(dp.astype(F32), axis=0, keepdims=True)
    for r, rows in block_rows(w_s):
        put_halves(nt(dp, w_s[rows, : 3 * width]), rows, own_o, send_o)
    whole.wait()


def mlp_forward(n_h, *refs):
    h_parts, weights, refs = refs[:n_h], refs[n_h], refs[n_h + 1 :]
    full_o, gu_o, z_o, own_o, send_o, h_s, w_s, acc, sems = refs
    units = z_o.shape[1]
    copies = into_rows(h_parts, h_s, sems, 0)
    w_copies = shared_tile_into(weights, w_s, sems, n_h)
    start_all(copies + w_copies)
    wait_all(copies)
    whole = pltpu.make_async_copy(h_s, full_o, sems.at[0])
    whole.start()
    for r, rows in block_rows(w_s):
        wait_all(w_copies[2 * r : 2 * r + 2])
        settle_tile(w_s, rows)
        part = nn(h_s[:, rows], w_s[rows, : 2 * units])
        acc[...] = part if r == 0 else acc[...] + part
    gu_o[...] = acc[...].astype(LOW)
    g = acc[:, :units]
    u = acc[:, units:]
    z_o[...] = (g * u / (1.0 + jnp.exp(-g))).astype(LOW)
    z = z_o[...]
    for r, rows in block_rows(w_s):
        put_halves(nt(z, w_s[rows, 2 * units : 3 * units]), rows, own_o, send_o)
    whole.wait()


def mlp_backward(n_h, *refs):
    d_parts, weights, refs = refs[:n_h], refs[n_h], refs[n_h + 1 :]
    gu_i, full_o, dp_o, own_o, send_o, d_s, w_s, acc, gu, sems = refs
    units = acc.shape[1]
    copies = into_rows(d_parts, d_s, sems, 0)
    w_copies = shared_tile_into(weights, w_s, sems, n_h)
    extra = load([(gu_i, gu)], sems, n_h + len(w_copies))
    start_all(copies + w_copies + extra)
    wait_all(copies)
    whole = pltpu.make_async_copy(d_s, full_o, sems.at[0])
    whole.start()
    for r, rows in block_rows(w_s):
        wait_all(w_copies[2 * r : 2 * r + 2])
        settle_tile(w_s, rows)
        part = nn(d_s[:, rows], w_s[rows, 2 * units : 3 * units])
        acc[...] = part if r == 0 else acc[...] + part
    wait_all(extra)
    g = gu[:, :units].astype(F32)
    u = gu[:, units:].astype(F32)
    sig = 1.0 / (1.0 + jnp.exp(-g))
    dz = acc[...]
    dp_o[:, :units] = (dz * u * sig * (1.0 + g * (1.0 - sig))).astype(LOW)
    dp_o[:, units:] = (dz * g * sig).astype(LOW)
    dp = dp_o[...]
    for r, rows in block_rows(w_s):
        put_halves(nt(dp, w_s[rows, : 2 * units]), rows, own_o, send_o)
    whole.wait()


def load_grads(args, a_s, b_s, da_s, db_s, sems):
    copies = load(list(zip(args, (a_s, b_s, da_s, db_s))), sems, 0)
    start_all(copies)
    wait_all(copies)


def weight_grads(*refs):
    out, a_s, b_s, da_s, db_s, slots, sems, out_sems = refs[4:]
    load_grads(refs[:4], a_s, b_s, da_s, db_s, sems)
    split, end = da_s.shape[1], da_s.shape[1] + db_s.shape[1]
    sent = []
    for i, at in enumerate(range(0, a_s.shape[1], BLOCK)):
        cols = slice(at, at + BLOCK)
        slot = slots.at[i % 2]
        if i >= 2:
            sent[i - 2].wait()
        slot[:, :split] = tn(a_s[:, cols], da_s[...]).astype(LOW)
        slot[:, split:end] = tn(b_s[:, cols], db_s[...]).astype(LOW)
        if end < slot.shape[1]:
            slot[:, end:] = jnp.zeros((BLOCK, slot.shape[1] - end), LOW)
        sent.append(pltpu.make_async_copy(slot, out.at[pl.ds(at, BLOCK)], out_sems.at[i]))
        sent[i].start()
    wait_all(sent[-2:])


def other_rows(block_sum, out, sem):
    rows = out.shape[0]
    at = (1 - lax.axis_index("clo")) * rows
    copy = pltpu.make_async_copy(
        block_sum.at[pl.ds(pl.multiple_of(at, rows), rows)], out, sem.at[0]
    )
    copy.start()
    copy.wait()


def put_grads(layer, n_old, n_first, *refs):
    block_sum, moved = refs[:2]
    first_o, second_o, mine_s, moved_s, first_s, second_s, sems = refs[2 + n_old :]
    rows = moved.shape[0]
    me = lax.axis_index("clo")
    own = block_sum
    if own.shape[0] > rows:
        own = own.at[pl.ds(pl.multiple_of(me * rows, rows), rows)]
    copies = load([(own, mine_s), (moved, moved_s)], sems, 0)
    start_all(copies)
    wait_all(copies)
    low = jnp.where(me == 0, mine_s[...], moved_s[...])
    high = jnp.where(me == 0, moved_s[...], mine_s[...])
    width = second_s.shape[1] // 2
    out = load([(first_s, first_o.at[layer]), (second_s, second_o.at[layer])], sems, 2)
    for core, part in enumerate((low, high)):
        to = slice(core * width, (core + 1) * width)
        for c in range(n_first):
            first_s[c, :, to] = part[:, c * width : (c + 1) * width].astype(F32)
        second_s[:, to] = part[:, n_first * width : (n_first + 1) * width].astype(F32)
    start_all(out)
    wait_all(out)


def order_columns(*refs):
    qkv, out, both, sems = refs
    width = both.shape[1] // 8
    copies = []
    for core in range(2):
        cols = pl.ds(core * width, width)
        for c in range(4):
            src = out.at[:, cols] if c == 3 else qkv.at[c, :, cols]
            dst = both.at[:, pl.ds((4 * core + c) * width, width)]
            copies.append(pltpu.make_async_copy(src, dst, sems.at[len(copies)]))
    start_all(copies)
    wait_all(copies)


def middle(own_i, moved_i, own_o, *sends):
    rows = own_o.shape[0]
    own_o[...] = own_i[:rows].astype(F32) + moved_i[:rows].astype(F32)
    for r, send in enumerate(sends):
        at = slice((r + 1) * rows, (r + 2) * rows)
        send[...] = (own_i[at].astype(F32) + moved_i[at].astype(F32)).astype(LOW)


def norm_of(value):
    center = value - jnp.mean(value, axis=-1, keepdims=True)
    inverse = lax.rsqrt(jnp.mean(center * center, axis=-1, keepdims=True) + NORM_EPS)
    return center * inverse, inverse


def norm_forward(x_i, gain, offset, *refs):
    terms, (x_o, h_o) = refs[:-2], refs[-2:]
    x = x_i[...]
    for t in terms:
        x = x + t[...].astype(F32)
    x_o[...] = x
    h_o[...] = (norm_of(x)[0] * gain[...] + offset[...]).astype(LOW)


def norm_backward(dx_i, y_i, gain, *refs):
    terms, (dy_o, low_o, small_o) = refs[:-3], refs[-3:]
    dh = terms[0][...]
    for t in terms[1:]:
        dh = dh + t[...].astype(F32)
    n, inverse = norm_of(y_i[...])
    small_o[0:1] = jnp.sum(dh * n, axis=0, keepdims=True)
    small_o[1:2] = jnp.sum(dh, axis=0, keepdims=True)
    scaled = dh * gain[...]
    dy = dx_i[...] + inverse * (
        scaled
        - jnp.mean(scaled, axis=-1, keepdims=True)
        - n * jnp.mean(scaled * n, axis=-1, keepdims=True)
    )
    dy_o[...] = dy
    low_o[...] = dy.astype(LOW)


def after(value, event):
    return lax.optimization_barrier((value, event))[0]


def log2(n):
    return n.bit_length() - 1


def reverse_bits(r, bits):
    return sum(((r >> k) & 1) << (bits - 1 - k) for k in range(bits))


def make_program(n_dp, n_chi, n_clo, n_mp):
    group_bits = [("chi", 1 << k) for k in range(log2(n_chi))]
    group_bits += [("dp", 1 << k) for k in range(log2(n_dp))]
    n_groups = n_dp * n_chi
    sizes = {"dp": n_dp, "chi": n_chi, "clo": n_clo, "mp": n_mp}

    def swap(value, axis, bit):
        return lax.ppermute(value, axis, [(i, i ^ bit) for i in range(sizes[axis])])

    def mp_gather(own):
        parts = [own]
        for k in reversed(range(log2(n_mp))):
            parts = parts + [swap(part, "mp", 1 << k) for part in parts]
        return [parts[reverse_bits(r, log2(n_mp))] for r in range(n_mp)]

    def token_gather(own):
        half = mp_gather(own)
        return half + [swap(part, "clo", 1) for part in half]

    def token_reduce(own_half, send_half, beside=None, before=None):
        rows, width = own_half.shape
        sub = rows // n_mp
        if before is not None:
            send_half, before = lax.optimization_barrier((send_half, before))
        moved = swap(send_half, "clo", 1)
        outs = [shape((sub, width), F32)] + [shape((sub, width), LOW)] * (n_mp - 1)
        parts = call(middle, 0, [own_half, moved], outs, [], rows * width)
        terms = [parts[0]] + [swap(parts[r], "mp", r) for r in range(1, n_mp)]
        result = None
        if beside is not None:
            work, args = beside
            terms, result = lax.optimization_barrier((terms, work(*after(args, parts[0]))))
        return terms, result, before

    def own_tokens(value):
        seqs, block, width = value.shape
        sub = block * n_chi // n_mp
        per_block = block // sub
        place = lax.axis_index("mp") % per_block
        mine = lax.dynamic_slice_in_dim(value, place * sub, sub, 1)
        chi = lax.axis_index("chi")
        here = lax.dynamic_index_in_dim(mine, chi, 0, keepdims=False)
        there = swap(lax.dynamic_index_in_dim(mine, 1 - chi, 0, keepdims=False), "chi", 1)
        return jnp.where(lax.axis_index("mp") // per_block == chi, here, there)

    def chi_swap(held, block, extra=None):
        chi = lax.axis_index("chi")
        mine = lax.dynamic_slice_in_dim(held, chi * block, block, 0)
        sent = lax.dynamic_slice_in_dim(held, (1 - chi) * block, block, 0)
        if extra is not None:
            sent = jnp.concatenate([sent, extra], axis=0)
        return mine, swap(sent, "chi", 1)

    def to_blocks(mine, moved, block):
        first = lax.axis_index("chi") == 0
        moved = moved[:block]
        return jnp.where(first, jnp.stack([mine, moved]), jnp.stack([moved, mine]))

    def by_place(parts):
        sub, width = parts[0].shape
        mp = lax.axis_index("mp")
        parts = jnp.stack(parts)
        for k in range(log2(n_mp)):
            pairs = parts.reshape(n_mp >> (k + 1), 2, 1 << k, sub, width)
            pairs = jnp.where((mp >> k) % 2 == 1, jnp.flip(pairs, 1), pairs)
            parts = pairs.reshape(n_mp, sub, width)
        return parts.reshape(n_mp * sub, width)

    def on_device(
        tokens, segments, cotangent, first_gain, first_bias, qkv_weight, qkv_bias,
        out_weight, second_gain, second_bias, gate_up_weight, down_weight,
    ):
        n_seq, block, width = tokens.shape
        rows_dev = qkv_weight.shape[1]
        half_in = qkv_weight.shape[3] // 2
        half_ff = down_weight.shape[2] // 2
        heads = half_in // HEAD
        total = block * n_chi * n_clo
        half_total = total // n_clo
        sub = half_total // n_mp
        n_parts = n_clo * n_mp
        mp, clo, chi = (lax.axis_index(a) for a in ("mp", "clo", "chi"))
        x_own = own_tokens(tokens).astype(F32)

        pad = -(3 * half_ff) % 128
        attn_cols, mlp_cols = 4 * half_in, 3 * half_ff + pad

        def attn_columns(l):
            view = jnp.transpose(qkv_weight[l], (1, 0, 2))
            outs = [shape((rows_dev, 2 * attn_cols), LOW)]
            args = [view, out_weight[l]]
            sems = [pltpu.SemaphoreType.DMA((8,))]
            return call(order_columns, 2, args, outs, sems, 0, hbm_outs=1)

        def mlp_columns(l):
            gu, down = jnp.transpose(gate_up_weight[l], (1, 0, 2)), down_weight[l]
            cut = half_ff - 64
            parts = [gu[0, :, :half_ff], gu[1, :, :half_ff], down[:, :half_ff]]
            parts += [down[:, half_ff + cut :], gu[0, :, half_ff:], gu[1, :, half_ff:]]
            parts += [down[:, half_ff : half_ff + cut]]
            return jnp.concatenate(parts, axis=1)

        def gather_weights(own):
            return lax.all_gather(own, ("dp", "chi", "clo"), axis=0, tiled=True)

        weights = []
        for l in range(LAYERS):
            attn = [gather_weights(attn_columns(l)[0])]
            weights.append([attn, gather_weights(mlp_columns(l))])
        dx = own_tokens(cotangent)
        gains = jnp.stack([first_gain, first_bias, second_gain, second_bias])
        half_bias = jnp.where(clo == 1, qkv_bias[:, :, half_in:], qkv_bias[:, :, :half_in])
        half_bias = half_bias.reshape(LAYERS, 1, 3 * half_in)

        there = swap(lax.dynamic_index_in_dim(segments, 1 - chi, 0, keepdims=False), "chi", 1)
        here = lax.dynamic_index_in_dim(segments, chi, 0, keepdims=False)
        pair = jnp.stack([jnp.where(chi == 0, here, there), jnp.where(chi == 0, there, here)])
        other = swap(pair, "clo", 1)
        whole = jnp.stack(
            [jnp.where(clo == 0, pair, other), jnp.where(clo == 0, other, pair)], axis=1
        ).reshape(total)
        core_of = jnp.arange(n_clo, dtype=jnp.int32) ^ clo
        mp_of = jnp.arange(n_mp, dtype=jnp.int32) ^ mp
        per_block = block // sub
        place = (
            (mp_of // per_block * (n_clo * block) + mp_of % per_block * sub)[None, :, None]
            + (core_of * block)[:, None, None]
            + jnp.arange(sub, dtype=jnp.int32)[None, None, :]
        ).reshape(total)
        match = place[:, None] == jnp.arange(total, dtype=jnp.int32)[None, :]
        seg = jnp.sum(jnp.where(match, whole[None, :], 0), axis=1)
        starts = jnp.sum((seg[None, :] < seg[:, None]).astype(jnp.int32), axis=1)
        freq = jnp.exp(
            jnp.arange(ROT // 2, dtype=F32) * (-2.0 * math.log(10000.0) / ROT)
        )
        angles = freq[:, None] * (place - starts).astype(F32)[None, :]
        cos_t, sin_t = jnp.cos(angles).T, jnp.sin(angles).T
        zeros = jnp.zeros((total, ROT // 2), F32)
        tail = jnp.zeros((total, HEAD - ROT), F32)
        per_slab = 128 // HEAD
        tables = jnp.stack(
            [
                jnp.tile(jnp.concatenate(parts, axis=1), (1, per_slab))
                for parts in (
                    (cos_t, cos_t, tail + 1.0),
                    (-sin_t, zeros, tail),
                    (zeros, sin_t, tail),
                )
            ]
        )
        row = jnp.stack([seg, place])
        geometry = [tables, row.T, row]
        geometry_scratch = [
            pltpu.VMEM((3, total, 128), F32),
            pltpu.VMEM((total, 2), jnp.int32),
        ]

        act = shape((total, half_in), LOW)
        reduced = [shape((half_total, width), LOW)] * 2
        sems = pltpu.SemaphoreType.DMA((n_parts + 2 * (width // BLOCK) + 5,))
        h_scratch = pltpu.VMEM((total, width), LOW)

        def mm(*dims):
            return 2 * math.prod(dims)

        def norm(x, gain, offset, terms):
            outs = [shape(x.shape, F32), shape(x.shape, LOW)]
            return call(norm_forward, 0, [x, gain[None], offset[None]] + terms, outs, [], 10 * x.size)

        def norm_back(dx, y, gain, terms):
            outs = [shape(y.shape, F32), shape(y.shape, LOW), shape((2, width), F32)]
            return call(norm_backward, 0, [dx, y, gain[None]] + terms, outs, [], 20 * y.size)

        def grads(a, b, da, db, cols):
            scratch = [pltpu.VMEM(x.shape, LOW) for x in (a, b, da, db)]
            scratch += [pltpu.VMEM((2, BLOCK, cols), LOW), pltpu.SemaphoreType.DMA((4,))]
            scratch += [pltpu.SemaphoreType.DMA((width // BLOCK,))]
            outs = [shape((width, cols), LOW)]
            flops = mm(total, width, cols)
            args = [a, b, da, db]
            return call(weight_grads, 4, args, outs, scratch, flops, hbm_outs=1, limit=60)

        def scatter(partial):
            return lax.psum_scatter(partial[0], ("dp", "chi"), scatter_dimension=0, tiled=True)

        def pick(block_sum):
            outs = [shape((rows_dev, block_sum.shape[1]), LOW)]
            sems = [pltpu.SemaphoreType.DMA((1,))]
            others = call(other_rows, 1, [block_sum], outs, sems, 0, hbm_outs=1)[0]
            return block_sum, swap(others, "clo", 1)

        def put(l, sums, n_first, unit, old):
            sums, moved = sums
            first, second = (n_first, rows_dev, 2 * unit), (rows_dev, 2 * unit)
            piece = pltpu.VMEM(moved.shape, LOW)
            return call(
                functools.partial(put_grads, l, len(old), n_first),
                2 + len(old),
                [sums, moved] + old,
                [shape((LAYERS,) + first, F32), shape((LAYERS,) + second, F32)],
                [
                    piece,
                    piece,
                    pltpu.VMEM(first, F32),
                    pltpu.VMEM(second, F32),
                    pltpu.SemaphoreType.DMA((4,)),
                ],
                0,
                hbm_outs=2,
                limit=60 if n_first == 2 else 32,
                aliases={2: 0, 3: 1} if old else None,
            )

        def put_attn(l, sums, old=()):
            return list(put(l, sums, 3, half_in, list(old)))

        def put_mlp(l, sums, old=()):
            return list(put(l, sums, 2, half_ff, list(old)))

        whole = shape((total, width), LOW)
        saved = []
        terms = []
        for l in range(LAYERS):
            w_attn, w_mlp = weights[l]
            x_own, h = norm(x_own, gains[0, l], gains[1, l], terms)
            h1 = token_gather(h)
            h1, q, k, v, o, own, send = call(
                functools.partial(attn_forward, n_parts, heads),
                n_parts + 3,
                h1 + w_attn + geometry + [half_bias[l]],
                [whole] + [act] * 4 + reduced,
                [
                    h_scratch,
                    pltpu.VMEM((width, attn_cols), LOW),
                    pltpu.VMEM((total, 3 * half_in), F32),
                ]
                + geometry_scratch
                + [sems],
                mm(total, width, attn_cols) + 2 * mm(heads, total, total, 2 * half_in),
                n_any=n_parts,
                hbm_outs=1,
                limit=56,
            )
            y_own, h = norm(x_own, gains[2, l], gains[3, l], token_reduce(own, send)[0])
            h2 = token_gather(h)
            if l == 0:
                h2, dm_parts = lax.optimization_barrier((h2, token_gather(dx)))
            h2, gu, z, own, send = call(
                functools.partial(mlp_forward, n_parts),
                n_parts + 1,
                h2 + [w_mlp],
                [whole, shape((total, 2 * half_ff), LOW), shape((total, half_ff), LOW)] + reduced,
                [
                    h_scratch,
                    pltpu.VMEM((width, mlp_cols), LOW),
                    pltpu.VMEM((total, 2 * half_ff), F32),
                    sems,
                ],
                mm(total, width, mlp_cols),
                n_any=n_parts,
                hbm_outs=1,
            )
            saved.append((x_own, h1, q, k, v, o, y_own, h2, gu, z))
            x_own, terms = y_own, token_reduce(own, send)[0]

        dx = dx.astype(F32)
        small_out = [None] * LAYERS
        done = None
        for l in reversed(range(LAYERS)):
            w_attn, w_mlp = weights[l]
            x_own, h1, q, k, v, o, y_own, h2, gu, z = saved[l]
            parts = dm_parts if done is None else token_gather(low)
            if done is None:
                gu = after(gu, terms[0])
            dm, dp2, own, send = call(
                functools.partial(mlp_backward, n_parts),
                n_parts + 2,
                parts + [w_mlp, gu],
                [whole, shape((total, 2 * half_ff), LOW)] + reduced,
                [
                    h_scratch,
                    pltpu.VMEM((width, mlp_cols), LOW),
                    pltpu.VMEM((total, half_ff), F32),
                    pltpu.VMEM(gu.shape, LOW),
                    sems,
                ],
                mm(total, width, mlp_cols),
                n_any=n_parts,
                hbm_outs=1,
            )
            work = functools.partial(grads, cols=mlp_cols)
            if done is None:
                before = terms, work(h2, dm, dp2, z)
                terms, _, (last, g_mlp) = token_reduce(own, send, before=before)
                x_last = y_own
                for t in last:
                    x_last = x_last + t.astype(F32)
                x_last = x_last.astype(LOW)
            else:
                terms, g_mlp, _ = token_reduce(own, send, (work, (h2, dm, dp2, z)))
            g_mlp = scatter(g_mlp)
            dy, low, small_two = norm_back(dx, y_own, gains[2, l], terms)
            parts = token_gather(low)
            if done is not None:
                parts, picked = lax.optimization_barrier((parts, [pick(x) for x in done]))
            da, dp1, bias_grad, own, send = call(
                functools.partial(attn_backward, n_parts, heads),
                n_parts + 6,
                parts + w_attn + [q, k, v] + geometry,
                [whole, shape((total, 3 * half_in), LOW), shape((1, 3 * half_in), F32)] + reduced,
                [
                    h_scratch,
                    pltpu.VMEM((width, attn_cols), LOW),
                    pltpu.VMEM((total, half_in), F32),
                    pltpu.VMEM((3, total, half_in), LOW),
                ]
                + geometry_scratch
                + [sems],
                mm(total, width, attn_cols) + 5 * mm(heads, total, total, half_in),
                n_any=n_parts,
                hbm_outs=1,
                limit=56,
            )
            work = functools.partial(grads, cols=attn_cols)
            beside = work, (h1, da, dp1, o)
            if done is None:
                terms, g_attn, _ = token_reduce(own, send, beside)
                done = (scatter(g_attn), g_mlp)
            else:
                terms, g_attn, x_parts = token_reduce(own, send, beside, mp_gather(x_last))
                x_mine, x_moved = chi_swap(by_place(x_parts), block)
            dx, low, small_one = norm_back(dy, x_own, gains[0, l], terms)
            small_out[l] = (small_one, small_two, bias_grad)
        norms = jnp.concatenate([part for l in range(LAYERS) for part in small_out[l][:2]], axis=0)
        bias = jnp.concatenate([small_out[l][2] for l in range(LAYERS)], axis=1)
        rows = -(-bias.size // width)
        bias = jnp.pad(bias, ((0, 0), (0, rows * width - bias.size))).reshape(rows, width)
        parts = mp_gather(jnp.concatenate([low, norms.astype(LOW)], axis=0))
        sums = put_attn(LAYERS - 1, picked[0]), put_mlp(LAYERS - 1, picked[1])
        parts, sums, x_moved = lax.optimization_barrier((parts, sums, x_moved))
        attn_sum, mlp_sum = sums
        norms = sum(part[sub:].astype(F32) for part in parts)
        both = jnp.concatenate([norms, bias], axis=0).astype(LOW)
        mine, moved = chi_swap(by_place([part[:sub] for part in parts]), block, both)
        g_mlp = after(g_mlp, parts[n_mp // 2])
        g_gu, g_down = put_mlp(0, pick(g_mlp), mlp_sum)
        g_gu = jnp.swapaxes(g_gu, 1, 2)
        g_gu = with_layout_constraint(g_gu, Layout(major_to_minor=(0, 1, 2, 3)))
        moved = after(moved, g_gu)
        tokens_grad = to_blocks(mine, moved, block).astype(F32)
        both = both.astype(F32) + moved[block:].astype(F32)
        activations = to_blocks(x_mine, x_moved, block)
        for name, bit in group_bits[1:]:
            both = both + swap(both, name, bit)
        other = swap(both, "clo", 1)
        norms = (both + other)[: 4 * LAYERS].reshape(LAYERS, 4, width)
        mine, others = (
            x[4 * LAYERS :].reshape(-1)[: LAYERS * 3 * half_in].reshape(LAYERS, 3, half_in)
            for x in (both, other)
        )
        low, high = jnp.where(clo == 0, mine, others), jnp.where(clo == 0, others, mine)
        bias = jnp.concatenate([low, high], axis=2)
        norms = [norms[:, i] for i in range(4)]
        g_attn = after(scatter(g_attn), (tokens_grad, activations, g_gu, norms, bias))
        g_qkv, g_out = put_attn(0, pick(g_attn), attn_sum)
        g_qkv = jnp.swapaxes(g_qkv, 1, 2)

        return (
            activations, tokens_grad, norms[0], norms[1],
            g_qkv, bias, g_out, norms[2], norms[3], g_gu, g_down,
        )

    return on_device


def solution(mesh):
    n_dp, n_ctx, n_mp = (mesh.shape[a] for a in ("dp", "ctx", "mp"))
    n_clo = 2
    n_chi = n_ctx // n_clo
    fine = Mesh(mesh.devices.reshape(n_dp, n_chi, n_clo, n_mp), ("dp", "chi", "clo", "mp"))
    rows = ("dp", "chi", "clo")
    ctx = ("chi", "clo")
    token_spec = P("dp", ctx, None)
    four, three = P(None, rows, None, "mp"), P(None, rows, "mp")
    bias_spec = P(None, None, "mp")
    return jax.shard_map(
        make_program(n_dp, n_chi, n_clo, n_mp),
        mesh=fine,
        in_specs=(
            token_spec, P("dp", ctx), token_spec, P(), P(), four, bias_spec, three, P(), P(),
            four, three,
        ),
        out_specs=(
            token_spec, token_spec, P(), P(), four, bias_spec, three, P(), P(), four, three,
        ),
        check_vma=False,
    )
```
